32 devices in a mesh: dp: 16 (over z, y, x), head: 2 (over core).
Axes of the slice: x: 2, y: 2, z: 4, core: 2. Of those that a mesh axis runs over, the one named last changes fastest.
Arguments:
- tokens: bfloat16 [24576, 768], P('dp')
- cotangent: bfloat16 [24576, 768], P('dp'), may hold values from -6 to 6
- item_units: int32 [16, 2], P('dp'), may hold values from 1 to 23, as said below
- counted: int32 [24576], P('dp'), may hold values 0 or 1
- inputs_weight: float32 [3, 768, 768], P(None, 'dp', 'head'), may hold values from -0.21875 to 0.21875
- inputs_moment: float32 [3, 768, 768], P(None, 'dp', 'head'), may hold values from -0.00024414062 to 0.00024414062
- inputs_square: float32 [3, 768, 768], P(None, 'dp', 'head'), may hold values from 1.4391535e-09 to 2.2998236e-08
- mixing_weight: float32 [768, 768], P('head', 'dp'), may hold values from -0.21875 to 0.21875
- mixing_moment: float32 [768, 768], P('head', 'dp'), may hold values from -0.00024414062 to 0.00024414062
- mixing_square: float32 [768, 768], P('head', 'dp'), may hold values from 1.4391535e-09 to 2.2998236e-08
- expand_weight: float32 [768, 3072], P('dp', 'head'), may hold values from -0.21875 to 0.21875
- expand_moment: float32 [768, 3072], P('dp', 'head'), may hold values from -0.00024414062 to 0.00024414062
- expand_square: float32 [768, 3072], P('dp', 'head'), may hold values from 1.4391535e-09 to 2.2998236e-08
- reduce_weight: float32 [3072, 768], P('head', 'dp'), may hold values from -0.15625 to 0.15625
- reduce_moment: float32 [3072, 768], P('head', 'dp'), may hold values from -0.00024414062 to 0.00024414062
- reduce_square: float32 [3072, 768], P('head', 'dp'), may hold values from 1.4391535e-09 to 2.2998236e-08
- biases_weight: float32 [2, 2304], P('head', 'dp'), may hold values from -1.75 to 1.75
- biases_moment: float32 [2, 2304], P('head', 'dp'), may hold values from -0.00061035156 to 0.00061035156
- biases_square: float32 [2, 2304], P('head', 'dp'), may hold values from 1.41093475e-08 to 5.643739e-08
- shared_weight: float32 [6, 768], P(None, 'dp')
- shared_moment: float32 [6, 768], P(None, 'dp'), may hold values from -0.00061035156 to 0.00061035156
- shared_square: float32 [6, 768], P(None, 'dp'), may hold values from 1.41093475e-08 to 5.643739e-08
- kernel_weight: float32 [12, 33], P('head'), may hold values from -1 to 1
- kernel_moment: float32 [12, 33], P('head'), may hold values from -0.0012207031 to 0.0012207031
- kernel_square: float32 [12, 33], P('head'), may hold values from 3.5978836e-08 to 5.756614e-07
Outputs:
- output: float32 [24576, 768], P('dp')
- input_grad: float32 [24576, 768], P('dp')
- inputs_master: float32 [3, 768, 768], P(None, 'dp', 'head')
- inputs_momentum: float32 [3, 768, 768], P(None, 'dp', 'head')
- inputs_variance: float32 [3, 768, 768], P(None, 'dp', 'head')
- mixing_master: float32 [768, 768], P('head', 'dp')
- mixing_momentum: float32 [768, 768], P('head', 'dp')
- mixing_variance: float32 [768, 768], P('head', 'dp')
- expand_master: float32 [768, 3072], P('dp', 'head')
- expand_momentum: float32 [768, 3072], P('dp', 'head')
- expand_variance: float32 [768, 3072], P('dp', 'head')
- reduce_master: float32 [3072, 768], P('head', 'dp')
- reduce_momentum: float32 [3072, 768], P('head', 'dp')
- reduce_variance: float32 [3072, 768], P('head', 'dp')
- biases_master: float32 [2, 2304], P('head', 'dp')
- biases_momentum: float32 [2, 2304], P('head', 'dp')
- biases_variance: float32 [2, 2304], P('head', 'dp')
- shared_master: float32 [6, 768], P(None, 'dp')
- shared_momentum: float32 [6, 768], P(None, 'dp')
- shared_variance: float32 [6, 768], P(None, 'dp')
- kernel_master: float32 [12, 33], P('head')
- kernel_momentum: float32 [12, 33], P('head')
- kernel_variance: float32 [12, 33], P('head')
- grad_norm: float32 [], replicated
- sublayer_rms: float32 [2], replicated
The draws below stay inside these ranges and needn't reach their ends.
Inputs may be any that keep to these rules, and one draw needn't show every extreme that they name: `item_units`: each row holds the lengths of one buffer's two items in blocks of 64 tokens; their sum is at most 24, and some buffer is filled to exactly that.
All inputs are finite; a program needn't handle non-finite values. No bound on the sum of `counted` on one device may be relied on, other than what follows from the above.
Results may differ from the reference program's by a relative error of at most 0.023.
Values may be sent and summed in bfloat16 or wider, within the bound.
No kernel may reach another device: no remote copies, remote signals or barrier semaphores. Data moves between devices by JAX's collectives and lax.ppermute only.
A program may use at most 320 MiB of HBM per device.

```python
import math
import jax
import jax.numpy as jnp
from jax import lax

D = 768
HEADS = 12
HEAD_DIM = 64
FF = 3072
LANDMARKS = 64
TAPS = 33
PINV_STEPS = 6
CAP = 1536
BLOCKS = 16
TOKENS = 24576
HEAD_GROUPS = 2
LOCAL_WIDTH = 384
BIAS_WIDTH = 2304


def draw_tokens(key, part):
    noise_key, column_key = jax.random.split(key)
    row_place = jnp.arange(TOKENS, dtype=jnp.float32) / (TOKENS - 1)
    row_scale = 0.6 * 3.0 ** row_place
    column_scale = jnp.exp(jax.random.uniform(column_key, (D,), minval=jnp.log(0.5), maxval=jnp.log(2.5)))
    noise = jnp.clip(jax.random.normal(noise_key, (TOKENS, D)), -5.0, 5.0)
    return (noise * row_scale[:, None] * column_scale[None, :]).astype(jnp.bfloat16)


def draw_item_units(key, part):
    unit_total = CAP // LANDMARKS
    long_key, first_key, second_key, forced_key = jax.random.split(key, 4)
    block_index = jnp.arange(BLOCKS)
    forced = jax.random.randint(forced_key, (), 0, BLOCKS)
    is_long = (jax.random.randint(long_key, (BLOCKS,), 0, 8) == 0) | (block_index == forced)
    second_units = jax.random.randint(second_key, (BLOCKS,), 1, unit_total // 4 + 1)
    second_units = jnp.where(block_index == forced, 1, second_units)
    short_first = jax.random.randint(first_key, (BLOCKS,), unit_total // 4, unit_total // 2 + 1)
    first_units = jnp.where(is_long, unit_total - second_units, short_first)
    return jnp.stack([first_units, second_units], axis=1).astype(jnp.int32)


def draw_shared_weight(key, part):
    noise = jnp.clip(jax.random.normal(key, (6, D)), -3.0, 3.0)
    row_index = jnp.arange(6)
    is_gain = (row_index == 2) | (row_index == 4)
    return jnp.where(is_gain[:, None], 1.0 + 0.2 * noise, 0.3 * noise).astype(jnp.float32)


def touch_ends(result, rng, smallest, high):
    dims = result.shape
    index_at = [jax.random.randint(jax.random.fold_in(rng, axis), (), 0, dims[axis]) for axis in range(len(dims))]
    result = result.at[tuple(index_at)].set(smallest)
    longest = dims.index(max(dims))
    index_at[longest] = (index_at[longest] + 1) % dims[longest]
    return result.at[tuple(index_at)].set(high)


def block_scale(rng, shape, cuts, smallest, high):
    level, own = 1.0, jax.random.fold_in(rng, 6)
    for dim, blocks in cuts:
        heights = jnp.exp(jax.random.uniform(jax.random.fold_in(own, dim), (blocks,), jnp.float32, smallest / len(cuts), high / len(cuts)))
        level = level * jnp.repeat(heights, shape[dim] // blocks).reshape([-1 if axis == dim else 1 for axis in range(len(shape))])
    return level


def gaussian(rng, shape, deviation, bound, cuts=(), kind=jnp.bfloat16):
    factor_of = block_scale(rng, shape, cuts, -0.22, 0.18) if cuts else 1.0
    values = jax.random.normal(rng, shape, jnp.float32) * deviation * factor_of
    return jnp.minimum(jnp.maximum(values, -bound), bound).astype(kind)


def setup_inputs(seed: int = 0) -> dict:
    key_list = jax.random.split(jax.random.key(seed), 26)
    return {
        "tokens": draw_tokens(jax.random.fold_in(key_list[25], 71), 0),
        "cotangent": gaussian(key_list[1], (TOKENS, D), 1.0, 6.0, ((0, 16),)),
        "item_units": draw_item_units(jax.random.fold_in(key_list[25], 71), 0),
        "counted": touch_ends((jax.random.randint(key_list[3], (TOKENS,), 0, 8) < 7).astype(jnp.int32), jax.random.fold_in(key_list[3], 1), 0, 1),
        "inputs_weight": gaussian(key_list[4], (3, D, D), D ** -0.5, 0.21875, ((1, 16), (2, 2)), jnp.float32),
        "inputs_moment": gaussian(key_list[5], (3, D, D), (0.111 * (4 * D * D + 2 * D * FF + 8 * D + FF + HEADS * TAPS) ** -0.5), 0.00024414062, ((1, 16), (2, 2)), jnp.float32),
        "inputs_square": jnp.clip(jnp.exp(math.log(2.299823620433017e-08) - 2.7713625 * jax.random.uniform(key_list[6], (3, D, D), jnp.float32) ** block_scale(key_list[6], (3, D, D), ((1, 16), (2, 2)), -0.2, 0.2)), 1.439153463067555e-09, 2.299823620433017e-08),
        "mixing_weight": gaussian(key_list[7], (D, D), D ** -0.5, 0.21875, ((0, 2), (1, 16)), jnp.float32),
        "mixing_moment": gaussian(key_list[8], (D, D), (0.111 * (4 * D * D + 2 * D * FF + 8 * D + FF + HEADS * TAPS) ** -0.5), 0.00024414062, ((0, 2), (1, 16)), jnp.float32),
        "mixing_square": jnp.clip(jnp.exp(math.log(2.299823620433017e-08) - 2.7713625 * jax.random.uniform(key_list[9], (D, D), jnp.float32) ** block_scale(key_list[9], (D, D), ((0, 2), (1, 16)), -0.2, 0.2)), 1.439153463067555e-09, 2.299823620433017e-08),
        "expand_weight": gaussian(key_list[10], (D, FF), D ** -0.5, 0.21875, ((0, 16), (1, 2)), jnp.float32),
        "expand_moment": gaussian(key_list[11], (D, FF), (0.111 * (4 * D * D + 2 * D * FF + 8 * D + FF + HEADS * TAPS) ** -0.5), 0.00024414062, ((0, 16), (1, 2)), jnp.float32),
        "expand_square": jnp.clip(jnp.exp(math.log(2.299823620433017e-08) - 2.7713625 * jax.random.uniform(key_list[12], (D, FF), jnp.float32) ** block_scale(key_list[12], (D, FF), ((0, 16), (1, 2)), -0.2, 0.2)), 1.439153463067555e-09, 2.299823620433017e-08),
        "reduce_weight": gaussian(key_list[13], (FF, D), (FF // 2) ** -0.5, 0.15625, ((0, 2), (1, 16)), jnp.float32),
        "reduce_moment": gaussian(key_list[14], (FF, D), (0.111 * (4 * D * D + 2 * D * FF + 8 * D + FF + HEADS * TAPS) ** -0.5), 0.00024414062, ((0, 2), (1, 16)), jnp.float32),
        "reduce_square": jnp.clip(jnp.exp(math.log(2.299823620433017e-08) - 2.7713625 * jax.random.uniform(key_list[15], (FF, D), jnp.float32) ** block_scale(key_list[15], (FF, D), ((0, 2), (1, 16)), -0.2, 0.2)), 1.439153463067555e-09, 2.299823620433017e-08),
        "biases_weight": gaussian(key_list[16], (HEAD_GROUPS, BIAS_WIDTH), 0.3, 1.75, ((0, 2), (1, 16)), jnp.float32),
        "biases_moment": gaussian(key_list[17], (HEAD_GROUPS, BIAS_WIDTH), (0.25 * (4 * D * D + 2 * D * FF + 8 * D + FF + HEADS * TAPS) ** -0.5), 0.00061035156, ((0, 2), (1, 16)), jnp.float32),
        "biases_square": jnp.clip(jnp.exp(math.log(5.643738987259894e-08) - 1.3862944 * jax.random.uniform(key_list[18], (HEAD_GROUPS, BIAS_WIDTH), jnp.float32) ** block_scale(key_list[18], (HEAD_GROUPS, BIAS_WIDTH), ((0, 2), (1, 16)), -0.2, 0.2)), 1.4109347468149736e-08, 5.643738987259894e-08),
        "shared_weight": draw_shared_weight(jax.random.fold_in(key_list[25], 71), 0),
        "shared_moment": gaussian(key_list[20], (6, D), (0.25 * (4 * D * D + 2 * D * FF + 8 * D + FF + HEADS * TAPS) ** -0.5), 0.00061035156, ((1, 16),), jnp.float32),
        "shared_square": jnp.clip(jnp.exp(math.log(5.643738987259894e-08) - 1.3862944 * jax.random.uniform(key_list[21], (6, D), jnp.float32) ** block_scale(key_list[21], (6, D), ((1, 16),), -0.2, 0.2)), 1.4109347468149736e-08, 5.643738987259894e-08),
        "kernel_weight": gaussian(key_list[22], (HEADS, TAPS), TAPS ** -0.5, 1.0, ((0, 2),), jnp.float32),
        "kernel_moment": gaussian(key_list[23], (HEADS, TAPS), (0.555 * (4 * D * D + 2 * D * FF + 8 * D + FF + HEADS * TAPS) ** -0.5), 0.0012207031, ((0, 2),), jnp.float32),
        "kernel_square": jnp.clip(jnp.exp(math.log(5.75661374568881e-07) - 2.7725887 * jax.random.uniform(key_list[24], (HEADS, TAPS), jnp.float32) ** block_scale(key_list[24], (HEADS, TAPS), ((0, 2),), -0.2, 0.2)), 3.597883591055506e-08, 5.75661374568881e-07),
    }


PRECISE = lax.Precision.HIGHEST
NORM_EPS = 1e-05
CLIP_NORM = 1.0
CLIP_EPS = 1e-06
BETA_ONE = 0.9
BETA_TWO = 0.98
ADAM_EPS = 1e-08
RATE_MATRIX = 0.04
RATE_VECTOR = 0.5
WEIGHT_DECAY = 0.01
CORRECT_ONE = 1.0 - BETA_ONE ** 5
CORRECT_TWO = 1.0 - BETA_TWO ** 5

@jax.custom_vjp
def low(v):
    return lax.optimization_barrier(v.astype(jnp.bfloat16)).astype(jnp.float32)

@jax.custom_vjp
def low_back(v):
    return v

def low_keep(v):
    return (low(v), None)

def low_pass(kept, grad):
    return (grad,)

def back_keep(v):
    return (v, None)

def back_low(kept, grad):
    return (low(grad),)
low.defvjp(low_keep, low_pass)
low_back.defvjp(back_keep, back_low)

def softmax_rows(scores):
    peak = lax.optimization_barrier(jnp.max(scores, axis=-1, keepdims=True))
    raised = jnp.exp(scores - peak)
    return raised / lax.optimization_barrier(jnp.sum(raised, axis=-1, keepdims=True))

def layer_norm(summed_rows, gain_row, shift_row):
    center = summed_rows - lax.optimization_barrier(jnp.mean(summed_rows, axis=-1, keepdims=True))
    spread = lax.optimization_barrier(jnp.mean(center * center, axis=-1, keepdims=True))
    return center * lax.rsqrt(spread + NORM_EPS) * gain_row + shift_row

def row_items(unit_pair, row_count, mark_count):
    position = lax.iota(jnp.int32, row_count)
    first_end = unit_pair[0] * mark_count
    second_end = first_end + unit_pair[1] * mark_count
    return jnp.where(position < first_end, 0, jnp.where(position < second_end, 1, 2)).astype(jnp.int32)

def landmark_select(unit_pair, row_item, mark_count):
    row_count = row_item.shape[0]
    position = lax.iota(jnp.int32, row_count)
    item_start = jnp.where(row_item == 1, unit_pair[0] * mark_count, 0).astype(jnp.int32)
    segment_size = jnp.where(row_item == 1, unit_pair[1], unit_pair[0]).astype(jnp.int32)
    segment = (position - item_start) // segment_size
    landmark = lax.iota(jnp.int32, 2 * mark_count)
    member = (row_item[None, :] == landmark[:, None] // mark_count) & (segment[None, :] == landmark[:, None] % mark_count)
    per_item = jnp.where(landmark < mark_count, unit_pair[0], unit_pair[1]).astype(jnp.float32)
    return member.astype(jnp.float32) / per_item[:, None]

def pseudo_inverse(matrix, step_count):
    size_last = matrix.shape[-1]
    identity = jnp.eye(size_last, dtype=matrix.dtype)
    column_peak = lax.optimization_barrier(jnp.max(lax.optimization_barrier(jnp.sum(matrix, axis=-2)), axis=-1))
    approx = jnp.swapaxes(matrix, -1, -2) / column_peak[..., None, None]
    for _ in range(step_count):
        product = jnp.matmul(matrix, approx, precision=PRECISE)
        inner_term = 7.0 * identity - product
        inner_term = 15.0 * identity - jnp.matmul(product, inner_term, precision=PRECISE)
        inner_term = 13.0 * identity - jnp.matmul(product, inner_term, precision=PRECISE)
        approx = jnp.matmul(0.25 * approx, inner_term, precision=PRECISE)
    return approx

def nystrom(queries, key_rows, value_rows, select, row_item, mark_count, step_count):
    head_count = queries.shape[1]
    head_size = queries.shape[2]
    scaling = head_size ** (-0.25)
    query_scaled = queries * scaling
    key_scaled = key_rows * scaling
    land_query = jnp.einsum('lr,rhe->lhe', select, query_scaled, precision=PRECISE)
    land_key = jnp.einsum('lr,rhe->lhe', select, key_scaled, precision=PRECISE)
    land_item = lax.iota(jnp.int32, 2 * mark_count) // mark_count
    own_item = jnp.minimum(row_item, 1)
    first_scores = jnp.einsum('rhe,lhe->hrl', query_scaled, land_key, precision=PRECISE)
    first_kernel = softmax_rows(jnp.where(own_item[None, :, None] == land_item[None, None, :], first_scores, -jnp.inf))
    pair_query = land_query.reshape(2, mark_count, head_count, head_size)
    pair_key = land_key.reshape(2, mark_count, head_count, head_size)
    middle_kernel = softmax_rows(jnp.einsum('aihe,ajhe->haij', pair_query, pair_key, precision=PRECISE))
    inverse = pseudo_inverse(middle_kernel, step_count)
    last_scores = jnp.einsum('lhe,rhe->hlr', land_query, key_scaled, precision=PRECISE)
    last_kernel = softmax_rows(jnp.where(land_item[None, :, None] == row_item[None, None, :], last_scores, -jnp.inf))
    landmark_values = jnp.einsum('hlr,rhe->hle', last_kernel, value_rows, precision=PRECISE).reshape(head_count, 2, mark_count, head_size)
    weighted = jnp.einsum('haij,haje->haie', inverse, landmark_values, precision=PRECISE).reshape(head_count, 2 * mark_count, head_size)
    return jnp.einsum('hrl,hle->rhe', first_kernel, weighted, precision=PRECISE)

def depthwise_conv(value_rows, kernel, row_item):
    row_count = value_rows.shape[0]
    tap_count = kernel.shape[1]
    half_width = tap_count // 2
    padded = jnp.pad(value_rows, ((half_width, half_width), (0, 0), (0, 0)))
    padded_item = jnp.pad(row_item, (half_width, half_width), constant_values=-1)
    summed = jnp.zeros_like(value_rows)
    for offset in range(tap_count):
        same_item = (padded_item[offset:offset + row_count] == row_item) & (row_item < 2)
        shifted = jnp.where(same_item[:, None, None], padded[offset:offset + row_count], 0.0)
        summed = summed + shifted * kernel[:, offset][None, :, None]
    return summed

def adamw(master, moment, square, gradient, factor, learn_rate, decay_rate):
    clipped = gradient * factor
    moment_new = BETA_ONE * moment + (1.0 - BETA_ONE) * clipped
    square_new = BETA_TWO * square + (1.0 - BETA_TWO) * clipped * clipped
    step_size = moment_new / CORRECT_ONE / (jnp.sqrt(square_new / CORRECT_TWO) + ADAM_EPS)
    return (master - learn_rate * (step_size + decay_rate * master), moment_new, square_new)

def block_layer(block_rows, unit_pair, keep_rows, params):
    inputs_param, mixing_param, expand_param, reduce_param, biases_param, shared_param, kernel_param = params
    row_count = block_rows.shape[0]
    query_bias = biases_param[:, :LOCAL_WIDTH].reshape(D)
    value_bias = biases_param[:, LOCAL_WIDTH:2 * LOCAL_WIDTH].reshape(D)
    expand_bias = biases_param[:, 2 * LOCAL_WIDTH:].reshape(FF)
    row_item = row_items(unit_pair, row_count, LANDMARKS)
    select = landmark_select(unit_pair, row_item, LANDMARKS)
    inside = (row_item < 2).astype(jnp.float32)
    projected = jnp.einsum('rd,cdk->rck', block_rows, inputs_param, precision=PRECISE)
    head_shape = (row_count, HEADS, HEAD_DIM)
    queries = low_back(low(projected[:, 0] + query_bias)).reshape(head_shape)
    key_rows = low_back(low(projected[:, 1])).reshape(head_shape)
    value_rows = low_back(low(projected[:, 2] + value_bias)).reshape(head_shape)
    mixed = nystrom(queries, key_rows, value_rows, select, row_item, LANDMARKS, PINV_STEPS) + depthwise_conv(value_rows, kernel_param, row_item)
    attended = low((mixed * inside[:, None, None]).reshape(row_count, D))
    branch_one = low_back(jnp.dot(attended, mixing_param, precision=PRECISE)) + shared_param[0]
    hidden_one = layer_norm(block_rows + branch_one, shared_param[2], shared_param[3])
    hidden_low = low(hidden_one)
    expanded = low_back(jnp.dot(hidden_low, expand_param, precision=PRECISE) + expand_bias)
    activated = low(jax.nn.gelu(expanded, approximate=True))
    branch_two = low_back(jnp.dot(activated, reduce_param, precision=PRECISE)) + shared_param[1]
    output_rows = layer_norm(hidden_one + branch_two, shared_param[4], shared_param[5])
    weight_rows = keep_rows.astype(jnp.float32) * inside
    block_stats = jnp.stack([jnp.sum(weight_rows[:, None] * branch_one * branch_one), jnp.sum(weight_rows[:, None] * branch_two * branch_two), jnp.sum(weight_rows)])
    return (output_rows, block_stats)

def reference(tokens, cotangent, item_units, counted, inputs_weight, inputs_moment, inputs_square, mixing_weight, mixing_moment, mixing_square, expand_weight, expand_moment, expand_square, reduce_weight, reduce_moment, reduce_square, biases_weight, biases_moment, biases_square, shared_weight, shared_moment, shared_square, kernel_weight, kernel_moment, kernel_square):
    token_rows = tokens.astype(jnp.float32)
    counted_blocks = counted.reshape(BLOCKS, CAP)

    def forward(rows_in, inputs_param, mixing_param, expand_param, reduce_param, biases_param, shared_param, kernel_param):
        params = (low(inputs_param), low(mixing_param), low(expand_param), low(reduce_param), low(biases_param), low(shared_param), kernel_param)

        def one_block(pieces):
            return block_layer(pieces[0], pieces[1], pieces[2], params)
        outputs, block_stats = lax.map(jax.checkpoint(one_block), (rows_in.reshape(BLOCKS, CAP, D), item_units, counted_blocks))
        return (outputs.reshape(TOKENS, D), lax.optimization_barrier(jnp.sum(block_stats, axis=0)))
    (output_rows, total_stats), pullback = jax.vjp(forward, token_rows, inputs_weight, mixing_weight, expand_weight, reduce_weight, biases_weight, shared_weight, kernel_weight)

    def block_inside(unit_pair):
        return (row_items(unit_pair, CAP, LANDMARKS) < 2).astype(jnp.float32)
    weight_rows = (jax.vmap(block_inside)(item_units) * counted_blocks.astype(jnp.float32)).reshape(TOKENS)
    gradients = pullback((cotangent.astype(jnp.float32) * weight_rows[:, None], jnp.zeros_like(total_stats)))
    input_grad = gradients[0]
    weight_grads = gradients[1:]
    squares_total = sum((jnp.sum(gradient * gradient) for gradient in weight_grads))
    grad_norm = jnp.sqrt(squares_total)
    factor = CLIP_NORM / (grad_norm + CLIP_EPS)
    inputs_master, inputs_momentum, inputs_variance = adamw(inputs_weight, inputs_moment, inputs_square, weight_grads[0], factor, RATE_MATRIX, WEIGHT_DECAY)
    mixing_master, mixing_momentum, mixing_variance = adamw(mixing_weight, mixing_moment, mixing_square, weight_grads[1], factor, RATE_MATRIX, WEIGHT_DECAY)
    expand_master, expand_momentum, expand_variance = adamw(expand_weight, expand_moment, expand_square, weight_grads[2], factor, RATE_MATRIX, WEIGHT_DECAY)
    reduce_master, reduce_momentum, reduce_variance = adamw(reduce_weight, reduce_moment, reduce_square, weight_grads[3], factor, RATE_MATRIX, WEIGHT_DECAY)
    biases_master, biases_momentum, biases_variance = adamw(biases_weight, biases_moment, biases_square, weight_grads[4], factor, RATE_VECTOR, 0.0)
    shared_master, shared_momentum, shared_variance = adamw(shared_weight, shared_moment, shared_square, weight_grads[5], factor, RATE_VECTOR, 0.0)
    kernel_master, kernel_momentum, kernel_variance = adamw(kernel_weight, kernel_moment, kernel_square, weight_grads[6], factor, RATE_VECTOR, 0.0)
    sublayer_rms = jnp.sqrt(total_stats[:2] / (total_stats[2] * D))
    return (output_rows, input_grad, inputs_master, inputs_momentum, inputs_variance, mixing_master, mixing_momentum, mixing_variance, expand_master, expand_momentum, expand_variance, reduce_master, reduce_momentum, reduce_variance, biases_master, biases_momentum, biases_variance, shared_master, shared_momentum, shared_variance, kernel_master, kernel_momentum, kernel_variance, grad_norm, sublayer_rms)
```

```python
import jax
import jax.numpy as jnp
from jax import lax
from jax.sharding import PartitionSpec as P

HEAD_DIM = 64
LANDMARKS = 64
PINV_STEPS = 6


PRECISE = lax.Precision.HIGH
FAST = lax.Precision.DEFAULT
NORM_EPS = 1e-05
CLIP_NORM = 1.0
CLIP_EPS = 1e-06
BETA_ONE = 0.9
BETA_TWO = 0.98
ADAM_EPS = 1e-08
RATE_MATRIX = 0.04
RATE_VECTOR = 0.5
WEIGHT_DECAY = 0.01
CORRECT_ONE = 1.0 - BETA_ONE**5
CORRECT_TWO = 1.0 - BETA_TWO**5


def bits_of(count):
    bit_count = 0
    while (1 << bit_count) < count:
        bit_count += 1
    return bit_count


def swap(array, axis, count, bit):
    return lax.ppermute(array, axis, [(i, i ^ (1 << bit)) for i in range(count)])


def gather_rows(array, axis, count, order):
    bit_count = bits_of(count)
    own = lax.axis_index(axis)
    current = array.reshape((1,) * bit_count + array.shape)
    for bit in order:
        dim = bit_count - 1 - bit
        other = swap(current, axis, count, bit)
        current = jnp.where(
            (own >> bit) & 1 == 0,
            jnp.concatenate([current, other], dim),
            jnp.concatenate([other, current], dim),
        )
    return current.reshape((count * array.shape[0],) + array.shape[1:])


def scatter_rows(array, axis, count, order):
    bit_count = bits_of(count)
    own = lax.axis_index(axis)
    rows = array.shape[0] // count
    current = array.reshape((2,) * bit_count + (rows,) + array.shape[1:])
    for bit in order:
        dim = bit_count - 1 - bit
        mine = (own >> bit) & 1
        sent = lax.dynamic_slice_in_dim(current, 1 - mine, 1, dim).astype(jnp.bfloat16)
        kept = lax.dynamic_slice_in_dim(current, mine, 1, dim).astype(jnp.float32)
        current = kept + swap(sent, axis, count, bit).astype(jnp.float32)
    return current.reshape((rows,) + array.shape[1:])


def sum_all(array, axis, count):
    for bit in range(bits_of(count)):
        array = array + swap(array, axis, count, bit)
    return array


def head_sum(array, count):
    low = array.astype(jnp.bfloat16)
    total = low.astype(jnp.float32)
    for bit in range(bits_of(count)):
        total = total + swap(low, "head", count, bit).astype(jnp.float32)
        if bit + 1 < bits_of(count):
            low = total.astype(jnp.bfloat16)
            total = low.astype(jnp.float32)
    return total


def scatter_orders(count):
    bits = list(range(bits_of(count)))
    first = bits
    second = bits[:2][::-1] + bits[2:]
    return first, second


def after(array, *others):
    return lax.optimization_barrier((array,) + others)[0]


def softmax_rows(scores):
    peak = jnp.max(scores, axis=-1, keepdims=True)
    raised = jnp.exp(scores - peak)
    return raised / jnp.sum(raised, axis=-1, keepdims=True)


def layer_norm(summed_rows, gain_row, shift_row):
    center = summed_rows - jnp.mean(summed_rows, axis=-1, keepdims=True)
    spread = jnp.mean(center * center, axis=-1, keepdims=True)
    return center * lax.rsqrt(spread + NORM_EPS) * gain_row + shift_row


def gelu_tanh(values_in):
    return jax.nn.gelu(values_in, approximate=True)


def row_items(unit_pair, row_count, mark_count):
    position = lax.iota(jnp.int32, row_count)
    first_end = unit_pair[0] * mark_count
    second_end = first_end + unit_pair[1] * mark_count
    return jnp.where(position < first_end, 0, jnp.where(position < second_end, 1, 2)).astype(
        jnp.int32
    )


def landmark_select(unit_pair, row_item, mark_count):
    row_count = row_item.shape[0]
    position = lax.iota(jnp.int32, row_count)
    item_start = jnp.where(row_item == 1, unit_pair[0] * mark_count, 0)
    segment_size = jnp.where(row_item == 1, unit_pair[1], unit_pair[0])
    segment = (position - item_start) // segment_size
    landmark = lax.iota(jnp.int32, 2 * mark_count)
    member = (row_item[None, :] == landmark[:, None] // mark_count) & (
        segment[None, :] == landmark[:, None] % mark_count
    )
    per_item = jnp.where(landmark < mark_count, unit_pair[0], unit_pair[1]).astype(jnp.float32)
    return member.astype(jnp.float32) / per_item[:, None]


def pseudo_inverse(matrix, step_count):
    size_last = matrix.shape[-1]
    identity = jnp.eye(size_last, dtype=matrix.dtype)
    column_peak = jnp.max(jnp.sum(matrix, axis=-2), axis=-1)
    approx = jnp.swapaxes(matrix, -1, -2) / column_peak[..., None, None]
    for _ in range(step_count):
        product = jnp.matmul(matrix, approx, precision=PRECISE)
        inner_term = 7.0 * identity - product
        inner_term = 15.0 * identity - jnp.matmul(product, inner_term, precision=PRECISE)
        inner_term = 13.0 * identity - jnp.matmul(product, inner_term, precision=PRECISE)
        approx = jnp.matmul(0.25 * approx, inner_term, precision=PRECISE)
    return approx


def nystrom(queries, key_rows, value_rows, select, row_item, mark_count, step_count):
    head_count = queries.shape[1]
    head_size = queries.shape[2]
    scaling = head_size ** (-0.25)
    query_scaled = queries * scaling
    key_scaled = key_rows * scaling
    land_query = jnp.einsum("lr,rhe->lhe", select, query_scaled, precision=PRECISE)
    land_key = jnp.einsum("lr,rhe->lhe", select, key_scaled, precision=PRECISE)
    land_item = lax.iota(jnp.int32, 2 * mark_count) // mark_count
    own_item = jnp.minimum(row_item, 1)
    first_scores = jnp.einsum("rhe,lhe->hrl", query_scaled, land_key, precision=FAST)
    first_kernel = softmax_rows(
        jnp.where(own_item[None, :, None] == land_item[None, None, :], first_scores, -jnp.inf)
    )
    pair_query = land_query.reshape(2, mark_count, head_count, head_size)
    pair_key = land_key.reshape(2, mark_count, head_count, head_size)
    middle_kernel = softmax_rows(
        jnp.einsum("aihe,ajhe->haij", pair_query, pair_key, precision=PRECISE)
    )
    inverse = pseudo_inverse(middle_kernel, step_count)
    last_scores = jnp.einsum("lhe,rhe->hlr", land_query, key_scaled, precision=FAST)
    last_kernel = softmax_rows(
        jnp.where(land_item[None, :, None] == row_item[None, None, :], last_scores, -jnp.inf)
    )
    landmark_values = jnp.einsum(
        "hlr,rhe->hle", last_kernel, value_rows, precision=FAST
    ).reshape(head_count, 2, mark_count, head_size)
    weighted = jnp.einsum("haij,haje->haie", inverse, landmark_values, precision=PRECISE).reshape(
        head_count, 2 * mark_count, head_size
    )
    return jnp.einsum("hrl,hle->rhe", first_kernel, weighted, precision=FAST)


def depthwise_conv(value_rows, kernel, row_item):
    row_count = value_rows.shape[0]
    tap_count = kernel.shape[1]
    half_width = tap_count // 2
    padded = jnp.pad(value_rows, ((half_width, half_width), (0, 0), (0, 0)))
    padded_item = jnp.pad(row_item, (half_width, half_width), constant_values=-1)
    summed = jnp.zeros_like(value_rows)
    for offset in range(tap_count):
        same_item = (padded_item[offset : offset + row_count] == row_item) & (row_item < 2)
        shifted = jnp.where(same_item[:, None, None], padded[offset : offset + row_count], 0.0)
        summed = summed + shifted * kernel[:, offset][None, :, None]
    return summed


def conv_backward(value_rows, kernel, row_item, grad_out):
    row_count = value_rows.shape[0]
    tap_count = kernel.shape[1]
    half_width = tap_count // 2
    padded = jnp.pad(value_rows, ((half_width, half_width), (0, 0), (0, 0)))
    padded_item = jnp.pad(row_item, (half_width, half_width), constant_values=-1)
    grad_values = jnp.zeros_like(value_rows)
    kernel_terms = []
    for offset in range(tap_count):
        same_item = (padded_item[offset : offset + row_count] == row_item) & (row_item < 2)
        masked_grad = jnp.where(same_item[:, None, None], grad_out, 0.0)
        kernel_terms.append(jnp.sum(masked_grad * padded[offset : offset + row_count], axis=(0, 2)))
        spread_grad = jnp.pad(masked_grad, ((half_width, half_width), (0, 0), (0, 0)))
        start_row = 2 * half_width - offset
        grad_values = (
            grad_values
            + spread_grad[start_row : start_row + row_count] * kernel[:, offset][None, :, None]
        )
    return (grad_values, jnp.stack(kernel_terms, axis=1))


def adamw(master, moment, square, gradient, factor, learn_rate, decay_rate):
    clipped = gradient * factor
    moment_new = BETA_ONE * moment + (1.0 - BETA_ONE) * clipped
    square_new = BETA_TWO * square + (1.0 - BETA_TWO) * clipped * clipped
    step_size = moment_new / CORRECT_ONE / (jnp.sqrt(square_new / CORRECT_TWO) + ADAM_EPS)
    return (master - learn_rate * (step_size + decay_rate * master), moment_new, square_new)


def body(
    tokens,
    cotangent,
    item_units,
    counted,
    inputs_weight,
    inputs_moment,
    inputs_square,
    mixing_weight,
    mixing_moment,
    mixing_square,
    expand_weight,
    expand_moment,
    expand_square,
    reduce_weight,
    reduce_moment,
    reduce_square,
    biases_weight,
    biases_moment,
    biases_square,
    shared_weight,
    shared_moment,
    shared_square,
    kernel_weight,
    kernel_moment,
    kernel_square,
):
    dp_count = lax.axis_size("dp")
    head_count = lax.axis_size("head")
    first_order, second_order = scatter_orders(dp_count)
    local_width = inputs_weight.shape[2]
    shard_rows = inputs_weight.shape[1]
    hidden_units = expand_weight.shape[1]
    bias_share = biases_weight.shape[1]
    inputs_low = jnp.concatenate([inputs_weight[c] for c in range(3)], axis=1).astype(jnp.bfloat16)
    mixing_low = mixing_weight.T.astype(jnp.bfloat16)
    expand_low = expand_weight.astype(jnp.bfloat16)
    reduce_low = reduce_weight.T.astype(jnp.bfloat16)
    small_low = jnp.concatenate([biases_weight.reshape(-1), shared_weight.reshape(-1)]).astype(
        jnp.bfloat16
    )[None, :]
    half = (3 * local_width // 2 + 127) // 128 * 128
    small_full = gather_rows(small_low, "dp", dp_count, first_order[::-1])
    inputs_left = gather_rows(inputs_low[:, :half], "dp", dp_count, first_order[::-1])
    inputs_right = gather_rows(inputs_low[:, half:], "dp", dp_count, second_order[::-1])
    inputs_full = jnp.concatenate([inputs_left, inputs_right], axis=1)
    mixing_low, expand_low = after(mixing_low, inputs_full), after(expand_low, inputs_full)
    reduce_low = after(reduce_low, inputs_full)
    mixing_full = gather_rows(mixing_low, "dp", dp_count, first_order[::-1])
    expand_full = gather_rows(expand_low, "dp", dp_count, second_order[::-1])
    reduce_full = gather_rows(reduce_low, "dp", dp_count, first_order[::-1])
    biases_full = small_full[:, :bias_share].reshape(1, -1)
    shared_full = small_full[:, bias_share:].reshape(dp_count, 6, shard_rows)
    shared_full = shared_full.transpose(1, 0, 2).reshape(6, -1)
    local_heads = local_width // HEAD_DIM
    row_count = tokens.shape[0]
    width_full = tokens.shape[1]
    shared_rows = shared_full.astype(jnp.float32)
    biases_row = biases_full[0].astype(jnp.float32)
    query_bias = biases_row[:local_width]
    value_bias = biases_row[local_width : 2 * local_width]
    expand_bias = biases_row[2 * local_width :]
    unit_pair = item_units[0]
    row_item = row_items(unit_pair, row_count, LANDMARKS)
    select = landmark_select(unit_pair, row_item, LANDMARKS)
    inside = (row_item < 2).astype(jnp.float32)
    head_shape = (row_count, local_heads, HEAD_DIM)
    weight_rows = counted.astype(jnp.float32) * inside
    projected = jnp.dot(tokens, inputs_full, preferred_element_type=jnp.float32).reshape(row_count, 3, local_width)
    queries = (
        (projected[:, 0] + query_bias).astype(jnp.bfloat16).astype(jnp.float32).reshape(head_shape)
    )
    key_rows = projected[:, 1].astype(jnp.bfloat16).astype(jnp.float32).reshape(head_shape)
    value_rows = (
        (projected[:, 2] + value_bias).astype(jnp.bfloat16).astype(jnp.float32).reshape(head_shape)
    )

    def attend(query_in, key_in, value_in):
        return nystrom(query_in, key_in, value_in, select, row_item, LANDMARKS, PINV_STEPS)

    core_out, core_pull = jax.vjp(attend, queries, key_rows, value_rows)
    mixed = core_out + depthwise_conv(value_rows, kernel_weight, row_item)
    attended = (mixed * inside[:, None, None]).reshape(row_count, local_width).astype(jnp.bfloat16)
    mixing_part = jnp.einsum("rk,dk->rd", attended, mixing_full, preferred_element_type=jnp.float32)
    branch_one = head_sum(mixing_part, head_count) + shared_rows[0]
    token_rows = tokens.astype(jnp.float32)
    hidden_one, norm_one_pull = jax.vjp(
        layer_norm, token_rows + branch_one, shared_rows[2], shared_rows[3]
    )
    hidden_low = hidden_one.astype(jnp.bfloat16)
    expanded = jnp.dot(hidden_low, expand_full, preferred_element_type=jnp.float32) + expand_bias
    activated, gelu_pull = jax.vjp(gelu_tanh, expanded)
    activated_low = activated.astype(jnp.bfloat16)
    reduce_part = jnp.einsum("rf,df->rd", activated_low, reduce_full, preferred_element_type=jnp.float32)
    branch_two = head_sum(reduce_part, head_count) + shared_rows[1]
    output_rows, norm_two_pull = jax.vjp(
        layer_norm, hidden_one + branch_two, shared_rows[4], shared_rows[5]
    )
    local_stats = jnp.stack(
        [
            jnp.sum(weight_rows[:, None] * branch_one * branch_one),
            jnp.sum(weight_rows[:, None] * branch_two * branch_two),
            jnp.sum(weight_rows),
        ]
    )
    grad_rows = cotangent.astype(jnp.float32) * weight_rows[:, None]
    d_res_two, d_gain_two, d_shift_two = norm_two_pull(grad_rows)
    d_two_low = d_res_two.astype(jnp.bfloat16)
    reduce_grad = jnp.einsum(
        "rd,rf->df", d_two_low, activated_low, preferred_element_type=jnp.float32
    )
    d_activated = jnp.einsum(
        "rd,df->rf", d_two_low, reduce_full, preferred_element_type=jnp.float32
    )
    (d_expanded,) = gelu_pull(d_activated)
    d_expanded_low = d_expanded.astype(jnp.bfloat16)
    expand_grad = jnp.einsum(
        "rd,rf->df", hidden_low, d_expanded_low, preferred_element_type=jnp.float32
    )
    hidden_part = jnp.einsum(
        "rf,df->rd", d_expanded_low, expand_full, preferred_element_type=jnp.float32
    )
    d_hidden = head_sum(hidden_part, head_count) + d_res_two
    d_res_one, d_gain_one, d_shift_one = norm_one_pull(d_hidden)
    shared_grad = jnp.stack(
        [
            jnp.sum(d_res_one, axis=0),
            jnp.sum(d_res_two, axis=0),
            d_gain_one,
            d_shift_one,
            d_gain_two,
            d_shift_two,
        ]
    )
    d_one_low = d_res_one.astype(jnp.bfloat16)
    mixing_grad = jnp.einsum("rd,rk->dk", d_one_low, attended, preferred_element_type=jnp.float32)
    d_attended = (
        jnp.einsum("rd,dk->rk", d_one_low, mixing_full, preferred_element_type=jnp.float32)
        * inside[:, None]
    )
    d_mixed = d_attended.reshape(head_shape)
    d_query, d_key, d_value = core_pull(d_mixed)
    d_value_conv, kernel_grad = conv_backward(value_rows, kernel_weight, row_item, d_mixed)
    projected_grad = (
        jnp.stack([d_query, d_key, d_value + d_value_conv], axis=1)
        .reshape(row_count, 3 * local_width)
        .astype(jnp.bfloat16)
    )
    inputs_grad = jnp.einsum(
        "rd,rk->dk", tokens, projected_grad, preferred_element_type=jnp.float32
    )
    token_part = jnp.einsum(
        "rk,dk->rd", projected_grad, inputs_full, preferred_element_type=jnp.float32
    )
    input_grad = head_sum(token_part, head_count) + d_res_one
    biases_grad = jnp.concatenate(
        [
            jnp.sum(projected_grad[:, :local_width], axis=0, dtype=jnp.float32),
            jnp.sum(projected_grad[:, 2 * local_width :], axis=0, dtype=jnp.float32),
            jnp.sum(d_expanded_low, axis=0, dtype=jnp.float32),
        ]
    )[None, :]
    expand_share = scatter_rows(expand_grad, "dp", dp_count, first_order)
    reduce_share = scatter_rows(reduce_grad, "dp", dp_count, second_order).T
    mixing_share = scatter_rows(mixing_grad, "dp", dp_count, first_order).T
    inputs_share = jnp.concatenate(
        [
            scatter_rows(inputs_grad[:, :half], "dp", dp_count, first_order),
            scatter_rows(inputs_grad[:, half:], "dp", dp_count, second_order),
        ],
        axis=1,
    )
    inputs_share = inputs_share.reshape(shard_rows, 3, local_width).transpose(1, 0, 2)
    small_parts = [biases_grad.reshape(-1), shared_grad.reshape(-1), kernel_grad.reshape(-1)]
    small_size = sum(part.shape[0] for part in small_parts)
    small_rows = (small_size + 1023) // 1024 * 8
    small_parts.append(jnp.zeros((small_rows * 128 - small_size,), jnp.float32))
    small_total = sum_all(jnp.concatenate(small_parts).reshape(small_rows, 128), "dp", dp_count)
    small_total = small_total.reshape(-1)
    dp_index = lax.axis_index("dp")
    biases_share = lax.dynamic_slice_in_dim(small_total, dp_index * bias_share, bias_share)[None, :]
    bias_size = biases_grad.shape[1]
    shared_total = small_total[bias_size : bias_size + 6 * width_full].reshape(6, width_full)
    shared_share = lax.dynamic_slice_in_dim(shared_total, dp_index * shard_rows, shard_rows, axis=1)
    kernel_total = small_total[bias_size + 6 * width_full : small_size].reshape(kernel_grad.shape)
    kernel_squares = jnp.where(lax.axis_index("dp") == 0, jnp.sum(kernel_total * kernel_total), 0.0)
    local_squares = (
        jnp.sum(inputs_share * inputs_share)
        + jnp.sum(mixing_share * mixing_share)
        + jnp.sum(expand_share * expand_share)
        + jnp.sum(reduce_share * reduce_share)
        + jnp.sum(biases_share * biases_share)
    )
    local_squares = (
        local_squares
        + jnp.where(lax.axis_index("head") == 0, jnp.sum(shared_share * shared_share), 0.0)
        + kernel_squares
    )
    final_row = jnp.concatenate([local_squares[None], local_stats, jnp.zeros((124,), jnp.float32)])
    final_row = sum_all(sum_all(final_row[None, :], "head", head_count), "dp", dp_count)[0]
    squares_total, summed_stats = final_row[0], final_row[1:4]
    grad_norm = jnp.sqrt(squares_total)
    factor = CLIP_NORM / (grad_norm + CLIP_EPS)
    inputs_master, inputs_momentum, inputs_variance = adamw(
        inputs_weight, inputs_moment, inputs_square, inputs_share, factor, RATE_MATRIX, WEIGHT_DECAY
    )
    mixing_master, mixing_momentum, mixing_variance = adamw(
        mixing_weight, mixing_moment, mixing_square, mixing_share, factor, RATE_MATRIX, WEIGHT_DECAY
    )
    expand_master, expand_momentum, expand_variance = adamw(
        expand_weight, expand_moment, expand_square, expand_share, factor, RATE_MATRIX, WEIGHT_DECAY
    )
    reduce_master, reduce_momentum, reduce_variance = adamw(
        reduce_weight, reduce_moment, reduce_square, reduce_share, factor, RATE_MATRIX, WEIGHT_DECAY
    )
    biases_master, biases_momentum, biases_variance = adamw(
        biases_weight, biases_moment, biases_square, biases_share, factor, RATE_VECTOR, 0.0
    )
    shared_master, shared_momentum, shared_variance = adamw(
        shared_weight, shared_moment, shared_square, shared_share, factor, RATE_VECTOR, 0.0
    )
    kernel_master, kernel_momentum, kernel_variance = adamw(
        kernel_weight, kernel_moment, kernel_square, kernel_total, factor, RATE_VECTOR, 0.0
    )
    sublayer_rms = jnp.sqrt(summed_stats[:2] / (summed_stats[2] * width_full))
    return (
        output_rows,
        input_grad,
        inputs_master,
        inputs_momentum,
        inputs_variance,
        mixing_master,
        mixing_momentum,
        mixing_variance,
        expand_master,
        expand_momentum,
        expand_variance,
        reduce_master,
        reduce_momentum,
        reduce_variance,
        biases_master,
        biases_momentum,
        biases_variance,
        shared_master,
        shared_momentum,
        shared_variance,
        kernel_master,
        kernel_momentum,
        kernel_variance,
        grad_norm,
        sublayer_rms,
    )


def solution(mesh):
    placed = (
        P("dp", None),
        P("dp", None),
        P("dp", None),
        P("dp"),
        P(None, "dp", "head"),
        P(None, "dp", "head"),
        P(None, "dp", "head"),
        P("head", "dp"),
        P("head", "dp"),
        P("head", "dp"),
        P("dp", "head"),
        P("dp", "head"),
        P("dp", "head"),
        P("head", "dp"),
        P("head", "dp"),
        P("head", "dp"),
        P("head", "dp"),
        P("head", "dp"),
        P("head", "dp"),
        P(None, "dp"),
        P(None, "dp"),
        P(None, "dp"),
        P("head", None),
        P("head", None),
        P("head", None),
    )
    return jax.shard_map(
        body,
        mesh=mesh,
        in_specs=placed,
        out_specs=(
            P("dp", None),
            P("dp", None),
            P(None, "dp", "head"),
            P(None, "dp", "head"),
            P(None, "dp", "head"),
            P("head", "dp"),
            P("head", "dp"),
            P("head", "dp"),
            P("dp", "head"),
            P("dp", "head"),
            P("dp", "head"),
            P("head", "dp"),
            P("head", "dp"),
            P("head", "dp"),
            P("head", "dp"),
            P("head", "dp"),
            P("head", "dp"),
            P(None, "dp"),
            P(None, "dp"),
            P(None, "dp"),
            P("head", None),
            P("head", None),
            P("head", None),
            P(),
            P(),
        ),
        check_vma=False,
    )
```

```python
import jax
import jax.numpy as jnp
from jax import lax
from jax.experimental import pallas as pl
from jax.experimental.pallas import tpu as pltpu
from jax.sharding import PartitionSpec as P

HEAD_DIM = 64
LANDMARKS = 64
PINV_STEPS = 6
ROUGH_STEPS = 4
TAPS = 33
NORM_EPS = 1e-05
CLIP_NORM = 1.0
CLIP_EPS = 1e-06
BETA_ONE = 0.9
BETA_TWO = 0.98
ADAM_EPS = 1e-08
RATE_MATRIX = 0.04
RATE_VECTOR = 0.5
WEIGHT_DECAY = 0.01
CORRECT_ONE = 1.0 - BETA_ONE**5
CORRECT_TWO = 1.0 - BETA_TWO**5

def bits_of(count):
    bit_count = 0
    while (1 << bit_count) < count:
        bit_count += 1
    return bit_count


def swap(array, axis, count, bit):
    return lax.ppermute(array, axis, [(i, i ^ (1 << bit)) for i in range(count)])


def gather_rows(array, count, order):
    bit_count = bits_of(count)
    own = lax.axis_index("dp")
    current = array.reshape((1,) * bit_count + array.shape)
    for bit in order:
        dim = bit_count - 1 - bit
        other = swap(current, "dp", count, bit)
        current = jnp.where(
            (own >> bit) & 1 == 0,
            jnp.concatenate([current, other], dim),
            jnp.concatenate([other, current], dim),
        )
    return current.reshape((count * array.shape[0],) + array.shape[1:])


def after(array, *others):
    return lax.optimization_barrier((array,) + others)[0]


class Scatter:
    def __init__(self, array, count, order):
        self.count = count
        self.order = list(order)
        self.shape = (array.shape[0] // count,) + array.shape[1:]
        self.current = array.reshape((2,) * bits_of(count) + self.shape)
        self.sent = self.kept = self.received = None

    def send(self):
        if self.order:
            bit = self.order.pop(0)
            dim = bits_of(self.count) - 1 - bit
            mine = (lax.axis_index("dp") >> bit) & 1
            self.sent = lax.dynamic_slice_in_dim(self.current, 1 - mine, 1, dim)
            self.sent = self.sent.astype(jnp.bfloat16)
            self.kept = lax.dynamic_slice_in_dim(self.current, mine, 1, dim)
            self.received = swap(self.sent, "dp", self.count, bit)
        return self

    def take(self, *others):
        if self.received is not None:
            received = after(self.received, *others) if others else self.received
            self.current = self.kept.astype(jnp.float32) + received.astype(jnp.float32)
            self.received = None
        return self

    def merge(self, *others):
        merged = Scatter.__new__(Scatter)
        merged.count, merged.order = self.count, list(self.order)
        every = (self,) + others
        merged.current = jnp.concatenate([one.take().current for one in every], axis=-1)
        merged.shape = self.shape[:-1] + (merged.current.shape[-1],)
        merged.sent = merged.kept = merged.received = None
        return merged

    def finish(self):
        self.take()
        while self.order:
            self.send().take()
        return self.current.reshape(self.shape).astype(jnp.float32)


def sum_all(array, axis, count):
    for bit in range(bits_of(count)):
        array = array + swap(array, axis, count, bit)
    return array


def row_items(unit_pair, row_count, mark_count):
    position = lax.iota(jnp.int32, row_count)
    first_end = unit_pair[0] * mark_count
    second_end = first_end + unit_pair[1] * mark_count
    return jnp.where(position < first_end, 0, jnp.where(position < second_end, 1, 2)).astype(
        jnp.int32
    )


NEGATIVE = -1e30
SCORE_SCALE = 0.125
BLOCK = 128
CHUNK = 256


def dot_with(left, right, left_dim, right_dim):
    return lax.dot_general(
        left, right, (((left_dim,), (right_dim,)), ((), ())), preferred_element_type=jnp.float32
    )


def halves(array):
    high = array.astype(jnp.bfloat16)
    return high, (array - high.astype(jnp.float32)).astype(jnp.bfloat16)


def dot_fine(left, right, left_dim, right_dim):
    left_high, left_low = halves(left)
    right_high, right_low = halves(right)
    return dot_with(
        jnp.concatenate([left_high, left_high, left_low], axis=left_dim),
        jnp.concatenate([right_high, right_low, right_high], axis=right_dim),
        left_dim,
        right_dim,
    )


def dot_low(left, right, left_dim, right_dim):
    return dot_with(left.astype(jnp.bfloat16), right.astype(jnp.bfloat16), left_dim, right_dim)


def item_ends(units_ref):
    first_end = units_ref[0, 0] * LANDMARKS
    return first_end, first_end + units_ref[0, 1] * LANDMARKS


def lane_items(units_ref, row_count):
    first_end, second_end = item_ends(units_ref)
    position = lax.broadcasted_iota(jnp.int32, (1, row_count), 1)
    first = (position < first_end).astype(jnp.float32)
    inside = (position < second_end).astype(jnp.float32)
    return first, inside - first, inside


def landmark_columns(units_ref):
    first_end, second_end = item_ends(units_ref)
    mark = lax.broadcasted_iota(jnp.int32, (2 * LANDMARKS, 1), 0)
    is_first = mark < LANDMARKS
    units = jnp.where(is_first, units_ref[0, 0], units_ref[0, 1])
    start = jnp.where(is_first, 0, first_end)
    low = start + jnp.where(is_first, mark, mark - LANDMARKS) * units
    return is_first, start, jnp.where(is_first, first_end, second_end), low, low + units


def select_matrix(units_ref, row_count):
    _, _, _, low, high = landmark_columns(units_ref)
    position = lax.broadcasted_iota(jnp.int32, (2 * LANDMARKS, row_count), 1)
    return ((position >= low) & (position < high)).astype(jnp.float32).astype(jnp.bfloat16)


def inverse_units(units_ref):
    lane = lax.broadcasted_iota(jnp.int32, (1, 2 * LANDMARKS), 1)
    units = jnp.where(lane < LANDMARKS, units_ref[0, 0], units_ref[0, 1]).astype(jnp.float32)
    return 1.0 / units


def same_item(size):
    row = lax.broadcasted_iota(jnp.int32, (size, size), 0)
    column = lax.broadcasted_iota(jnp.int32, (size, size), 1)
    return (row < LANDMARKS) == (column < LANDMARKS)


def scaled_eye(size, value):
    row = lax.broadcasted_iota(jnp.int32, (size, size), 0)
    column = lax.broadcasted_iota(jnp.int32, (size, size), 1)
    return jnp.where(row == column, value, 0.0)


def column_peaks(matrix):
    sums = jnp.sum(matrix, axis=0, keepdims=True)
    lane = lax.broadcasted_iota(jnp.int32, sums.shape, 1)
    first = jnp.max(jnp.where(lane < LANDMARKS, sums, NEGATIVE), axis=1, keepdims=True)
    second = jnp.max(jnp.where(lane < LANDMARKS, NEGATIVE, sums), axis=1, keepdims=True)
    return sums, jnp.where(lane < LANDMARKS, first, second)


def fill_windows(window_ref, rows, first, second):
    row_count = rows.shape[1]
    lane = lax.broadcasted_iota(jnp.int32, (1, BLOCK), 1)
    before = (lane >= BLOCK - 16).astype(jnp.float32).astype(jnp.bfloat16)
    behind = (lane < 16).astype(jnp.float32).astype(jnp.bfloat16)
    block_count = row_count // BLOCK
    for item, mask in ((0, first), (1, second)):
        kept = rows * mask.astype(jnp.bfloat16)
        for block in range(block_count):
            at = block * BLOCK
            edge = jnp.zeros((rows.shape[0], BLOCK), jnp.bfloat16)
            if block > 0:
                edge = edge + kept[:, at - BLOCK : at] * before
            if block + 1 < block_count:
                edge = edge + kept[:, at + BLOCK : at + 2 * BLOCK] * behind
            base = (2 * block + item) * HEAD_DIM
            window_ref[base : base + HEAD_DIM, :BLOCK] = kept[:, at : at + BLOCK]
            window_ref[base : base + HEAD_DIM, BLOCK:] = edge


def tap_matrix(tap_row):
    return pltpu.roll(
        jnp.broadcast_to(tap_row, (BLOCK, 2 * BLOCK)), 0, axis=1, stride=1, stride_axis=0
    ).astype(jnp.bfloat16)


def attention_forward_body(
    units_ref,
    proj_ref,
    taps_ref,
    attended_ref,
    first_ref,
    last_ref,
    marks_ref,
    middle_ref,
    rough_ref,
    fine_ref,
    values_ref,
    weighted_ref,
    select_ref,
    own_ref,
    in_ref,
    approx_ref,
    window_ref,
    conv_ref,
):
    parts, _, part_width, row_count = proj_ref.shape
    part_heads = part_width // HEAD_DIM
    heads = parts * part_heads
    marks = 2 * LANDMARKS
    select_ref[...] = select_matrix(units_ref, row_count)
    is_first, start, end, _, _ = landmark_columns(units_ref)
    first_end, _ = item_ends(units_ref)
    position = lax.broadcasted_iota(jnp.int32, (marks, row_count), 1)
    in_ref[...] = jnp.where((position >= start) & (position < end), 0.0, NEGATIVE)
    own_ref[...] = jnp.where((position < first_end) == is_first, 0.0, NEGATIVE)
    first, second, inside = lane_items(units_ref, row_count)
    for part in range(parts):
        for kind in range(2):
            sums = dot_with(proj_ref[part, kind], select_ref[...], 1, 1)
            rows = slice(part * part_width, (part + 1) * part_width)
            marks_ref[kind, rows] = sums * inverse_units(units_ref)
    same = same_item(marks)

    def head_start(head, carry):
        at = pl.multiple_of(head * HEAD_DIM, HEAD_DIM)
        part = head // part_heads
        part_at = pl.multiple_of((head - part * part_heads) * HEAD_DIM, HEAD_DIM)
        mark_query = marks_ref[0, pl.ds(at, HEAD_DIM), :]
        mark_key = marks_ref[1, pl.ds(at, HEAD_DIM), :]
        logits = dot_fine(mark_query, mark_key, 0, 0) * SCORE_SCALE
        logits = jnp.where(same, logits, NEGATIVE)
        raised = jnp.exp(logits - jnp.max(logits, axis=1, keepdims=True))
        middle = raised / jnp.sum(raised, axis=1, keepdims=True)
        middle_ref[head] = middle
        _, peak = column_peaks(middle)
        approx_ref[head] = middle.T / peak
        query_rows = (mark_query * SCORE_SCALE).T.astype(jnp.bfloat16)
        scores = dot_with(query_rows, proj_ref[part, 1, pl.ds(part_at, HEAD_DIM), :], 1, 0) + in_ref[...]
        raised = jnp.exp(scores - jnp.max(scores, axis=1, keepdims=True))
        scale = 1.0 / jnp.sum(raised, axis=1, keepdims=True)
        last = (raised * scale).astype(jnp.bfloat16)
        last_ref[head] = last
        values_ref[head] = dot_with(last, proj_ref[part, 2, pl.ds(part_at, HEAD_DIM), :], 1, 1)
        return carry

    lax.fori_loop(0, heads, head_start, 0)

    seven, fifteen, thirteen = (scaled_eye(marks, value) for value in (7.0, 15.0, 13.0))

    def pinv_steps(saved_ref, count):
        kind = saved_ref.dtype

        def one_step(slot, carry):
            approx = [approx_ref[head] for head in range(heads)]
            product = [dot_fine(middle_ref[head], approx[head], 1, 0) for head in range(heads)]
            inner = [
                fifteen - dot_fine(product[head], seven - product[head], 1, 0)
                for head in range(heads)
            ]
            outer = [thirteen - dot_fine(product[head], inner[head], 1, 0) for head in range(heads)]
            for head in range(heads):
                saved_ref[slot, 0, head] = approx[head].astype(kind)
                saved_ref[slot, 1, head] = product[head].astype(kind)
                saved_ref[slot, 2, head] = inner[head].astype(kind)
                saved_ref[slot, 3, head] = outer[head].astype(kind)
                approx_ref[head] = dot_fine(0.25 * approx[head], outer[head], 1, 0)
            return carry

        lax.fori_loop(0, count, one_step, 0)

    pinv_steps(rough_ref, ROUGH_STEPS)
    pinv_steps(fine_ref, PINV_STEPS - ROUGH_STEPS)

    def head_end(head, carry):
        at = pl.multiple_of(head * HEAD_DIM, HEAD_DIM)
        part = head // part_heads
        part_at = pl.multiple_of((head - part * part_heads) * HEAD_DIM, HEAD_DIM)
        weighted = dot_fine(approx_ref[head], values_ref[head], 1, 0)
        weighted_ref[head] = weighted
        weighted_rows = weighted.T.astype(jnp.bfloat16)
        key_rows = (marks_ref[1, pl.ds(at, HEAD_DIM), :] * SCORE_SCALE).T.astype(jnp.bfloat16)
        values = proj_ref[part, 2, pl.ds(part_at, HEAD_DIM), :]
        fill_windows(window_ref, values, first, second)
        conv_ref[...] = dot_with(window_ref[...], tap_matrix(taps_ref[pl.ds(head, 1), :]), 1, 1)
        for chunk in range(row_count // CHUNK):
            lanes = slice(chunk * CHUNK, (chunk + 1) * CHUNK)
            query = proj_ref[part, 0, pl.ds(part_at, HEAD_DIM), lanes]
            scores = dot_with(key_rows, query, 1, 0) + own_ref[:, lanes]
            raised = jnp.exp(scores - jnp.max(scores, axis=0, keepdims=True))
            scale = 1.0 / jnp.sum(raised, axis=0, keepdims=True)
            kept = (raised * scale).astype(jnp.bfloat16)
            first_ref[head, :, lanes] = kept
            mixed = dot_with(weighted_rows, kept, 1, 0) * inside[:, lanes]
            for piece in range(CHUNK // BLOCK):
                block = chunk * (CHUNK // BLOCK) + piece
                base = 2 * block * HEAD_DIM
                columns = slice(block * BLOCK, (block + 1) * BLOCK)
                conv = (
                    conv_ref[base : base + HEAD_DIM] * first[:, columns]
                    + conv_ref[base + HEAD_DIM : base + 2 * HEAD_DIM] * second[:, columns]
                )
                attended_ref[pl.ds(at, HEAD_DIM), columns] = (
                    mixed[:, piece * BLOCK : (piece + 1) * BLOCK] + conv
                ).astype(jnp.bfloat16)
        return carry

    lax.fori_loop(0, heads, head_end, 0)


def whole(count):
    return [pl.BlockSpec(memory_space=pltpu.VMEM)] * count


def attention_forward(item_units, proj, tap_rows):
    width = proj.shape[0] * proj.shape[2]
    row_count = proj.shape[3]
    heads = width // HEAD_DIM
    marks = 2 * LANDMARKS
    square = (heads, marks, marks)
    return pl.pallas_call(
        attention_forward_body,
        in_specs=[pl.BlockSpec(memory_space=pltpu.SMEM)] + whole(2),
        out_specs=whole(9),
        out_shape=[
            jax.ShapeDtypeStruct((width, row_count), jnp.bfloat16),
            jax.ShapeDtypeStruct((heads, marks, row_count), jnp.bfloat16),
            jax.ShapeDtypeStruct((heads, marks, row_count), jnp.bfloat16),
            jax.ShapeDtypeStruct((2, width, marks), jnp.float32),
            jax.ShapeDtypeStruct(square, jnp.float32),
            jax.ShapeDtypeStruct((ROUGH_STEPS, 4) + square, jnp.bfloat16),
            jax.ShapeDtypeStruct((PINV_STEPS - ROUGH_STEPS, 4) + square, jnp.float32),
            jax.ShapeDtypeStruct((heads, marks, HEAD_DIM), jnp.float32),
            jax.ShapeDtypeStruct((heads, marks, HEAD_DIM), jnp.float32),
        ],
        scratch_shapes=[
            pltpu.VMEM((marks, row_count), jnp.bfloat16),
            pltpu.VMEM((marks, row_count), jnp.float32),
            pltpu.VMEM((marks, row_count), jnp.float32),
            pltpu.VMEM(square, jnp.float32),
            pltpu.VMEM((2 * row_count // BLOCK * HEAD_DIM, 2 * BLOCK), jnp.bfloat16),
            pltpu.VMEM((2 * row_count // BLOCK * HEAD_DIM, BLOCK), jnp.float32),
        ],
        compiler_params=pltpu.CompilerParams(vmem_limit_bytes=48 * 1024 * 1024),
        cost_estimate=pl.CostEstimate(flops=20_000_000_000, bytes_accessed=20_000_000, transcendentals=0),
    )(item_units, proj, tap_rows)


def tap_rows_of(kernel):
    half = kernel.shape[1] // 2
    gap = jnp.zeros((kernel.shape[0], 2 * BLOCK - kernel.shape[1]), jnp.float32)
    return jnp.concatenate([kernel[:, half:], gap, kernel[:, :half]], axis=1)

def attention_backward_body(
    units_ref,
    proj_ref,
    taps_ref,
    grad_ref,
    first_ref,
    last_ref,
    marks_ref,
    middle_ref,
    rough_ref,
    fine_ref,
    values_ref,
    weighted_ref,
    out_ref,
    kernel_ref,
    select_ref,
    d_first_ref,
    d_last_ref,
    d_marks_ref,
    d_weighted_ref,
    d_values_ref,
    d_approx_ref,
    d_middle_ref,
    window_ref,
    d_window_ref,
    conv_ref,
):
    width = proj_ref.shape[1]
    row_count = proj_ref.shape[2]
    heads = width // HEAD_DIM
    marks = 2 * LANDMARKS
    select_ref[...] = select_matrix(units_ref, row_count)
    first, second, _ = lane_items(units_ref, row_count)
    inverse = inverse_units(units_ref)
    same = same_item(marks)
    chunks = [slice(at, at + CHUNK) for at in range(0, row_count, CHUNK)]

    def head_start(head, carry):
        at = pl.multiple_of(head * HEAD_DIM, HEAD_DIM)
        weighted_low = weighted_ref[head].astype(jnp.bfloat16)
        for lanes in chunks:
            kept = first_ref[head, :, lanes].astype(jnp.float32)
            d_kept = dot_with(weighted_low, grad_ref[pl.ds(at, HEAD_DIM), lanes], 1, 0)
            scaled = kept * d_kept
            d_scores = scaled - kept * jnp.sum(scaled, axis=0, keepdims=True)
            d_first_ref[head, :, lanes] = d_scores.astype(jnp.bfloat16)
        d_weighted = dot_with(first_ref[head], grad_ref[pl.ds(at, HEAD_DIM), :], 1, 1)
        d_weighted_ref[head] = d_weighted
        d_marks_ref[1, pl.ds(at, HEAD_DIM), :] = SCORE_SCALE * dot_with(
            proj_ref[0, pl.ds(at, HEAD_DIM), :], d_first_ref[head], 1, 1
        )
        d_approx = dot_fine(d_weighted, values_ref[head], 1, 1)
        d_approx_ref[head] = jnp.where(same, d_approx, 0.0)
        inverse_last = dot_fine(
            0.25 * fine_ref[PINV_STEPS - ROUGH_STEPS - 1, 0, head],
            fine_ref[PINV_STEPS - ROUGH_STEPS - 1, 3, head],
            1,
            0,
        )
        d_values_ref[head] = dot_fine(inverse_last, d_weighted, 0, 0)
        d_middle_ref[head] = jnp.zeros((marks, marks), jnp.float32)
        return carry

    lax.fori_loop(0, heads, head_start, 0)

    seven = scaled_eye(marks, 7.0)
    every = range(heads)

    def pinv_steps(saved_ref, count, dot):
        def one_step(step, carry):
            slot = count - 1 - step
            d_next = [d_approx_ref[head] for head in every]
            d_outer = [0.25 * dot(saved_ref[slot, 0, head], d_next[head], 0, 0) for head in every]
            d_inner = [-dot(saved_ref[slot, 1, head], d_outer[head], 0, 0) for head in every]
            d_lowest = [-dot(saved_ref[slot, 1, head], d_inner[head], 0, 0) for head in every]
            for head in every:
                product = saved_ref[slot, 1, head].astype(jnp.float32)
                d_product = (
                    -dot(d_outer[head], saved_ref[slot, 2, head], 1, 1)
                    - dot(d_inner[head], seven - product, 1, 1)
                    - d_lowest[head]
                )
                d_middle_ref[head] += dot(d_product, saved_ref[slot, 0, head], 1, 1)
                d_approx_ref[head] = 0.25 * dot(d_next[head], saved_ref[slot, 3, head], 1, 1) + dot(
                    middle_ref[head], d_product, 0, 0
                )
            return carry

        lax.fori_loop(0, count, one_step, 0)

    pinv_steps(fine_ref, PINV_STEPS - ROUGH_STEPS, dot_fine)
    pinv_steps(rough_ref, ROUGH_STEPS, dot_low)

    lane = lax.broadcasted_iota(jnp.int32, (1, marks), 1)

    def item_sums(row):
        total = jnp.sum(row, axis=1, keepdims=True)
        start = jnp.sum(jnp.where(lane < LANDMARKS, row, 0.0), axis=1, keepdims=True)
        return jnp.where(lane < LANDMARKS, start, total - start)

    def head_middle(head, carry):
        at = pl.multiple_of(head * HEAD_DIM, HEAD_DIM)
        middle = middle_ref[head]
        sums, peak = column_peaks(middle)
        d_start = d_approx_ref[head]
        d_start_turned = (d_start / peak).T
        d_peak = -item_sums(jnp.sum(d_start_turned * middle, axis=0, keepdims=True)) / peak
        at_peak = (sums == peak).astype(jnp.float32)
        d_column = at_peak * d_peak / item_sums(at_peak)
        d_middle = d_middle_ref[head] + d_start_turned + jnp.where(same, d_column, 0.0)
        scaled = middle * d_middle
        d_logits = SCORE_SCALE * (scaled - middle * jnp.sum(scaled, axis=1, keepdims=True))
        rows = pl.ds(at, HEAD_DIM)
        d_marks_ref[0, rows, :] = dot_fine(marks_ref[1, rows, :], d_logits, 1, 1)
        d_marks_ref[1, rows, :] += dot_fine(marks_ref[0, rows, :], d_logits, 1, 0)
        return carry

    lax.fori_loop(0, heads, head_middle, 0)

    row_index = lax.broadcasted_iota(jnp.int32, (BLOCK, BLOCK), 0)
    column_index = lax.broadcasted_iota(jnp.int32, (BLOCK, BLOCK), 1)
    turn = jnp.where(row_index + column_index == BLOCK - 1, 1.0, 0.0).astype(jnp.bfloat16)

    def head_end(head, carry):
        at = pl.multiple_of(head * HEAD_DIM, HEAD_DIM)
        rows = pl.ds(at, HEAD_DIM)
        d_values = d_values_ref[head]
        d_values_low = d_values.astype(jnp.bfloat16)
        d_values_turned = d_values.T.astype(jnp.bfloat16)
        inner = jnp.sum(d_values * values_ref[head], axis=1, keepdims=True)
        for lanes in chunks:
            d_kept = dot_with(d_values_low, proj_ref[2, rows, lanes], 1, 0)
            d_scores = last_ref[head, :, lanes].astype(jnp.float32) * (d_kept - inner)
            d_last_ref[:, lanes] = d_scores.astype(jnp.bfloat16)
        d_query = d_marks_ref[0, rows, :] + SCORE_SCALE * dot_with(
            proj_ref[1, rows, :], d_last_ref[...], 1, 1
        )
        d_query_low = (d_query * inverse).astype(jnp.bfloat16)
        d_key_low = (d_marks_ref[1, rows, :] * inverse).astype(jnp.bfloat16)
        mark_query = (marks_ref[0, rows, :] * SCORE_SCALE).astype(jnp.bfloat16)
        mark_key = (marks_ref[1, rows, :] * SCORE_SCALE).astype(jnp.bfloat16)
        fill_windows(window_ref, proj_ref[2, rows, :], first, second)
        fill_windows(d_window_ref, grad_ref[rows, :], first, second)
        conv_ref[...] = dot_with(d_window_ref[...], tap_matrix(taps_ref[pl.ds(head, 1), :]), 1, 1)
        joined = dot_with(d_window_ref[:, :BLOCK], window_ref[...], 0, 0)
        joined_high, joined_low = halves(joined)
        joined = dot_with(
            jnp.concatenate([turn, turn], axis=1),
            jnp.concatenate([joined_high, joined_low], axis=0),
            1,
            0,
        )
        joined = pltpu.roll(joined, BLOCK + 1, axis=1, stride=1, stride_axis=0)
        kernel_ref[pl.ds(head, 1), :] = jnp.sum(joined, axis=0, keepdims=True)
        for index, lanes in enumerate(chunks):
            select = select_ref[:, lanes]
            out_ref[rows, lanes] = (
                dot_with(mark_key, d_first_ref[head, :, lanes], 1, 0)
                + dot_with(d_query_low, select, 1, 0)
            ).astype(jnp.bfloat16)
            out_ref[pl.ds(width + at, HEAD_DIM), lanes] = (
                dot_with(mark_query, d_last_ref[:, lanes], 1, 0) + dot_with(d_key_low, select, 1, 0)
            ).astype(jnp.bfloat16)
            d_value = dot_with(d_values_turned, last_ref[head, :, lanes], 1, 0)
            for part in range(CHUNK // BLOCK):
                block = index * (CHUNK // BLOCK) + part
                base = 2 * block * HEAD_DIM
                columns = slice(block * BLOCK, (block + 1) * BLOCK)
                conv = (
                    conv_ref[base : base + HEAD_DIM] * first[:, columns]
                    + conv_ref[base + HEAD_DIM : base + 2 * HEAD_DIM] * second[:, columns]
                )
                out_ref[pl.ds(2 * width + at, HEAD_DIM), columns] = (
                    d_value[:, part * BLOCK : (part + 1) * BLOCK] + conv
                ).astype(jnp.bfloat16)
        return carry

    lax.fori_loop(0, heads, head_end, 0)


def attention_backward(item_units, proj, tap_rows, grad, *saved, part):
    parts, _, width, row_count = proj.shape
    heads = width // HEAD_DIM
    marks = 2 * LANDMARKS
    square = (heads, marks, marks)
    thin = (heads, marks, HEAD_DIM)
    stacked = 2 * row_count // BLOCK * HEAD_DIM

    def block(shape, split):
        place = tuple(part if dim == split else 0 for dim in range(len(shape)))
        sizes = tuple(size // parts if dim == split else size for dim, size in enumerate(shape))
        sizes = (None,) + sizes[1:] if len(shape) == 4 and split == 0 else sizes
        return pl.BlockSpec(sizes, lambda step: place, pipeline_mode=pl.Buffered(1))

    splits = (0, None, 0, 0, 0, 1, 0, 2, 2, 0, 0)
    tap_rows = tap_rows[part * heads : (part + 1) * heads]
    arrays = (proj, tap_rows, grad) + saved
    out, joined = pl.pallas_call(
        attention_backward_body,
        grid=(1,),
        in_specs=[pl.BlockSpec(memory_space=pltpu.SMEM)]
        + [block(array.shape, split) for array, split in zip(arrays, splits)],
        out_specs=[
            pl.BlockSpec((3 * width, row_count), lambda step: (0, 0)),
            pl.BlockSpec((heads, 2 * BLOCK), lambda step: (0, 0)),
        ],
        out_shape=[
            jax.ShapeDtypeStruct((3 * width, row_count), jnp.bfloat16),
            jax.ShapeDtypeStruct((heads, 2 * BLOCK), jnp.float32),
        ],
        scratch_shapes=[
            pltpu.VMEM((marks, row_count), jnp.bfloat16),
            pltpu.VMEM((heads, marks, row_count), jnp.bfloat16),
            pltpu.VMEM((marks, row_count), jnp.bfloat16),
            pltpu.VMEM((2, width, marks), jnp.float32),
            pltpu.VMEM(thin, jnp.float32),
            pltpu.VMEM(thin, jnp.float32),
            pltpu.VMEM(square, jnp.float32),
            pltpu.VMEM(square, jnp.float32),
            pltpu.VMEM((stacked, 2 * BLOCK), jnp.bfloat16),
            pltpu.VMEM((stacked, 2 * BLOCK), jnp.bfloat16),
            pltpu.VMEM((stacked, BLOCK), jnp.float32),
        ],
        compiler_params=pltpu.CompilerParams(vmem_limit_bytes=48 * 1024 * 1024),
        cost_estimate=pl.CostEstimate(
            flops=30_000_000_000 // parts, bytes_accessed=20_000_000 // parts, transcendentals=0
        ),
    )(item_units, *arrays)
    half = TAPS // 2
    return out, jnp.concatenate([joined[:, 2 * BLOCK - half :], joined[:, : TAPS - half]], axis=1)


ROWS = 256
GELU_SCALE = 0.7978845608
GELU_CUBE = 0.044715


def row_block(width):
    return pl.BlockSpec((ROWS, width), lambda step: (step, 0))


def fixed_block(shape, column=0):
    return pl.BlockSpec(shape, lambda step: (0, column))


def dense_params():
    return pltpu.CompilerParams(vmem_limit_bytes=56 * 1024 * 1024)


def cost(flops, size):
    return pl.CostEstimate(flops=flops, bytes_accessed=size, transcendentals=0)


def normalized(rows):
    center = rows - jnp.mean(rows, axis=-1, keepdims=True)
    spread = jnp.mean(center * center, axis=-1, keepdims=True)
    scale = lax.rsqrt(spread + NORM_EPS)
    return center * scale, scale


def norm_backward(grad, gain, unit, scale):
    scaled = grad * gain
    lean = jnp.mean(scaled * unit, axis=-1, keepdims=True)
    return scale * (scaled - jnp.mean(scaled, axis=-1, keepdims=True) - unit * lean)


def column_sum(rows):
    return jnp.sum(rows, axis=0, keepdims=True)


def both(own_ref, other_ref):
    return own_ref[...].astype(jnp.float32) + other_ref[...].astype(jnp.float32)


def hidden_forward_body(
    own_ref,
    other_ref,
    tokens_ref,
    weight_ref,
    shared_ref,
    bias_ref,
    expand_ref,
    reduce_ref,
    part_ref,
    hidden_ref,
    low_ref,
    unit_ref,
    scale_ref,
    active_ref,
    slope_ref,
    stat_ref,
):
    branch = both(own_ref, other_ref) + shared_ref[0:1]
    squares = column_sum(weight_ref[...] * branch * branch)

    @pl.when(pl.program_id(0) == 0)
    def _():
        stat_ref[...] = jnp.zeros_like(stat_ref)

    stat_ref[...] += squares
    unit, scale = normalized(tokens_ref[...].astype(jnp.float32) + branch)
    hidden = unit * shared_ref[2:3] + shared_ref[3:4]
    hidden_ref[...] = hidden
    unit_ref[...] = unit.astype(jnp.bfloat16)
    scale_ref[...] = scale
    hidden_low = hidden.astype(jnp.bfloat16)
    low_ref[...] = hidden_low
    total = jnp.zeros(part_ref.shape, jnp.float32)
    units = expand_ref.shape[1]
    for at in range(0, units, 512):
        lanes = slice(at, at + 512)
        expanded = dot_with(hidden_low, expand_ref[:, lanes], 1, 0) + bias_ref[:, lanes]
        square = expanded * expanded
        bend = jnp.tanh(expanded * (GELU_SCALE + (GELU_SCALE * GELU_CUBE) * square))
        half = 0.5 + 0.5 * bend
        active = (expanded * half).astype(jnp.bfloat16)
        active_ref[:, lanes] = active
        slope = half + (0.5 * expanded) * (1.0 - bend * bend) * (
            GELU_SCALE + (3.0 * GELU_SCALE * GELU_CUBE) * square
        )
        slope_ref[:, lanes] = slope.astype(jnp.bfloat16)
        total += dot_with(active, reduce_ref[:, lanes], 1, 1)
    part_ref[...] = total.astype(jnp.bfloat16)


def hidden_forward(own, other, tokens, weight_column, shared_rows, expand_bias, late_full):
    row_count, width = tokens.shape
    units = expand_bias.shape[1]
    return pl.pallas_call(
        hidden_forward_body,
        grid=(row_count // ROWS,),
        in_specs=[
            row_block(width),
            row_block(width),
            row_block(width),
            row_block(1),
            fixed_block((6, width)),
            fixed_block((1, units)),
            fixed_block((width, units), 0),
            fixed_block((width, units), 1),
        ],
        out_specs=[
            row_block(width),
            row_block(width),
            row_block(width),
            row_block(width),
            row_block(1),
            row_block(units),
            row_block(units),
            fixed_block((1, width)),
        ],
        out_shape=[
            jax.ShapeDtypeStruct((row_count, width), jnp.bfloat16),
            jax.ShapeDtypeStruct((row_count, width), jnp.float32),
            jax.ShapeDtypeStruct((row_count, width), jnp.bfloat16),
            jax.ShapeDtypeStruct((row_count, width), jnp.bfloat16),
            jax.ShapeDtypeStruct((row_count, 1), jnp.float32),
            jax.ShapeDtypeStruct((row_count, units), jnp.bfloat16),
            jax.ShapeDtypeStruct((row_count, units), jnp.bfloat16),
            jax.ShapeDtypeStruct((1, width), jnp.float32),
        ],
        compiler_params=dense_params(),
        cost_estimate=cost(4 * row_count * width * units, 30_000_000),
    )(own, other, tokens, weight_column, shared_rows, expand_bias, late_full, late_full)


def hidden_backward_body(
    own_ref,
    other_ref,
    hidden_ref,
    cotangent_ref,
    weight_ref,
    shared_ref,
    expand_ref,
    reduce_ref,
    slope_ref,
    output_ref,
    d_two_ref,
    d_expanded_ref,
    part_ref,
    sums_ref,
    bias_ref,
):
    branch = both(own_ref, other_ref) + shared_ref[1:2]
    weight = weight_ref[...]
    unit, scale = normalized(hidden_ref[...] + branch)
    output_ref[...] = unit * shared_ref[4:5] + shared_ref[5:6]
    grad = cotangent_ref[...].astype(jnp.float32) * weight
    d_res = norm_backward(grad, shared_ref[4:5], unit, scale)
    d_two = d_res.astype(jnp.bfloat16)
    d_two_ref[...] = d_two

    @pl.when(pl.program_id(0) == 0)
    def _():
        sums_ref[...] = jnp.zeros_like(sums_ref)
        bias_ref[...] = jnp.zeros_like(bias_ref)

    sums_ref[...] += jnp.concatenate(
        [
            column_sum(weight * branch * branch),
            column_sum(d_res),
            column_sum(grad * unit),
            column_sum(grad),
            jnp.zeros((4, grad.shape[1]), jnp.float32),
        ],
        axis=0,
    )
    total = jnp.zeros(part_ref.shape, jnp.float32)
    units = expand_ref.shape[1]
    for at in range(0, units, 512):
        lanes = slice(at, at + 512)
        d_active = dot_with(d_two, reduce_ref[:, lanes], 1, 0)
        d_expanded = (slope_ref[:, lanes].astype(jnp.float32) * d_active).astype(jnp.bfloat16)
        d_expanded_ref[:, lanes] = d_expanded
        bias_ref[:, lanes] += column_sum(d_expanded.astype(jnp.float32))
        total += dot_with(d_expanded, expand_ref[:, lanes], 1, 1)
    part_ref[...] = total.astype(jnp.bfloat16)


def hidden_backward(own, other, hidden, cotangent, weight_column, shared_rows, late_full, slope):
    row_count, width = cotangent.shape
    units = slope.shape[1]
    return pl.pallas_call(
        hidden_backward_body,
        grid=(row_count // ROWS,),
        in_specs=[
            row_block(width),
            row_block(width),
            row_block(width),
            row_block(width),
            row_block(1),
            fixed_block((6, width)),
            fixed_block((width, units), 0),
            fixed_block((width, units), 1),
            row_block(units),
        ],
        out_specs=[
            row_block(width),
            row_block(width),
            row_block(units),
            row_block(width),
            fixed_block((8, width)),
            fixed_block((1, units)),
        ],
        out_shape=[
            jax.ShapeDtypeStruct((row_count, width), jnp.float32),
            jax.ShapeDtypeStruct((row_count, width), jnp.bfloat16),
            jax.ShapeDtypeStruct((row_count, units), jnp.bfloat16),
            jax.ShapeDtypeStruct((row_count, width), jnp.bfloat16),
            jax.ShapeDtypeStruct((8, width), jnp.float32),
            jax.ShapeDtypeStruct((1, units), jnp.float32),
        ],
        compiler_params=dense_params(),
        cost_estimate=cost(4 * row_count * width * units, 30_000_000),
    )(own, other, hidden, cotangent, weight_column, shared_rows, late_full, late_full, slope)


def norm_one_body(
    own_ref,
    other_ref,
    d_two_ref,
    unit_ref,
    scale_ref,
    inside_ref,
    shared_ref,
    mixing_ref,
    d_one_ref,
    d_mixed_ref,
    sums_ref,
    turned_ref,
):
    @pl.when(pl.program_id(0) == 0)
    def _():
        sums_ref[...] = jnp.zeros_like(sums_ref)
        turned_ref[...] = mixing_ref[...].astype(jnp.float32).T.astype(jnp.bfloat16)

    grad = both(own_ref, other_ref) + d_two_ref[...].astype(jnp.float32)
    unit = unit_ref[...].astype(jnp.float32)
    d_res = norm_backward(grad, shared_ref[2:3], unit, scale_ref[...])
    d_one = d_res.astype(jnp.bfloat16)
    d_one_ref[...] = d_one
    sums_ref[...] += jnp.concatenate(
        [
            column_sum(d_res),
            column_sum(grad * unit),
            column_sum(grad),
            jnp.zeros((5, grad.shape[1]), jnp.float32),
        ],
        axis=0,
    )
    d_mixed = dot_with(turned_ref[...], d_one, 1, 1) * inside_ref[...]
    d_mixed_ref[...] = d_mixed.astype(jnp.bfloat16)


def norm_one_backward(own, other, d_two, unit, scale, inside_row, shared_rows, late_full, local_width):
    row_count, width = d_two.shape
    return pl.pallas_call(
        norm_one_body,
        grid=(row_count // ROWS,),
        in_specs=[
            row_block(width),
            row_block(width),
            row_block(width),
            row_block(width),
            row_block(1),
            pl.BlockSpec((1, ROWS), lambda step: (0, step)),
            fixed_block((6, width)),
            fixed_block((width, local_width), late_full.shape[1] // local_width - 1),
        ],
        out_specs=[
            row_block(width),
            pl.BlockSpec((local_width, ROWS), lambda step: (0, step)),
            fixed_block((8, width)),
        ],
        out_shape=[
            jax.ShapeDtypeStruct((row_count, width), jnp.bfloat16),
            jax.ShapeDtypeStruct((local_width, row_count), jnp.bfloat16),
            jax.ShapeDtypeStruct((8, width), jnp.float32),
        ],
        scratch_shapes=[pltpu.VMEM((local_width, width), jnp.bfloat16)],
        compiler_params=dense_params(),
        cost_estimate=cost(2 * row_count * width * local_width, 14_000_000),
    )(own, other, d_two, unit, scale, inside_row, shared_rows, late_full)


def turned_dot_body(*refs):
    *pairs, out_ref = refs
    total = jnp.zeros(out_ref.shape, jnp.float32)
    for at in range(0, len(pairs), 2):
        left = pairs[at][...]
        left = left.reshape(-1, left.shape[-1])
        total += dot_with(left, pairs[at + 1][...], 0, 1)
    out_ref[...] = total.astype(jnp.bfloat16)


def turned_dot(lefts, rights, columns, width):
    row_count = lefts[0].shape[-1]
    specs, arrays, terms = [], [], 0
    for left, right, column in zip(lefts, rights, columns):
        shape = left.shape[:-1] + (ROWS,)
        place = (0,) * (left.ndim - 1)
        specs.append(pl.BlockSpec(shape, lambda step, place=place: place + (step,)))
        depth = left.size // row_count
        specs.append(fixed_block((width, depth), column))
        arrays += [left, right]
        terms += depth
    return pl.pallas_call(
        turned_dot_body,
        grid=(row_count // ROWS,),
        in_specs=specs,
        out_specs=row_block(width),
        out_shape=jax.ShapeDtypeStruct((row_count, width), jnp.bfloat16),
        compiler_params=dense_params(),
        cost_estimate=cost(2 * row_count * width * terms, 8_000_000),
    )(*arrays)

def project_body(first_ref, second_ref, tokens_ref, bias_ref, out_ref, turned_ref):
    part_width = first_ref.shape[1]

    @pl.when(pl.program_id(0) == 0)
    def _():
        for part, weight_ref in enumerate((first_ref, second_ref)):
            turned = weight_ref[...].astype(jnp.float32).T
            turned_ref[part * part_width : (part + 1) * part_width] = turned.astype(jnp.bfloat16)

    rows = dot_with(turned_ref[...], tokens_ref[...], 1, 1) + bias_ref[...]
    out_ref[...] = rows.astype(jnp.bfloat16).reshape(out_ref.shape)


def project(first, second, tokens, bias_column):
    row_count, width = tokens.shape
    part_width = first.shape[1]
    shape = (2, 3, part_width // 3, row_count)
    return pl.pallas_call(
        project_body,
        grid=(row_count // ROWS,),
        in_specs=[
            fixed_block((width, part_width)),
            fixed_block((width, part_width)),
            row_block(width),
            fixed_block((2 * part_width, 1)),
        ],
        out_specs=pl.BlockSpec(shape[:3] + (ROWS,), lambda step: (0, 0, 0, step)),
        out_shape=jax.ShapeDtypeStruct(shape, jnp.bfloat16),
        scratch_shapes=[pltpu.VMEM((2 * part_width, width), jnp.bfloat16)],
        compiler_params=dense_params(),
        cost_estimate=cost(4 * row_count * width * part_width, 8_000_000),
    )(first, second, tokens, bias_column)


def adamw(master, moment, square, gradient, factor, learn_rate, decay_rate):
    clipped = gradient * factor
    moment_new = BETA_ONE * moment + (1.0 - BETA_ONE) * clipped
    square_new = BETA_TWO * square + (1.0 - BETA_TWO) * clipped * clipped
    step_size = moment_new / CORRECT_ONE / (jnp.sqrt(square_new / CORRECT_TWO) + ADAM_EPS)
    return (master - learn_rate * (step_size + decay_rate * master), moment_new, square_new)


def body(
    tokens,
    cotangent,
    item_units,
    counted,
    inputs_weight,
    inputs_moment,
    inputs_square,
    mixing_weight,
    mixing_moment,
    mixing_square,
    expand_weight,
    expand_moment,
    expand_square,
    reduce_weight,
    reduce_moment,
    reduce_square,
    biases_weight,
    biases_moment,
    biases_square,
    shared_weight,
    shared_moment,
    shared_square,
    kernel_weight,
    kernel_moment,
    kernel_square,
):
    dp_count = lax.axis_size("dp")
    bits = list(range(bits_of(dp_count)))
    first_order, second_order = bits, bits[:2][::-1] + bits[2:]
    row_count, width_full = tokens.shape
    local_width = inputs_weight.shape[2]
    shard_rows = inputs_weight.shape[1]
    bias_share = biases_weight.shape[1]
    hidden_units = expand_weight.shape[1]
    part_width = local_width // 2
    part_lanes = [slice(0, part_width), slice(part_width, local_width)]

    late_low = jnp.concatenate(
        [expand_weight.astype(jnp.bfloat16)]
        + [weight.astype(jnp.bfloat16).T for weight in (reduce_weight, mixing_weight)],
        axis=1,
    )
    small_low = jnp.concatenate([biases_weight.reshape(-1), shared_weight.reshape(-1)])
    small_low = jnp.pad(small_low, (0, (-small_low.shape[0]) % (3 * part_width)))
    small_low = small_low.astype(jnp.bfloat16).reshape(-1, 3 * part_width)
    left_low, right_low = [
        jnp.concatenate([inputs_weight[c][:, lanes] for c in range(3)], axis=1).astype(jnp.bfloat16)
        for lanes in part_lanes
    ]
    left_low = jnp.concatenate([left_low, small_low], axis=0)
    left_full = gather_rows(left_low, dp_count, first_order[::-1])
    left_full = left_full.reshape(dp_count, left_low.shape[0], 3 * part_width)
    inputs_left = left_full[:, :shard_rows].reshape(-1, 3 * part_width)
    small_full = left_full[:, shard_rows:].reshape(dp_count, -1)
    inputs_right = gather_rows(right_low, dp_count, second_order[::-1])
    late_full = lax.all_gather(late_low, "dp", axis=0, tiled=True)
    biases_row = small_full[:, :bias_share].reshape(-1).astype(jnp.float32)
    shared_rows = small_full[:, bias_share : bias_share + 6 * shard_rows]
    shared_rows = shared_rows.reshape(dp_count, 6, shard_rows).transpose(1, 0, 2)
    shared_rows = shared_rows.reshape(6, -1).astype(jnp.float32)
    query_bias = biases_row[:local_width]
    value_bias = biases_row[local_width : 2 * local_width]
    expand_bias = biases_row[2 * local_width :][None, :]
    zero_bias = jnp.zeros((part_width,), jnp.float32)
    bias_column = jnp.concatenate(
        [
            piece
            for lanes in part_lanes
            for piece in (query_bias[lanes], zero_bias, value_bias[lanes])
        ]
    )[:, None]

    row_item = row_items(item_units[0], row_count, LANDMARKS)
    inside = (row_item < 2).astype(jnp.float32)
    weight_rows = counted.astype(jnp.float32) * inside
    weight_column = weight_rows[:, None]

    proj = project(inputs_left, inputs_right, tokens, bias_column)
    attended, *saved = attention_forward(item_units, proj, tap_rows_of(kernel_weight))
    mixing_column = late_full.shape[1] // local_width - 1
    own_one = turned_dot([attended], [late_full], [mixing_column], width_full)
    other_one = swap(own_one, "head", 2, 0)
    own_two, hidden_one, hidden_low, unit_one, scale_one, active, slope, stat_one = hidden_forward(
        own_one, other_one, tokens, weight_column, shared_rows, expand_bias, late_full
    )
    other_two = swap(own_two, "head", 2, 0)
    output_rows, d_two, d_expanded, own_three, sums_two, expand_sums = hidden_backward(
        own_two, other_two, hidden_one, cotangent, weight_column, shared_rows, late_full, slope
    )
    other_three = swap(own_three, "head", 2, 0)
    reduce_grad = jnp.einsum("rd,rf->df", d_two, active, preferred_element_type=jnp.float32)
    expand_grad = jnp.einsum("rd,rf->df", hidden_low, d_expanded, preferred_element_type=jnp.float32)
    reduce_scatter = Scatter(reduce_grad.astype(jnp.bfloat16), dp_count, second_order).send()
    expand_scatter = Scatter(expand_grad.astype(jnp.bfloat16), dp_count, first_order).send()
    d_one, d_mixed, sums_one = norm_one_backward(
        own_three,
        other_three,
        d_two,
        unit_one,
        scale_one,
        inside[None, :],
        shared_rows,
        late_full,
        local_width,
    )
    mixing_grad = jnp.einsum("rd,kr->dk", d_one, attended, preferred_element_type=jnp.float32)
    mixing_scatter = Scatter(mixing_grad.astype(jnp.bfloat16), dp_count, first_order).send()
    first_scatters = (reduce_scatter, expand_scatter, mixing_scatter)
    d_mixed = after(d_mixed, *[scatter.sent for scatter in first_scatters])
    back_taps = tap_rows_of(kernel_weight[:, ::-1])
    d_left, kernel_left = attention_backward(item_units, proj, back_taps, d_mixed, *saved, part=0)

    def inputs_part(gradient):
        product = jnp.einsum("rd,kr->dk", tokens, gradient, preferred_element_type=jnp.float32)
        return product.astype(jnp.bfloat16)

    for scatter in first_scatters:
        scatter.take(d_left).send()
    left_scatter = Scatter(inputs_part(d_left), dp_count, second_order).send()
    d_mixed = after(d_mixed, left_scatter.sent, *[scatter.sent for scatter in first_scatters])
    d_right, kernel_right = attention_backward(item_units, proj, back_taps, d_mixed, *saved, part=1)
    right_scatter = Scatter(inputs_part(d_right), dp_count, first_order).send()
    for scatter in first_scatters:
        scatter.take(d_right)
    hidden_scatter = expand_scatter.merge(reduce_scatter).send()
    left_scatter.take(d_right).send()
    d_both = after(d_right, right_scatter.sent, hidden_scatter.sent, left_scatter.sent)
    own_four = turned_dot([d_left, d_both], [inputs_left, inputs_right], [0, 0], width_full)
    other_four = swap(own_four, "head", 2, 0)
    right_scatter.take(own_four).send()
    inputs_scatter = right_scatter.merge(left_scatter, mixing_scatter)

    kernel_grad = jnp.concatenate([kernel_left, kernel_right], axis=0)
    left_sums, right_sums = [
        jnp.sum(gradient.astype(jnp.float32), axis=1).reshape(3, part_width)
        for gradient in (d_left, d_right)
    ]
    bias_size = 2 * local_width + hidden_units
    small_parts = [
        left_sums[0],
        right_sums[0],
        left_sums[2],
        right_sums[2],
        expand_sums.reshape(-1),
        sums_one[0],
        sums_two[1],
        sums_one[1],
        sums_one[2],
        sums_two[2],
        sums_two[3],
        kernel_grad.reshape(-1),
    ]
    small_size = sum(part.shape[0] for part in small_parts)
    small_count = (small_size + 1023) // 1024 * 8
    small_parts.append(jnp.zeros((small_count * 128 - small_size,), jnp.float32))
    small_total = jnp.concatenate(small_parts).reshape(small_count, 128)
    small_total = sum_all(small_total, "dp", dp_count).reshape(-1)
    dp_index = lax.axis_index("dp")
    biases_share = lax.dynamic_slice_in_dim(small_total, dp_index * bias_share, bias_share)[None, :]
    shared_total = small_total[bias_size : bias_size + 6 * width_full].reshape(6, width_full)
    shared_share = lax.dynamic_slice_in_dim(shared_total, dp_index * shard_rows, shard_rows, axis=1)
    kernel_total = small_total[bias_size + 6 * width_full : small_size].reshape(kernel_grad.shape)

    hidden_share = hidden_scatter.finish()
    expand_share, reduce_share = hidden_share[:, :hidden_units], hidden_share[:, hidden_units:].T
    merged_share = inputs_scatter.finish()
    columns = 3 * part_width
    right_share, left_share = [
        merged_share[:, at : at + columns].reshape(shard_rows, 3, part_width)
        for at in (0, columns)
    ]
    mixing_share = merged_share[:, 2 * columns :].T
    inputs_share = jnp.concatenate([left_share, right_share], axis=2).transpose(1, 0, 2)
    input_grad = (
        own_four.astype(jnp.float32) + other_four.astype(jnp.float32) + d_one.astype(jnp.float32)
    )
    local_stats = jnp.stack([jnp.sum(stat_one), jnp.sum(sums_two[0]), jnp.sum(weight_rows)])
    kernel_squares = jnp.where(lax.axis_index("dp") == 0, jnp.sum(kernel_total * kernel_total), 0.0)
    local_squares = (
        jnp.sum(inputs_share * inputs_share)
        + jnp.sum(mixing_share * mixing_share)
        + jnp.sum(expand_share * expand_share)
        + jnp.sum(reduce_share * reduce_share)
        + jnp.sum(biases_share * biases_share)
    )
    local_squares = (
        local_squares
        + jnp.where(lax.axis_index("head") == 0, jnp.sum(shared_share * shared_share), 0.0)
        + kernel_squares
    )
    final_row = jnp.concatenate([local_squares[None], local_stats, jnp.zeros((124,), jnp.float32)])
    final_row = sum_all(sum_all(final_row[None, :], "head", 2), "dp", dp_count)[0]
    squares_total, summed_stats = final_row[0], final_row[1:4]
    grad_norm = jnp.sqrt(squares_total)
    factor = CLIP_NORM / (grad_norm + CLIP_EPS)
    inputs_master, inputs_momentum, inputs_variance = adamw(
        inputs_weight, inputs_moment, inputs_square, inputs_share, factor, RATE_MATRIX, WEIGHT_DECAY
    )
    mixing_master, mixing_momentum, mixing_variance = adamw(
        mixing_weight, mixing_moment, mixing_square, mixing_share, factor, RATE_MATRIX, WEIGHT_DECAY
    )
    expand_master, expand_momentum, expand_variance = adamw(
        expand_weight, expand_moment, expand_square, expand_share, factor, RATE_MATRIX, WEIGHT_DECAY
    )
    reduce_master, reduce_momentum, reduce_variance = adamw(
        reduce_weight, reduce_moment, reduce_square, reduce_share, factor, RATE_MATRIX, WEIGHT_DECAY
    )
    biases_master, biases_momentum, biases_variance = adamw(
        biases_weight, biases_moment, biases_square, biases_share, factor, RATE_VECTOR, 0.0
    )
    shared_master, shared_momentum, shared_variance = adamw(
        shared_weight, shared_moment, shared_square, shared_share, factor, RATE_VECTOR, 0.0
    )
    kernel_master, kernel_momentum, kernel_variance = adamw(
        kernel_weight, kernel_moment, kernel_square, kernel_total, factor, RATE_VECTOR, 0.0
    )
    sublayer_rms = jnp.sqrt(summed_stats[:2] / (summed_stats[2] * width_full))
    return (
        output_rows,
        input_grad,
        inputs_master,
        inputs_momentum,
        inputs_variance,
        mixing_master,
        mixing_momentum,
        mixing_variance,
        expand_master,
        expand_momentum,
        expand_variance,
        reduce_master,
        reduce_momentum,
        reduce_variance,
        biases_master,
        biases_momentum,
        biases_variance,
        shared_master,
        shared_momentum,
        shared_variance,
        kernel_master,
        kernel_momentum,
        kernel_variance,
        grad_norm,
        sublayer_rms,
    )


def solution(mesh):
    placed = (
        P("dp", None),
        P("dp", None),
        P("dp", None),
        P("dp"),
        P(None, "dp", "head"),
        P(None, "dp", "head"),
        P(None, "dp", "head"),
        P("head", "dp"),
        P("head", "dp"),
        P("head", "dp"),
        P("dp", "head"),
        P("dp", "head"),
        P("dp", "head"),
        P("head", "dp"),
        P("head", "dp"),
        P("head", "dp"),
        P("head", "dp"),
        P("head", "dp"),
        P("head", "dp"),
        P(None, "dp"),
        P(None, "dp"),
        P(None, "dp"),
        P("head", None),
        P("head", None),
        P("head", None),
    )
    return jax.shard_map(
        body,
        mesh=mesh,
        in_specs=placed,
        out_specs=(
            P("dp", None),
            P("dp", None),
            P(None, "dp", "head"),
            P(None, "dp", "head"),
            P(None, "dp", "head"),
            P("head", "dp"),
            P("head", "dp"),
            P("head", "dp"),
            P("dp", "head"),
            P("dp", "head"),
            P("dp", "head"),
            P("head", "dp"),
            P("head", "dp"),
            P("head", "dp"),
            P("head", "dp"),
            P("head", "dp"),
            P("head", "dp"),
            P(None, "dp"),
            P(None, "dp"),
            P(None, "dp"),
            P("head", None),
            P("head", None),
            P("head", None),
            P(),
            P(),
        ),
        check_vma=False,
    )
```

```python
import functools

import jax
import jax.numpy as jnp
from jax import lax
from jax.experimental import pallas as pl
from jax.experimental.pallas import tpu as pltpu
from jax.sharding import PartitionSpec as P

HEAD_DIM = 64
LANDMARKS = 64
PINV_STEPS = 6
ROUGH_STEPS = 4
TAPS = 33
NORM_EPS = 1e-05
CLIP_NORM = 1.0
CLIP_EPS = 1e-06
BETA_ONE = 0.9
BETA_TWO = 0.98
ADAM_EPS = 1e-08
RATE_MATRIX = 0.04
RATE_VECTOR = 0.5
WEIGHT_DECAY = 0.01
CORRECT_ONE = 1.0 - BETA_ONE**5
CORRECT_TWO = 1.0 - BETA_TWO**5

def bits_of(count):
    bit_count = 0
    while (1 << bit_count) < count:
        bit_count += 1
    return bit_count


def swap(array, axis, count, bit):
    return lax.ppermute(array, axis, [(i, i ^ (1 << bit)) for i in range(count)])


class Gather:
    def __init__(self, array, count, order):
        self.count, self.order = count, list(order)
        self.shape = (count * array.shape[0],) + array.shape[1:]
        self.current = array.reshape((1,) * bits_of(count) + array.shape)

    def step(self, *others):
        bit = self.order.pop(0)
        dim = bits_of(self.count) - 1 - bit
        other = swap(self.current, "dp", self.count, bit)
        other = after(other, *others) if others else other
        self.current = jnp.where(
            (lax.axis_index("dp") >> bit) & 1 == 0,
            jnp.concatenate([self.current, other], dim),
            jnp.concatenate([other, self.current], dim),
        )
        return self

    def split(self, sizes, dim, orders):
        pieces, at = [], 0
        for size, order in zip(sizes, orders):
            piece = Gather.__new__(Gather)
            piece.count, piece.order = self.count, list(order)
            axis = self.current.ndim + dim
            piece.current = lax.slice_in_dim(self.current, at, at + size, axis=axis)
            rows = self.count * piece.current.shape[-2]
            piece.shape = (rows, piece.current.shape[-1])
            pieces.append(piece)
            at += size
        return pieces

    def finish(self):
        while self.order:
            self.step()
        return self.current.reshape(self.shape)


def after(array, *others):
    return lax.optimization_barrier((array,) + others)[0]


class Scatter:
    def __init__(self, arrays, count, order, join=-1):
        self.count = count
        self.join = join
        self.order = list(order)
        self.shapes = [(array.shape[0] // count,) + array.shape[1:] for array in arrays]
        lead = (2,) * bits_of(count)
        self.currents = [array.reshape(lead + shape) for array, shape in zip(arrays, self.shapes)]
        self.sent = self.kept = self.received = None

    def send(self):
        if self.order:
            bit = self.order.pop(0)
            dim = bits_of(self.count) - 1 - bit
            mine = (lax.axis_index("dp") >> bit) & 1
            sent = [
                lax.dynamic_slice_in_dim(current, 1 - mine, 1, dim).astype(jnp.bfloat16)
                for current in self.currents
            ]
            self.sent = sent[0] if len(sent) == 1 else jnp.concatenate(sent, axis=self.join)
            self.kept = [
                lax.dynamic_slice_in_dim(current, mine, 1, dim) for current in self.currents
            ]
            self.received = swap(self.sent, "dp", self.count, bit)
        return self

    def take(self, *others):
        if self.received is not None:
            received = after(self.received, *others) if others else self.received
            currents, at = [], 0
            for kept in self.kept:
                size = kept.shape[self.join]
                piece = lax.slice_in_dim(received, at, at + size, axis=self.join % kept.ndim)
                currents.append(kept.astype(jnp.float32) + piece.astype(jnp.float32))
                at += size
            self.currents, self.received = currents, None
        return self

    def merge(self, *others, join=-1):
        every = (self,) + others
        merged = Scatter([], self.count, self.order, join)
        merged.shapes = [shape for one in every for shape in one.shapes]
        merged.currents = [current for one in every for current in one.take().currents]
        return merged

    def finish(self):
        self.take()
        while self.order:
            self.send().take()
        pairs = zip(self.currents, self.shapes)
        return [current.reshape(shape).astype(jnp.float32) for current, shape in pairs]


def sum_all(array, axis, count):
    for bit in range(bits_of(count)):
        array = array + swap(array, axis, count, bit)
    return array


def row_items(unit_pair, row_count, mark_count):
    position = lax.iota(jnp.int32, row_count)
    first_end = unit_pair[0] * mark_count
    second_end = first_end + unit_pair[1] * mark_count
    return jnp.where(position < first_end, 0, jnp.where(position < second_end, 1, 2)).astype(
        jnp.int32
    )


NEGATIVE = -1e30
SCORE_SCALE = 0.125
BLOCK = 128
CHUNK = 256


def dot_with(left, right, left_dim, right_dim):
    return lax.dot_general(
        left, right, (((left_dim,), (right_dim,)), ((), ())), preferred_element_type=jnp.float32
    )


def halves(array):
    high = array.astype(jnp.bfloat16)
    return high, (array - high.astype(jnp.float32)).astype(jnp.bfloat16)


def dot_fine(left, right, left_dim, right_dim):
    left_high, left_low = halves(left)
    right_high, right_low = halves(right)
    return dot_with(
        jnp.concatenate([left_high, left_high, left_low], axis=left_dim),
        jnp.concatenate([right_high, right_low, right_high], axis=right_dim),
        left_dim,
        right_dim,
    )


def dot_low(left, right, left_dim, right_dim):
    return dot_with(left.astype(jnp.bfloat16), right.astype(jnp.bfloat16), left_dim, right_dim)


def item_ends(units_ref):
    first_end = units_ref[0, 0] * LANDMARKS
    return first_end, first_end + units_ref[0, 1] * LANDMARKS


def lane_items(units_ref, row_count):
    first_end, second_end = item_ends(units_ref)
    position = lax.broadcasted_iota(jnp.int32, (1, row_count), 1)
    first = (position < first_end).astype(jnp.float32)
    inside = (position < second_end).astype(jnp.float32)
    return first, inside - first, inside


def landmark_columns(units_ref):
    first_end, second_end = item_ends(units_ref)
    mark = lax.broadcasted_iota(jnp.int32, (2 * LANDMARKS, 1), 0)
    is_first = mark < LANDMARKS
    units = jnp.where(is_first, units_ref[0, 0], units_ref[0, 1])
    start = jnp.where(is_first, 0, first_end)
    low = start + jnp.where(is_first, mark, mark - LANDMARKS) * units
    return is_first, start, jnp.where(is_first, first_end, second_end), low, low + units


def select_matrix(units_ref, row_count):
    _, _, _, low, high = landmark_columns(units_ref)
    position = lax.broadcasted_iota(jnp.int32, (2 * LANDMARKS, row_count), 1)
    return ((position >= low) & (position < high)).astype(jnp.float32).astype(jnp.bfloat16)


def inverse_units(units_ref):
    lane = lax.broadcasted_iota(jnp.int32, (1, 2 * LANDMARKS), 1)
    units = jnp.where(lane < LANDMARKS, units_ref[0, 0], units_ref[0, 1]).astype(jnp.float32)
    return 1.0 / units


def same_item(size):
    row = lax.broadcasted_iota(jnp.int32, (size, size), 0)
    column = lax.broadcasted_iota(jnp.int32, (size, size), 1)
    return (row < LANDMARKS) == (column < LANDMARKS)


def scaled_eye(size, value):
    row = lax.broadcasted_iota(jnp.int32, (size, size), 0)
    column = lax.broadcasted_iota(jnp.int32, (size, size), 1)
    return jnp.where(row == column, value, 0.0)


def column_peaks(matrix):
    sums = jnp.sum(matrix, axis=0, keepdims=True)
    lane = lax.broadcasted_iota(jnp.int32, sums.shape, 1)
    first = jnp.max(jnp.where(lane < LANDMARKS, sums, NEGATIVE), axis=1, keepdims=True)
    second = jnp.max(jnp.where(lane < LANDMARKS, NEGATIVE, sums), axis=1, keepdims=True)
    return sums, jnp.where(lane < LANDMARKS, first, second)


def fill_windows(window_ref, rows, first, second):
    row_count = rows.shape[1]
    lane = lax.broadcasted_iota(jnp.int32, (1, BLOCK), 1)
    before = (lane >= BLOCK - 16).astype(jnp.float32).astype(jnp.bfloat16)
    behind = (lane < 16).astype(jnp.float32).astype(jnp.bfloat16)
    block_count = row_count // BLOCK
    for item, mask in ((0, first), (1, second)):
        kept = rows * mask.astype(jnp.bfloat16)
        for block in range(block_count):
            at = block * BLOCK
            edge = jnp.zeros((rows.shape[0], BLOCK), jnp.bfloat16)
            if block > 0:
                edge = edge + kept[:, at - BLOCK : at] * before
            if block + 1 < block_count:
                edge = edge + kept[:, at + BLOCK : at + 2 * BLOCK] * behind
            base = (2 * block + item) * HEAD_DIM
            window_ref[base : base + HEAD_DIM, :BLOCK] = kept[:, at : at + BLOCK]
            window_ref[base : base + HEAD_DIM, BLOCK:] = edge


def tap_matrix(tap_row):
    return pltpu.roll(
        jnp.broadcast_to(tap_row, (BLOCK, 2 * BLOCK)), 0, axis=1, stride=1, stride_axis=0
    ).astype(jnp.bfloat16)


def attention_start_body(
    units_ref,
    proj_ref,
    marks_ref,
    middle_ref,
    last_ref,
    values_ref,
    approx_ref,
    select_ref,
    in_ref,
):
    parts, _, part_width, row_count = proj_ref.shape
    part_heads = part_width // HEAD_DIM
    heads = parts * part_heads
    marks = 2 * LANDMARKS
    select_ref[...] = select_matrix(units_ref, row_count)
    _, start, end, _, _ = landmark_columns(units_ref)
    position = lax.broadcasted_iota(jnp.int32, (marks, row_count), 1)
    in_ref[...] = jnp.where((position >= start) & (position < end), 0.0, NEGATIVE)
    for part in range(parts):
        for kind in range(2):
            sums = dot_with(proj_ref[part, kind], select_ref[...], 1, 1)
            rows = slice(part * part_width, (part + 1) * part_width)
            marks_ref[kind, rows] = sums * inverse_units(units_ref)
    same = same_item(marks)

    def head_start(head, carry):
        at = pl.multiple_of(head * HEAD_DIM, HEAD_DIM)
        part = head // part_heads
        part_at = pl.multiple_of((head - part * part_heads) * HEAD_DIM, HEAD_DIM)
        mark_query = marks_ref[0, pl.ds(at, HEAD_DIM), :]
        mark_key = marks_ref[1, pl.ds(at, HEAD_DIM), :]
        logits = dot_fine(mark_query, mark_key, 0, 0) * SCORE_SCALE
        logits = jnp.where(same, logits, NEGATIVE)
        raised = jnp.exp(logits - jnp.max(logits, axis=1, keepdims=True))
        middle = raised / jnp.sum(raised, axis=1, keepdims=True)
        middle_ref[head] = middle
        _, peak = column_peaks(middle)
        approx_ref[head] = middle.T / peak
        query_rows = (mark_query * SCORE_SCALE).T.astype(jnp.bfloat16)
        scores = dot_with(query_rows, proj_ref[part, 1, pl.ds(part_at, HEAD_DIM), :], 1, 0) + in_ref[...]
        raised = jnp.exp(scores - jnp.max(scores, axis=1, keepdims=True))
        scale = 1.0 / jnp.sum(raised, axis=1, keepdims=True)
        last = (raised * scale).astype(jnp.bfloat16)
        last_ref[head] = last
        values_ref[head] = dot_with(last, proj_ref[part, 2, pl.ds(part_at, HEAD_DIM), :], 1, 1)
        return carry

    lax.fori_loop(0, heads, head_start, 0)


def attention_finish_body(
    units_ref,
    proj_ref,
    taps_ref,
    marks_ref,
    middle_ref,
    values_ref,
    approx_ref,
    attended_ref,
    first_ref,
    rough_ref,
    fine_ref,
    weighted_ref,
    own_ref,
    state_ref,
    window_ref,
    conv_ref,
):
    parts, _, part_width, row_count = proj_ref.shape
    part_heads = part_width // HEAD_DIM
    heads = parts * part_heads
    marks = 2 * LANDMARKS
    is_first = landmark_columns(units_ref)[0]
    first_end, _ = item_ends(units_ref)
    position = lax.broadcasted_iota(jnp.int32, (marks, row_count), 1)
    own_ref[...] = jnp.where((position < first_end) == is_first, 0.0, NEGATIVE)
    first, second, inside = lane_items(units_ref, row_count)
    state_ref[...] = approx_ref[...]
    seven, fifteen, thirteen = (scaled_eye(marks, value) for value in (7.0, 15.0, 13.0))

    def pinv_steps(saved_ref, count):
        kind = saved_ref.dtype

        def one_step(slot, carry):
            approx = [state_ref[head] for head in range(heads)]
            product = [dot_fine(middle_ref[head], approx[head], 1, 0) for head in range(heads)]
            inner = [
                fifteen - dot_fine(product[head], seven - product[head], 1, 0)
                for head in range(heads)
            ]
            outer = [thirteen - dot_fine(product[head], inner[head], 1, 0) for head in range(heads)]
            for head in range(heads):
                saved_ref[slot, 0, head] = approx[head].astype(kind)
                saved_ref[slot, 1, head] = product[head].astype(kind)
                saved_ref[slot, 2, head] = inner[head].astype(kind)
                saved_ref[slot, 3, head] = outer[head].astype(kind)
                state_ref[head] = dot_fine(0.25 * approx[head], outer[head], 1, 0)
            return carry

        lax.fori_loop(0, count, one_step, 0)

    pinv_steps(rough_ref, ROUGH_STEPS)
    pinv_steps(fine_ref, PINV_STEPS - ROUGH_STEPS)

    def head_end(head, carry):
        at = pl.multiple_of(head * HEAD_DIM, HEAD_DIM)
        part = head // part_heads
        part_at = pl.multiple_of((head - part * part_heads) * HEAD_DIM, HEAD_DIM)
        weighted = dot_fine(state_ref[head], values_ref[head], 1, 0)
        weighted_ref[head] = weighted
        weighted_rows = weighted.T.astype(jnp.bfloat16)
        key_rows = (marks_ref[1, pl.ds(at, HEAD_DIM), :] * SCORE_SCALE).T.astype(jnp.bfloat16)
        values = proj_ref[part, 2, pl.ds(part_at, HEAD_DIM), :]
        fill_windows(window_ref, values, first, second)
        conv_ref[...] = dot_with(window_ref[...], tap_matrix(taps_ref[pl.ds(head, 1), :]), 1, 1)
        for chunk in range(row_count // CHUNK):
            lanes = slice(chunk * CHUNK, (chunk + 1) * CHUNK)
            query = proj_ref[part, 0, pl.ds(part_at, HEAD_DIM), lanes]
            scores = dot_with(key_rows, query, 1, 0) + own_ref[:, lanes]
            raised = jnp.exp(scores - jnp.max(scores, axis=0, keepdims=True))
            scale = 1.0 / jnp.sum(raised, axis=0, keepdims=True)
            kept = (raised * scale).astype(jnp.bfloat16)
            first_ref[head, :, lanes] = kept
            mixed = dot_with(weighted_rows, kept, 1, 0) * inside[:, lanes]
            for piece in range(CHUNK // BLOCK):
                block = chunk * (CHUNK // BLOCK) + piece
                base = 2 * block * HEAD_DIM
                columns = slice(block * BLOCK, (block + 1) * BLOCK)
                conv = (
                    conv_ref[base : base + HEAD_DIM] * first[:, columns]
                    + conv_ref[base + HEAD_DIM : base + 2 * HEAD_DIM] * second[:, columns]
                )
                attended_ref[pl.ds(at, HEAD_DIM), columns] = (
                    mixed[:, piece * BLOCK : (piece + 1) * BLOCK] + conv
                ).astype(jnp.bfloat16)
        return carry

    lax.fori_loop(0, heads, head_end, 0)


def whole(count):
    return [pl.BlockSpec(memory_space=pltpu.VMEM)] * count


def attention_sizes(proj):
    parts, _, part_width, row_count = proj.shape
    width = parts * part_width
    heads = width // HEAD_DIM
    marks = 2 * LANDMARKS
    return width, row_count, heads, marks, (heads, marks, marks), (heads, marks, HEAD_DIM)


def attention_start(item_units, proj):
    width, row_count, heads, marks, square, thin = attention_sizes(proj)
    return pl.pallas_call(
        attention_start_body,
        in_specs=[pl.BlockSpec(memory_space=pltpu.SMEM)]
        + whole(1),
        out_specs=whole(5),
        out_shape=[
            jax.ShapeDtypeStruct((2, width, marks), jnp.float32),
            jax.ShapeDtypeStruct(square, jnp.float32),
            jax.ShapeDtypeStruct((heads, marks, row_count), jnp.bfloat16),
            jax.ShapeDtypeStruct(thin, jnp.float32),
            jax.ShapeDtypeStruct(square, jnp.float32),
        ],
        scratch_shapes=[
            pltpu.VMEM((marks, row_count), jnp.bfloat16),
            pltpu.VMEM((marks, row_count), jnp.float32),
        ],
        compiler_params=pltpu.CompilerParams(vmem_limit_bytes=48 * 1024 * 1024),
        cost_estimate=pl.CostEstimate(
            flops=9_000_000_000, bytes_accessed=8_000_000, transcendentals=0
        ),
    )(item_units, proj)


def attention_finish(item_units, proj, tap_rows, marks_rows, middle, last, values, approx):
    width, row_count, heads, marks, square, thin = attention_sizes(proj)
    stacked = 2 * row_count // BLOCK * HEAD_DIM
    return pl.pallas_call(
        attention_finish_body,
        in_specs=[pl.BlockSpec(memory_space=pltpu.SMEM)] + whole(6),
        out_specs=whole(5),
        out_shape=[
            jax.ShapeDtypeStruct((width, row_count), jnp.bfloat16),
            jax.ShapeDtypeStruct((heads, marks, row_count), jnp.bfloat16),
            jax.ShapeDtypeStruct((ROUGH_STEPS, 4) + square, jnp.bfloat16),
            jax.ShapeDtypeStruct((PINV_STEPS - ROUGH_STEPS, 4) + square, jnp.float32),
            jax.ShapeDtypeStruct(thin, jnp.float32),
        ],
        scratch_shapes=[
            pltpu.VMEM((marks, row_count), jnp.float32),
            pltpu.VMEM(square, jnp.float32),
            pltpu.VMEM((stacked, 2 * BLOCK), jnp.bfloat16),
            pltpu.VMEM((stacked, BLOCK), jnp.float32),
        ],
        compiler_params=pltpu.CompilerParams(vmem_limit_bytes=48 * 1024 * 1024),
        cost_estimate=pl.CostEstimate(
            flops=18_000_000_000, bytes_accessed=16_000_000, transcendentals=0
        ),
    )(item_units, proj, tap_rows, marks_rows, middle, values, approx)


def tap_rows_of(kernel):
    half = kernel.shape[1] // 2
    gap = jnp.zeros((kernel.shape[0], 2 * BLOCK - kernel.shape[1]), jnp.float32)
    return jnp.concatenate([kernel[:, half:], gap, kernel[:, :half]], axis=1)

def attention_backward_body(
    units_ref,
    proj_ref,
    taps_ref,
    grad_ref,
    first_ref,
    last_ref,
    marks_ref,
    middle_ref,
    rough_ref,
    fine_ref,
    values_ref,
    weighted_ref,
    out_ref,
    kernel_ref,
    select_ref,
    d_first_ref,
    d_last_ref,
    d_marks_ref,
    d_weighted_ref,
    d_values_ref,
    d_approx_ref,
    d_middle_ref,
    window_ref,
    d_window_ref,
    conv_ref,
):
    width = proj_ref.shape[1]
    row_count = proj_ref.shape[2]
    heads = width // HEAD_DIM
    marks = 2 * LANDMARKS
    select_ref[...] = select_matrix(units_ref, row_count)
    first, second, _ = lane_items(units_ref, row_count)
    inverse = inverse_units(units_ref)
    same = same_item(marks)
    chunks = [slice(at, at + CHUNK) for at in range(0, row_count, CHUNK)]

    def head_start(head, carry):
        at = pl.multiple_of(head * HEAD_DIM, HEAD_DIM)
        weighted_low = weighted_ref[head].astype(jnp.bfloat16)
        for lanes in chunks:
            kept = first_ref[head, :, lanes].astype(jnp.float32)
            d_kept = dot_with(weighted_low, grad_ref[pl.ds(at, HEAD_DIM), lanes], 1, 0)
            scaled = kept * d_kept
            d_scores = scaled - kept * jnp.sum(scaled, axis=0, keepdims=True)
            d_first_ref[head, :, lanes] = d_scores.astype(jnp.bfloat16)
        d_weighted = dot_with(first_ref[head], grad_ref[pl.ds(at, HEAD_DIM), :], 1, 1)
        d_weighted_ref[head] = d_weighted
        d_marks_ref[1, pl.ds(at, HEAD_DIM), :] = SCORE_SCALE * dot_with(
            proj_ref[0, pl.ds(at, HEAD_DIM), :], d_first_ref[head], 1, 1
        )
        d_approx = dot_fine(d_weighted, values_ref[head], 1, 1)
        d_approx_ref[head] = jnp.where(same, d_approx, 0.0)
        inverse_last = dot_fine(
            0.25 * fine_ref[PINV_STEPS - ROUGH_STEPS - 1, 0, head],
            fine_ref[PINV_STEPS - ROUGH_STEPS - 1, 3, head],
            1,
            0,
        )
        d_values_ref[head] = dot_fine(inverse_last, d_weighted, 0, 0)
        d_middle_ref[head] = jnp.zeros((marks, marks), jnp.float32)
        return carry

    lax.fori_loop(0, heads, head_start, 0)

    seven = scaled_eye(marks, 7.0)
    every = range(heads)

    def pinv_steps(saved_ref, count, dot):
        def one_step(step, carry):
            slot = count - 1 - step
            d_next = [d_approx_ref[head] for head in every]
            d_outer = [0.25 * dot(saved_ref[slot, 0, head], d_next[head], 0, 0) for head in every]
            d_inner = [-dot(saved_ref[slot, 1, head], d_outer[head], 0, 0) for head in every]
            d_lowest = [-dot(saved_ref[slot, 1, head], d_inner[head], 0, 0) for head in every]
            for head in every:
                product = saved_ref[slot, 1, head].astype(jnp.float32)
                d_product = (
                    -dot(d_outer[head], saved_ref[slot, 2, head], 1, 1)
                    - dot(d_inner[head], seven - product, 1, 1)
                    - d_lowest[head]
                )
                d_middle_ref[head] += dot(d_product, saved_ref[slot, 0, head], 1, 1)
                d_approx_ref[head] = 0.25 * dot(d_next[head], saved_ref[slot, 3, head], 1, 1) + dot(
                    middle_ref[head], d_product, 0, 0
                )
            return carry

        lax.fori_loop(0, count, one_step, 0)

    pinv_steps(fine_ref, PINV_STEPS - ROUGH_STEPS, dot_fine)
    pinv_steps(rough_ref, ROUGH_STEPS, dot_low)

    lane = lax.broadcasted_iota(jnp.int32, (1, marks), 1)

    def item_sums(row):
        total = jnp.sum(row, axis=1, keepdims=True)
        start = jnp.sum(jnp.where(lane < LANDMARKS, row, 0.0), axis=1, keepdims=True)
        return jnp.where(lane < LANDMARKS, start, total - start)

    def head_middle(head, carry):
        at = pl.multiple_of(head * HEAD_DIM, HEAD_DIM)
        middle = middle_ref[head]
        sums, peak = column_peaks(middle)
        d_start = d_approx_ref[head]
        d_start_turned = (d_start / peak).T
        d_peak = -item_sums(jnp.sum(d_start_turned * middle, axis=0, keepdims=True)) / peak
        at_peak = (sums == peak).astype(jnp.float32)
        d_column = at_peak * d_peak / item_sums(at_peak)
        d_middle = d_middle_ref[head] + d_start_turned + jnp.where(same, d_column, 0.0)
        scaled = middle * d_middle
        d_logits = SCORE_SCALE * (scaled - middle * jnp.sum(scaled, axis=1, keepdims=True))
        rows = pl.ds(at, HEAD_DIM)
        d_marks_ref[0, rows, :] = dot_fine(marks_ref[1, rows, :], d_logits, 1, 1)
        d_marks_ref[1, rows, :] += dot_fine(marks_ref[0, rows, :], d_logits, 1, 0)
        return carry

    lax.fori_loop(0, heads, head_middle, 0)

    row_index = lax.broadcasted_iota(jnp.int32, (BLOCK, BLOCK), 0)
    column_index = lax.broadcasted_iota(jnp.int32, (BLOCK, BLOCK), 1)
    turn = jnp.where(row_index + column_index == BLOCK - 1, 1.0, 0.0).astype(jnp.bfloat16)

    def head_end(head, carry):
        at = pl.multiple_of(head * HEAD_DIM, HEAD_DIM)
        rows = pl.ds(at, HEAD_DIM)
        d_values = d_values_ref[head]
        d_values_low = d_values.astype(jnp.bfloat16)
        d_values_turned = d_values.T.astype(jnp.bfloat16)
        inner = jnp.sum(d_values * values_ref[head], axis=1, keepdims=True)
        for lanes in chunks:
            d_kept = dot_with(d_values_low, proj_ref[2, rows, lanes], 1, 0)
            d_scores = last_ref[head, :, lanes].astype(jnp.float32) * (d_kept - inner)
            d_last_ref[:, lanes] = d_scores.astype(jnp.bfloat16)
        d_query = d_marks_ref[0, rows, :] + SCORE_SCALE * dot_with(
            proj_ref[1, rows, :], d_last_ref[...], 1, 1
        )
        d_query_low = (d_query * inverse).astype(jnp.bfloat16)
        d_key_low = (d_marks_ref[1, rows, :] * inverse).astype(jnp.bfloat16)
        mark_query = (marks_ref[0, rows, :] * SCORE_SCALE).astype(jnp.bfloat16)
        mark_key = (marks_ref[1, rows, :] * SCORE_SCALE).astype(jnp.bfloat16)
        fill_windows(window_ref, proj_ref[2, rows, :], first, second)
        fill_windows(d_window_ref, grad_ref[rows, :], first, second)
        conv_ref[...] = dot_with(d_window_ref[...], tap_matrix(taps_ref[pl.ds(head, 1), :]), 1, 1)
        joined = dot_with(d_window_ref[:, :BLOCK], window_ref[...], 0, 0)
        joined_high, joined_low = halves(joined)
        joined = dot_with(
            jnp.concatenate([turn, turn], axis=1),
            jnp.concatenate([joined_high, joined_low], axis=0),
            1,
            0,
        )
        joined = pltpu.roll(joined, BLOCK + 1, axis=1, stride=1, stride_axis=0)
        kernel_ref[pl.ds(head, 1), :] = jnp.sum(joined, axis=0, keepdims=True)
        for index, lanes in enumerate(chunks):
            select = select_ref[:, lanes]
            out_ref[rows, lanes] = (
                dot_with(mark_key, d_first_ref[head, :, lanes], 1, 0)
                + dot_with(d_query_low, select, 1, 0)
            ).astype(jnp.bfloat16)
            out_ref[pl.ds(width + at, HEAD_DIM), lanes] = (
                dot_with(mark_query, d_last_ref[:, lanes], 1, 0) + dot_with(d_key_low, select, 1, 0)
            ).astype(jnp.bfloat16)
            d_value = dot_with(d_values_turned, last_ref[head, :, lanes], 1, 0)
            for part in range(CHUNK // BLOCK):
                block = index * (CHUNK // BLOCK) + part
                base = 2 * block * HEAD_DIM
                columns = slice(block * BLOCK, (block + 1) * BLOCK)
                conv = (
                    conv_ref[base : base + HEAD_DIM] * first[:, columns]
                    + conv_ref[base + HEAD_DIM : base + 2 * HEAD_DIM] * second[:, columns]
                )
                out_ref[pl.ds(2 * width + at, HEAD_DIM), columns] = (
                    d_value[:, part * BLOCK : (part + 1) * BLOCK] + conv
                ).astype(jnp.bfloat16)
        return carry

    lax.fori_loop(0, heads, head_end, 0)


def attention_backward(item_units, proj, tap_rows, grad, *saved, part):
    parts, _, width, row_count = proj.shape
    heads = width // HEAD_DIM
    marks = 2 * LANDMARKS
    square = (heads, marks, marks)
    thin = (heads, marks, HEAD_DIM)
    stacked = 2 * row_count // BLOCK * HEAD_DIM

    def block(shape, split):
        place = tuple(part if dim == split else 0 for dim in range(len(shape)))
        sizes = tuple(size // parts if dim == split else size for dim, size in enumerate(shape))
        sizes = (None,) + sizes[1:] if len(shape) == 4 and split == 0 else sizes
        return pl.BlockSpec(sizes, lambda step: place, pipeline_mode=pl.Buffered(1))

    splits = (0, None, 0, 0, 0, 1, 0, 2, 2, 0, 0)
    tap_rows = tap_rows[part * heads : (part + 1) * heads]
    arrays = (proj, tap_rows, grad) + saved
    out, joined = pl.pallas_call(
        attention_backward_body,
        grid=(1,),
        in_specs=[pl.BlockSpec(memory_space=pltpu.SMEM)]
        + [block(array.shape, split) for array, split in zip(arrays, splits)],
        out_specs=[
            pl.BlockSpec((3 * width, row_count), lambda step: (0, 0)),
            pl.BlockSpec((heads, 2 * BLOCK), lambda step: (0, 0)),
        ],
        out_shape=[
            jax.ShapeDtypeStruct((3 * width, row_count), jnp.bfloat16),
            jax.ShapeDtypeStruct((heads, 2 * BLOCK), jnp.float32),
        ],
        scratch_shapes=[
            pltpu.VMEM((marks, row_count), jnp.bfloat16),
            pltpu.VMEM((heads, marks, row_count), jnp.bfloat16),
            pltpu.VMEM((marks, row_count), jnp.bfloat16),
            pltpu.VMEM((2, width, marks), jnp.float32),
            pltpu.VMEM(thin, jnp.float32),
            pltpu.VMEM(thin, jnp.float32),
            pltpu.VMEM(square, jnp.float32),
            pltpu.VMEM(square, jnp.float32),
            pltpu.VMEM((stacked, 2 * BLOCK), jnp.bfloat16),
            pltpu.VMEM((stacked, 2 * BLOCK), jnp.bfloat16),
            pltpu.VMEM((stacked, BLOCK), jnp.float32),
        ],
        compiler_params=pltpu.CompilerParams(vmem_limit_bytes=48 * 1024 * 1024),
        cost_estimate=pl.CostEstimate(
            flops=30_000_000_000 // parts, bytes_accessed=20_000_000 // parts, transcendentals=0
        ),
    )(item_units, *arrays)
    half = TAPS // 2
    return out, jnp.concatenate([joined[:, 2 * BLOCK - half :], joined[:, : TAPS - half]], axis=1)


ROWS = 256
LONG_ROWS = 512
OUTER = 384
PIECE = 512
GELU_SCALE = 0.7978845608
GELU_CUBE = 0.044715


def row_block(width, rows=ROWS):
    return pl.BlockSpec((rows, width), lambda step: (step, 0))


def fixed_block(shape, column=0):
    return pl.BlockSpec(shape, lambda step: (0, column))


def row_lanes(rows=ROWS):
    return pl.BlockSpec((1, rows), lambda step: (0, step))


def as_column(row):
    return jnp.broadcast_to(row, (128, row.shape[1])).T[:, 0:1]


def as_row(column):
    return jnp.broadcast_to(column, (column.shape[0], 128)).T[0:1]


def dense_params():
    return pltpu.CompilerParams(vmem_limit_bytes=56 * 1024 * 1024)


def cost(flops, size):
    return pl.CostEstimate(flops=flops, bytes_accessed=size, transcendentals=0)


def normalized(rows):
    center = rows - jnp.mean(rows, axis=-1, keepdims=True)
    spread = jnp.mean(center * center, axis=-1, keepdims=True)
    scale = lax.rsqrt(spread + NORM_EPS)
    return center * scale, scale


def norm_backward(grad, gain, unit, scale):
    scaled = grad * gain
    lean = jnp.mean(scaled * unit, axis=-1, keepdims=True)
    return scale * (scaled - jnp.mean(scaled, axis=-1, keepdims=True) - unit * lean)


def column_sum(rows):
    return jnp.sum(rows, axis=0, keepdims=True)


def both(own_ref, other_ref):
    return own_ref[...].astype(jnp.float32) + other_ref[...].astype(jnp.float32)


def weight_blocks(expand, reduce):
    return [fixed_block(reduce.shape), fixed_block(reduce.shape)]


def hidden_forward_body(
    own_ref,
    other_ref,
    tokens_ref,
    weight_ref,
    shared_ref,
    bias_ref,
    expand_ref,
    reduce_ref,
    part_ref,
    hidden_ref,
    low_ref,
    unit_ref,
    scale_ref,
    active_ref,
    slope_ref,
    stat_ref,
):
    branch = both(own_ref, other_ref) + shared_ref[0:1]
    squares = column_sum(as_column(weight_ref[...]) * branch * branch)

    @pl.when(pl.program_id(0) == 0)
    def _():
        stat_ref[...] = jnp.zeros_like(stat_ref)

    stat_ref[...] += squares
    unit, scale = normalized(tokens_ref[...].astype(jnp.float32) + branch)
    hidden = unit * shared_ref[2:3] + shared_ref[3:4]
    hidden_ref[...] = hidden
    unit_ref[...] = unit.astype(jnp.bfloat16)
    scale_ref[...] = as_row(scale)
    hidden_low = hidden.astype(jnp.bfloat16)
    low_ref[...] = hidden_low
    total = jnp.zeros(part_ref.shape, jnp.float32)
    for at in range(0, reduce_ref.shape[1], PIECE):
        lanes = slice(at, at + PIECE)
        expanded = dot_with(hidden_low, expand_ref[:, lanes], 1, 0) + bias_ref[:, lanes]
        square = expanded * expanded
        bend = jnp.tanh(expanded * (GELU_SCALE + (GELU_SCALE * GELU_CUBE) * square))
        half = 0.5 + 0.5 * bend
        active = (expanded * half).astype(jnp.bfloat16)
        active_ref[:, lanes] = active
        slope = half + (0.5 * expanded) * (1.0 - bend * bend) * (
            GELU_SCALE + (3.0 * GELU_SCALE * GELU_CUBE) * square
        )
        slope_ref[:, lanes] = slope.astype(jnp.bfloat16)
        total += dot_with(active, reduce_ref[:, lanes], 1, 1)
    part_ref[...] = total.astype(jnp.bfloat16)


def hidden_forward(own, other, tokens, weight_row, shared_rows, expand_bias, *weights):
    row_count, width = tokens.shape
    units = expand_bias.shape[1]
    return pl.pallas_call(
        hidden_forward_body,
        grid=(row_count // ROWS,),
        in_specs=[
            row_block(width),
            row_block(width),
            row_block(width),
            row_lanes(),
            fixed_block((6, width)),
            fixed_block((1, units)),
        ]
        + weight_blocks(*weights),
        out_specs=[
            row_block(width),
            row_block(width),
            row_block(width),
            row_block(width),
            row_lanes(),
            row_block(units),
            row_block(units),
            fixed_block((1, width)),
        ],
        out_shape=[
            jax.ShapeDtypeStruct((row_count, width), jnp.bfloat16),
            jax.ShapeDtypeStruct((row_count, width), jnp.float32),
            jax.ShapeDtypeStruct((row_count, width), jnp.bfloat16),
            jax.ShapeDtypeStruct((row_count, width), jnp.bfloat16),
            jax.ShapeDtypeStruct((1, row_count), jnp.float32),
            jax.ShapeDtypeStruct((row_count, units), jnp.bfloat16),
            jax.ShapeDtypeStruct((row_count, units), jnp.bfloat16),
            jax.ShapeDtypeStruct((1, width), jnp.float32),
        ],
        compiler_params=dense_params(),
        cost_estimate=cost(4 * row_count * width * units, 30_000_000),
    )(own, other, tokens, weight_row, shared_rows, expand_bias, *weights)


def hidden_backward_body(
    own_ref,
    other_ref,
    hidden_ref,
    cotangent_ref,
    weight_ref,
    shared_ref,
    slope_ref,
    expand_ref,
    reduce_ref,
    output_ref,
    d_two_ref,
    d_expanded_ref,
    part_ref,
    sums_ref,
    bias_ref,
):
    branch = both(own_ref, other_ref) + shared_ref[1:2]
    weight = as_column(weight_ref[...])
    unit, scale = normalized(hidden_ref[...] + branch)
    output_ref[...] = unit * shared_ref[4:5] + shared_ref[5:6]
    grad = cotangent_ref[...].astype(jnp.float32) * weight
    d_res = norm_backward(grad, shared_ref[4:5], unit, scale)
    d_two = d_res.astype(jnp.bfloat16)
    d_two_ref[...] = d_two

    @pl.when(pl.program_id(0) == 0)
    def _():
        sums_ref[...] = jnp.zeros_like(sums_ref)
        bias_ref[...] = jnp.zeros_like(bias_ref)

    sums_ref[...] += jnp.concatenate(
        [
            column_sum(weight * branch * branch),
            column_sum(d_res),
            column_sum(grad * unit),
            column_sum(grad),
            jnp.broadcast_to(column_sum(weight), (1, grad.shape[1])),
            jnp.zeros((3, grad.shape[1]), jnp.float32),
        ],
        axis=0,
    )
    total = jnp.zeros(part_ref.shape, jnp.float32)
    for at in range(0, reduce_ref.shape[1], PIECE):
        lanes = slice(at, at + PIECE)
        d_active = dot_with(d_two, reduce_ref[:, lanes], 1, 0)
        d_expanded = (slope_ref[:, lanes].astype(jnp.float32) * d_active).astype(jnp.bfloat16)
        d_expanded_ref[:, lanes] = d_expanded
        bias_ref[:, lanes] += column_sum(d_expanded.astype(jnp.float32))
        total += dot_with(d_expanded, expand_ref[:, lanes], 1, 1)
    part_ref[...] = total.astype(jnp.bfloat16)


def hidden_backward(own, other, hidden, cotangent, weight_row, shared_rows, slope, *weights):
    row_count, width = cotangent.shape
    units = slope.shape[1]
    return pl.pallas_call(
        hidden_backward_body,
        grid=(row_count // ROWS,),
        in_specs=[
            row_block(width),
            row_block(width),
            row_block(width),
            row_block(width),
            row_lanes(),
            fixed_block((6, width)),
            row_block(units),
        ]
        + weight_blocks(*weights),
        out_specs=[
            row_block(width),
            row_block(width),
            row_block(units),
            row_block(width),
            fixed_block((8, width)),
            fixed_block((1, units)),
        ],
        out_shape=[
            jax.ShapeDtypeStruct((row_count, width), jnp.float32),
            jax.ShapeDtypeStruct((row_count, width), jnp.bfloat16),
            jax.ShapeDtypeStruct((row_count, units), jnp.bfloat16),
            jax.ShapeDtypeStruct((row_count, width), jnp.bfloat16),
            jax.ShapeDtypeStruct((8, width), jnp.float32),
            jax.ShapeDtypeStruct((1, units), jnp.float32),
        ],
        compiler_params=dense_params(),
        cost_estimate=cost(4 * row_count * width * units, 30_000_000),
    )(own, other, hidden, cotangent, weight_row, shared_rows, slope, *weights)


def norm_one_body(
    own_ref,
    other_ref,
    d_two_ref,
    unit_ref,
    scale_ref,
    inside_ref,
    shared_ref,
    mixing_ref,
    d_one_ref,
    d_mixed_ref,
    sums_ref,
    turned_ref,
):
    @pl.when(pl.program_id(0) == 0)
    def _():
        sums_ref[...] = jnp.zeros_like(sums_ref)
        turned_ref[...] = mixing_ref[...].astype(jnp.float32).T.astype(jnp.bfloat16)

    grad = both(own_ref, other_ref) + d_two_ref[...].astype(jnp.float32)
    unit = unit_ref[...].astype(jnp.float32)
    d_res = norm_backward(grad, shared_ref[2:3], unit, as_column(scale_ref[...]))
    d_one = d_res.astype(jnp.bfloat16)
    d_one_ref[...] = d_one
    sums_ref[...] += jnp.concatenate(
        [
            column_sum(d_res),
            column_sum(grad * unit),
            column_sum(grad),
            jnp.zeros((5, grad.shape[1]), jnp.float32),
        ],
        axis=0,
    )
    d_mixed = dot_with(turned_ref[...], d_one, 1, 1) * inside_ref[...]
    d_mixed_ref[...] = d_mixed.astype(jnp.bfloat16)


def norm_one_backward(own, other, d_two, unit, scale, inside_row, shared_rows, late_full, local_width):
    row_count, width = d_two.shape
    return pl.pallas_call(
        norm_one_body,
        grid=(row_count // LONG_ROWS,),
        in_specs=[
            row_block(width, LONG_ROWS),
            row_block(width, LONG_ROWS),
            row_block(width, LONG_ROWS),
            row_block(width, LONG_ROWS),
            row_lanes(LONG_ROWS),
            pl.BlockSpec((1, LONG_ROWS), lambda step: (0, step)),
            fixed_block((6, width)),
            fixed_block((width, local_width), late_full.shape[1] // local_width - 1),
        ],
        out_specs=[
            row_block(width, LONG_ROWS),
            pl.BlockSpec((local_width, LONG_ROWS), lambda step: (0, step)),
            fixed_block((8, width)),
        ],
        out_shape=[
            jax.ShapeDtypeStruct((row_count, width), jnp.bfloat16),
            jax.ShapeDtypeStruct((local_width, row_count), jnp.bfloat16),
            jax.ShapeDtypeStruct((8, width), jnp.float32),
        ],
        scratch_shapes=[pltpu.VMEM((local_width, width), jnp.bfloat16)],
        compiler_params=dense_params(),
        cost_estimate=cost(2 * row_count * width * local_width, 14_000_000),
    )(own, other, d_two, unit, scale, inside_row, shared_rows, late_full)


def turned_dot_body(*refs):
    *pairs, out_ref = refs
    total = jnp.zeros(out_ref.shape, jnp.float32)
    for at in range(0, len(pairs), 2):
        left = pairs[at][...]
        left = left.reshape(-1, left.shape[-1])
        total += dot_with(left, pairs[at + 1][...], 0, 1)
    out_ref[...] = total.astype(jnp.bfloat16)


def turned_dot(lefts, rights, columns, width):
    row_count = lefts[0].shape[-1]
    specs, arrays, terms = [], [], 0
    for left, right, column in zip(lefts, rights, columns):
        shape = left.shape[:-1] + (LONG_ROWS,)
        place = (0,) * (left.ndim - 1)
        specs.append(pl.BlockSpec(shape, lambda step, place=place: place + (step,)))
        depth = left.size // row_count
        specs.append(fixed_block((width, depth), column))
        arrays += [left, right]
        terms += depth
    return pl.pallas_call(
        turned_dot_body,
        grid=(row_count // LONG_ROWS,),
        in_specs=specs,
        out_specs=row_block(width, LONG_ROWS),
        out_shape=jax.ShapeDtypeStruct((row_count, width), jnp.bfloat16),
        compiler_params=dense_params(),
        cost_estimate=cost(2 * row_count * width * terms, 8_000_000),
    )(*arrays)

def turned_outer_body(left_ref, right_ref, out_ref):
    product = dot_with(left_ref[...], right_ref[...], 1, 0)
    out_ref[...] = product.T.astype(jnp.bfloat16)


def turned_outer(left, right):
    depth, width = right.shape
    return pl.pallas_call(
        turned_outer_body,
        grid=(width // OUTER,),
        in_specs=[
            fixed_block(left.shape),
            pl.BlockSpec((depth, OUTER), lambda step: (0, step)),
        ],
        out_specs=pl.BlockSpec((OUTER, left.shape[0]), lambda step: (step, 0)),
        out_shape=jax.ShapeDtypeStruct((width, left.shape[0]), jnp.bfloat16),
        compiler_params=dense_params(),
        cost_estimate=cost(2 * depth * width * left.shape[0], 6_000_000),
    )(left, right)


def project_body(first_ref, second_ref, tokens_ref, bias_ref, out_ref, turned_ref):
    part_width = first_ref.shape[1]

    @pl.when(pl.program_id(0) == 0)
    def _():
        for part, weight_ref in enumerate((first_ref, second_ref)):
            turned = weight_ref[...].astype(jnp.float32).T
            turned_ref[part * part_width : (part + 1) * part_width] = turned.astype(jnp.bfloat16)

    rows = dot_with(turned_ref[...], tokens_ref[...], 1, 1) + bias_ref[...]
    out_ref[...] = rows.astype(jnp.bfloat16).reshape(out_ref.shape)


def project(first, second, tokens, bias_column):
    row_count, width = tokens.shape
    part_width = first.shape[1]
    shape = (2, 3, part_width // 3, row_count)
    return pl.pallas_call(
        project_body,
        grid=(row_count // LONG_ROWS,),
        in_specs=[
            fixed_block((width, part_width)),
            fixed_block((width, part_width)),
            row_block(width, LONG_ROWS),
            fixed_block((2 * part_width, 1)),
        ],
        out_specs=pl.BlockSpec(shape[:3] + (LONG_ROWS,), lambda step: (0, 0, 0, step)),
        out_shape=jax.ShapeDtypeStruct(shape, jnp.bfloat16),
        scratch_shapes=[pltpu.VMEM((2 * part_width, width), jnp.bfloat16)],
        compiler_params=dense_params(),
        cost_estimate=cost(4 * row_count * width * part_width, 8_000_000),
    )(first, second, tokens, bias_column)


def adamw(master, moment, square, gradient, factor, learn_rate, decay_rate):
    clipped = gradient * factor
    moment_new = BETA_ONE * moment + (1.0 - BETA_ONE) * clipped
    square_new = BETA_TWO * square + (1.0 - BETA_TWO) * clipped * clipped
    step_size = moment_new / CORRECT_ONE / (jnp.sqrt(square_new / CORRECT_TWO) + ADAM_EPS)
    return (master - learn_rate * (step_size + decay_rate * master), moment_new, square_new)

def finish_body(
    places_ref,
    expand_ref,
    reduce_ref,
    mixing_ref,
    hidden_ref,
    left_ref,
    right_ref,
    inputs_ref,
    stat_ref,
    sums_ref,
    expand_out,
    reduce_out,
    mixing_out,
    left_out,
    right_out,
    row_ref,
    *,
    bias_share,
    shared_share,
):
    mine = places_ref[0]
    squares = jnp.zeros((1, 1), jnp.float32)

    def total(values):
        return jnp.sum(jnp.sum(values, axis=0, keepdims=True), axis=1, keepdims=True)

    at = 0
    for current_ref, out_ref in (
        (expand_ref, expand_out),
        (reduce_ref, reduce_out),
        (mixing_ref, mixing_out),
    ):
        width = out_ref.shape[1]
        share = current_ref[mine] + hidden_ref[:, at : at + width].astype(jnp.float32)
        out_ref[...] = share
        squares += total(share * share)
        at += width
    rows = left_ref.shape[1]
    received = inputs_ref[...].astype(jnp.float32)
    left = left_ref[mine] + received[:rows]
    right = right_ref[mine] + received[rows:]
    left_out[...] = left
    right_out[...] = right
    squares += total(left * left) + total(right[:rows] * right[:rows])
    small = right[rows : rows + 1]
    kernel = right[rows + 1 :]
    lane = lax.broadcasted_iota(jnp.int32, small.shape, 1)
    shared_counts = places_ref[1].astype(jnp.float32)
    factor = jnp.where(
        lane < bias_share, 1.0, jnp.where(lane < bias_share + shared_share, shared_counts, 0.0)
    )
    squares += total(small * small * factor) + total(kernel * kernel)
    lane = lax.broadcasted_iota(jnp.int32, (1, 128), 1)
    row = jnp.where(lane == 0, squares, 0.0)
    row += jnp.where(lane == 1, total(stat_ref[...]), 0.0)
    row += jnp.where(lane == 2, total(sums_ref[0:1]), 0.0)
    row_ref[:, :128] = row + jnp.where(lane == 3, sums_ref[4:5, 0:1], 0.0)
    row_ref[:, 128:] = kernel[:, : row_ref.shape[1] - 128]


def finish(places, hidden, inputs, stat_one, sums_two, bias_share, shared_share):
    def flat(array):
        return array.reshape(array.shape[-2:])

    def pair(array):
        return array.reshape((2,) + array.shape[-2:])

    arrays = [pair(array) for array in hidden.currents] + [flat(hidden.received)]
    arrays += [pair(array) for array in inputs.currents] + [flat(inputs.received)]
    arrays += [stat_one, sums_two]
    shapes = [array.shape[-2:] for array in hidden.currents + inputs.currents] + [(1, 384)]
    return pl.pallas_call(
        functools.partial(finish_body, bias_share=bias_share, shared_share=shared_share),
        in_specs=[pl.BlockSpec(memory_space=pltpu.SMEM)] + whole(len(arrays)),
        out_specs=whole(len(shapes)),
        out_shape=[jax.ShapeDtypeStruct(shape, jnp.float32) for shape in shapes],
        compiler_params=dense_params(),
        cost_estimate=cost(1_000_000, 3_000_000),
    )(places, *arrays)


def update_body(*refs, width, bias_share, shard_rows):
    totals_ref, kernel_ref, expand_ref, reduce_ref, mixing_ref, left_ref, right_ref = refs[:7]
    old_refs, new_refs, row_ref = refs[7:28], refs[28:49], refs[49]
    rows = left_ref.shape[0]
    totals = totals_ref[...]
    lane = lax.broadcasted_iota(jnp.int32, totals.shape, 1)
    means = jnp.sqrt(totals / jnp.where(lane == 0, 1.0, totals[:, 3:4] * width))
    row_ref[...] = means
    factor = CLIP_NORM / (means[:, 0:1] + CLIP_EPS)

    def put(index, place, gradient, rate, decay):
        old = [old_refs[3 * index + kind][place] for kind in range(3)]
        for kind, value in enumerate(adamw(*old, gradient, factor, rate, decay)):
            new_refs[3 * index + kind][place] = value

    part_width = right_ref.shape[1] // 3
    for part, share_ref in enumerate((left_ref, right_ref)):
        for kind in range(3):
            gradient = share_ref[:rows, kind * part_width : (kind + 1) * part_width]
            lanes = slice(part * part_width, (part + 1) * part_width)
            put(0, (kind, slice(None), lanes), gradient, RATE_MATRIX, WEIGHT_DECAY)
    put(1, ..., mixing_ref[...], RATE_MATRIX, WEIGHT_DECAY)
    put(2, ..., expand_ref[...], RATE_MATRIX, WEIGHT_DECAY)
    put(3, ..., reduce_ref[...], RATE_MATRIX, WEIGHT_DECAY)
    small = slice(rows, rows + 1)
    put(4, ..., right_ref[small, :bias_share], RATE_VECTOR, 0.0)
    for row in range(6):
        start = bias_share + row * shard_rows
        place = (slice(row, row + 1), slice(None))
        put(5, place, right_ref[small, start : start + shard_rows], RATE_VECTOR, 0.0)
    heads, taps = old_refs[18].shape
    for row in range(heads):
        start = 128 + row * taps
        place = (slice(row, row + 1), slice(None))
        put(6, place, kernel_ref[:, start : start + taps], RATE_VECTOR, 0.0)


def update(totals, kernel_row, shares, olds, width, bias_share, shard_rows):
    arrays = [totals, kernel_row] + shares + olds
    shapes = [old.shape for old in olds] + [(1, 128)]
    return pl.pallas_call(
        functools.partial(update_body, width=width, bias_share=bias_share, shard_rows=shard_rows),
        in_specs=whole(len(arrays)),
        out_specs=whole(len(shapes)),
        out_shape=[jax.ShapeDtypeStruct(shape, jnp.float32) for shape in shapes],
        compiler_params=dense_params(),
        cost_estimate=cost(5_000_000, 6_000_000),
    )(*arrays)


def body(
    tokens,
    cotangent,
    item_units,
    counted,
    inputs_weight,
    inputs_moment,
    inputs_square,
    mixing_weight,
    mixing_moment,
    mixing_square,
    expand_weight,
    expand_moment,
    expand_square,
    reduce_weight,
    reduce_moment,
    reduce_square,
    biases_weight,
    biases_moment,
    biases_square,
    shared_weight,
    shared_moment,
    shared_square,
    kernel_weight,
    kernel_moment,
    kernel_square,
):
    dp_count = lax.axis_size("dp")
    bits = list(range(bits_of(dp_count)))
    first_order, second_order = bits, bits[:2][::-1] + bits[2:]
    row_count, width_full = tokens.shape
    local_width = inputs_weight.shape[2]
    shard_rows = inputs_weight.shape[1]
    bias_share = biases_weight.shape[1]
    hidden_units = expand_weight.shape[1]
    part_width = local_width // 2
    part_lanes = [slice(0, part_width), slice(part_width, local_width)]

    high_bits = bits[2:][::-1]
    low_orders = (bits[:2][::-1], bits[:2])
    small_low = jnp.concatenate([biases_weight.reshape(-1), shared_weight.reshape(-1)])
    small_low = jnp.pad(small_low, (0, (-small_low.shape[0]) % (3 * part_width)))
    small_low = small_low.astype(jnp.bfloat16).reshape(-1, 3 * part_width)
    inputs_low = [
        jnp.concatenate([inputs_weight[c][:, lanes] for c in range(3)], axis=1).astype(jnp.bfloat16)
        for lanes in part_lanes
    ]
    inputs_low = jnp.concatenate([inputs_low[1], inputs_low[0], small_low], axis=0)
    sizes = (shard_rows, inputs_low.shape[0] - shard_rows)
    inputs_gather = Gather(inputs_low, dp_count, high_bits)
    late_low = jnp.concatenate(
        [expand_weight.astype(jnp.bfloat16)]
        + [weight.astype(jnp.bfloat16).T for weight in (mixing_weight, reduce_weight)],
        axis=1,
    )
    inputs_gather.step()
    late_low = after(late_low, inputs_gather.current)
    for _ in high_bits[1:]:
        inputs_gather.step()
    right_gather, left_gather = inputs_gather.split(sizes, -2, low_orders)
    inputs_right = right_gather.finish()
    left_full = left_gather.finish().reshape(dp_count, sizes[1], 3 * part_width)
    inputs_left = left_full[:, :shard_rows].reshape(-1, 3 * part_width)
    small_full = left_full[:, shard_rows:].reshape(dp_count, -1)
    late_gather = Gather(late_low, dp_count, high_bits)
    for _ in high_bits:
        late_gather.step()
    sizes = (hidden_units + local_width, hidden_units)
    expand_gather, reduce_gather = late_gather.split(sizes, -1, low_orders)
    biases_row = small_full[:, :bias_share].reshape(-1).astype(jnp.float32)
    shared_rows = small_full[:, bias_share : bias_share + 6 * shard_rows]
    shared_rows = shared_rows.reshape(dp_count, 6, shard_rows).transpose(1, 0, 2)
    shared_rows = shared_rows.reshape(6, -1).astype(jnp.float32)
    query_bias = biases_row[:local_width]
    value_bias = biases_row[local_width : 2 * local_width]
    expand_bias = biases_row[2 * local_width :][None, :]
    zero_bias = jnp.zeros((part_width,), jnp.float32)
    bias_column = jnp.concatenate(
        [
            piece
            for lanes in part_lanes
            for piece in (query_bias[lanes], zero_bias, value_bias[lanes])
        ]
    )[:, None]

    row_item = row_items(item_units[0], row_count, LANDMARKS)
    inside = (row_item < 2).astype(jnp.float32)
    weight_rows = counted.astype(jnp.float32) * inside
    weight_row = weight_rows[None, :]

    tied_tokens = after(tokens, expand_gather.current, reduce_gather.current)
    proj = project(inputs_left, inputs_right, tied_tokens, bias_column)
    marks, middle, last, values, approx = attention_start(item_units, proj)
    expand_gather.step(marks)
    reduce_gather.step(marks)
    tied_marks = after(marks, expand_gather.current, reduce_gather.current)
    attended, kept, rough, fine, weighted = attention_finish(
        item_units, proj, tap_rows_of(kernel_weight), tied_marks, middle, last, values, approx
    )
    saved = (kept, last, marks, middle, rough, fine, values, weighted)
    expand_full = expand_gather.finish()
    reduce_full = reduce_gather.finish()
    hidden_weights = (expand_full, reduce_full)
    mixing_column = expand_full.shape[1] // local_width - 1
    tied_attended = after(attended, reduce_full)
    own_one = turned_dot([tied_attended], [expand_full], [mixing_column], width_full)
    other_one = swap(own_one, "head", 2, 0)
    own_two, hidden_one, hidden_low, unit_one, scale_one, active, slope, stat_one = hidden_forward(
        own_one, other_one, tokens, weight_row, shared_rows, expand_bias, *hidden_weights
    )
    other_two = swap(own_two, "head", 2, 0)
    output_rows, d_two, d_expanded, own_three, sums_two, expand_sums = hidden_backward(
        own_two, other_two, hidden_one, cotangent, weight_row, shared_rows, slope, *hidden_weights
    )
    other_three = swap(own_three, "head", 2, 0)
    reduce_grad = jnp.einsum("rd,rf->df", d_two, active, preferred_element_type=jnp.float32)
    expand_grad = jnp.einsum("rd,rf->df", hidden_low, d_expanded, preferred_element_type=jnp.float32)
    reduce_scatter = Scatter([reduce_grad.astype(jnp.bfloat16)], dp_count, second_order).send()
    expand_scatter = Scatter([expand_grad.astype(jnp.bfloat16)], dp_count, first_order).send()
    d_one, d_mixed, sums_one = norm_one_backward(
        own_three,
        other_three,
        d_two,
        unit_one,
        scale_one,
        inside[None, :],
        shared_rows,
        expand_full,
        local_width,
    )
    mixing_grad = jnp.einsum("rd,kr->dk", d_one, attended, preferred_element_type=jnp.float32)
    mixing_scatter = Scatter([mixing_grad.astype(jnp.bfloat16)], dp_count, first_order).send()
    first_scatters = (reduce_scatter, expand_scatter, mixing_scatter)
    d_mixed = after(d_mixed, *[scatter.sent for scatter in first_scatters])
    back_taps = tap_rows_of(kernel_weight[:, ::-1])
    d_left, kernel_left = attention_backward(item_units, proj, back_taps, d_mixed, *saved, part=0)

    for scatter in first_scatters:
        scatter.take(d_left).send()
    left_grad = turned_outer(d_left, tokens)
    left_scatter = Scatter([left_grad], dp_count, second_order).send()
    d_mixed = after(d_mixed, left_scatter.sent, *[scatter.sent for scatter in first_scatters])
    d_right, kernel_right = attention_backward(item_units, proj, back_taps, d_mixed, *saved, part=1)
    right_grad = turned_outer(d_right, tokens)
    left_sums, right_sums = [
        jnp.sum(gradient.astype(jnp.float32), axis=1).reshape(3, part_width)
        for gradient in (d_left, d_right)
    ]
    biases_grad = jnp.concatenate(
        [left_sums[0], right_sums[0], left_sums[2], right_sums[2], expand_sums.reshape(-1)]
    )
    shared_grad = jnp.concatenate(
        [sums_one[0:1], sums_two[1:2], sums_one[1:3], sums_two[2:4]], axis=0
    )
    shared_grad = shared_grad.reshape(6, dp_count, shard_rows).transpose(1, 0, 2)
    kernel_grad = jnp.concatenate([kernel_left, kernel_right], axis=0)
    columns = 3 * part_width

    def widened(array):
        return jnp.pad(array, ((0, 0), (0, columns - array.shape[1])))[:, None]

    tap_count = kernel_grad.shape[1]
    tap_share = -(-tap_count // dp_count)
    tap_owner = jnp.arange(tap_count) // tap_share
    kernel_rows = jnp.where(
        tap_owner[None, None, :] == jnp.arange(dp_count)[:, None, None], kernel_grad[None], 0.0
    )
    small_rows = jnp.concatenate(
        [biases_grad.reshape(dp_count, bias_share), shared_grad.reshape(dp_count, -1)], axis=1
    )
    right_rows = jnp.concatenate(
        [
            right_grad.reshape(dp_count, shard_rows, columns),
            widened(small_rows).astype(jnp.bfloat16),
            widened(kernel_rows.reshape(dp_count, -1)).astype(jnp.bfloat16),
        ],
        axis=1,
    )
    right_rows = right_rows.reshape(-1, columns)
    right_scatter = Scatter([right_rows], dp_count, first_order).send()
    for scatter in first_scatters:
        scatter.take(right_scatter.sent)
    hidden_scatter = expand_scatter.merge(reduce_scatter, mixing_scatter).send()
    left_scatter.take(right_scatter.sent).send()
    d_both = after(d_right, right_scatter.sent, hidden_scatter.sent, left_scatter.sent)
    own_four = turned_dot([d_left, d_both], [inputs_left, inputs_right], [0, 0], width_full)
    other_four = swap(own_four, "head", 2, 0)
    hidden_scatter.take(own_four).send()
    right_scatter.take(own_four).send()
    input_grad = (
        own_four.astype(jnp.float32) + other_four.astype(jnp.float32) + d_one.astype(jnp.float32)
    )
    inputs_scatter = left_scatter.merge(right_scatter, join=-2).send()
    dp_index, head_index = lax.axis_index("dp"), lax.axis_index("head")
    places = jnp.stack([(dp_index >> bits[-1]) & 1, head_index == 0]).astype(jnp.int32)
    inputs_scatter.take(input_grad)
    while hidden_scatter.order:
        hidden_scatter.take().send()
    while inputs_scatter.order:
        inputs_scatter.take().send()
    *shares, final_row = finish(
        places, hidden_scatter, inputs_scatter, stat_one, sums_two, bias_share, 6 * shard_rows
    )
    final_row = sum_all(final_row, "dp", dp_count)
    totals = sum_all(final_row[:, :128], "head", 2)
    olds = [
        inputs_weight,
        inputs_moment,
        inputs_square,
        mixing_weight.T,
        mixing_moment.T,
        mixing_square.T,
        expand_weight,
        expand_moment,
        expand_square,
        reduce_weight.T,
        reduce_moment.T,
        reduce_square.T,
        biases_weight,
        biases_moment,
        biases_square,
        shared_weight,
        shared_moment,
        shared_square,
        kernel_weight,
        kernel_moment,
        kernel_square,
    ]
    *news, row = update(totals, final_row, shares, olds, width_full, bias_share, shard_rows)
    for index in (3, 4, 5, 9, 10, 11):
        news[index] = news[index].T
    return (output_rows, input_grad, *news, row[0, 0], row[0, 1:3])


def solution(mesh):
    placed = (
        P("dp", None),
        P("dp", None),
        P("dp", None),
        P("dp"),
        P(None, "dp", "head"),
        P(None, "dp", "head"),
        P(None, "dp", "head"),
        P("head", "dp"),
        P("head", "dp"),
        P("head", "dp"),
        P("dp", "head"),
        P("dp", "head"),
        P("dp", "head"),
        P("head", "dp"),
        P("head", "dp"),
        P("head", "dp"),
        P("head", "dp"),
        P("head", "dp"),
        P("head", "dp"),
        P(None, "dp"),
        P(None, "dp"),
        P(None, "dp"),
        P("head", None),
        P("head", None),
        P("head", None),
    )
    return jax.shard_map(
        body,
        mesh=mesh,
        in_specs=placed,
        out_specs=(
            P("dp", None),
            P("dp", None),
            P(None, "dp", "head"),
            P(None, "dp", "head"),
            P(None, "dp", "head"),
            P("head", "dp"),
            P("head", "dp"),
            P("head", "dp"),
            P("dp", "head"),
            P("dp", "head"),
            P("dp", "head"),
            P("head", "dp"),
            P("head", "dp"),
            P("head", "dp"),
            P("head", "dp"),
            P("head", "dp"),
            P("head", "dp"),
            P(None, "dp"),
            P(None, "dp"),
            P(None, "dp"),
            P("head", None),
            P("head", None),
            P("head", None),
            P(),
            P(),
        ),
        check_vma=False,
    )
```

```python
import functools

import jax
import jax.numpy as jnp
from jax import lax
from jax.experimental import pallas as pl
from jax.experimental.pallas import tpu as pltpu
from jax.sharding import PartitionSpec as P

HEAD_DIM = 64
LANDMARKS = 64
PINV_STEPS = 6
ROUGH_STEPS = 4
TAPS = 33
NORM_EPS = 1e-05
CLIP_NORM = 1.0
CLIP_EPS = 1e-06
BETA_ONE = 0.9
BETA_TWO = 0.98
ADAM_EPS = 1e-08
RATE_MATRIX = 0.04
RATE_VECTOR = 0.5
WEIGHT_DECAY = 0.01
CORRECT_ONE = 1.0 - BETA_ONE**5
CORRECT_TWO = 1.0 - BETA_TWO**5

def bits_of(count):
    bit_count = 0
    while (1 << bit_count) < count:
        bit_count += 1
    return bit_count


def swap(array, axis, count, bit):
    return lax.ppermute(array, axis, [(i, i ^ (1 << bit)) for i in range(count)])


class Gather:
    def __init__(self, array, count, order):
        self.count, self.order = count, list(order)
        self.shape = (count * array.shape[0],) + array.shape[1:]
        self.current = array.reshape((1,) * bits_of(count) + array.shape)

    def step(self, *others):
        bit = self.order.pop(0)
        dim = bits_of(self.count) - 1 - bit
        other = swap(self.current, "dp", self.count, bit)
        other = after(other, *others) if others else other
        self.current = jnp.where(
            (lax.axis_index("dp") >> bit) & 1 == 0,
            jnp.concatenate([self.current, other], dim),
            jnp.concatenate([other, self.current], dim),
        )
        return self

    def split(self, sizes, dim, orders):
        pieces, at = [], 0
        for size, order in zip(sizes, orders):
            piece = Gather.__new__(Gather)
            piece.count, piece.order = self.count, list(order)
            axis = self.current.ndim + dim
            piece.current = lax.slice_in_dim(self.current, at, at + size, axis=axis)
            rows = self.count * piece.current.shape[-2]
            piece.shape = (rows, piece.current.shape[-1])
            pieces.append(piece)
            at += size
        return pieces

    def finish(self):
        while self.order:
            self.step()
        return self.current.reshape(self.shape)


def after(array, *others):
    return lax.optimization_barrier((array,) + others)[0]


class Scatter:
    def __init__(self, arrays, count, order, join=-1):
        self.count = count
        self.join = join
        self.order = list(order)
        self.shapes = [(array.shape[0] // count,) + array.shape[1:] for array in arrays]
        lead = (2,) * bits_of(count)
        self.currents = [array.reshape(lead + shape) for array, shape in zip(arrays, self.shapes)]
        self.sent = self.kept = self.received = None

    def send(self):
        if self.order:
            bit = self.order.pop(0)
            dim = bits_of(self.count) - 1 - bit
            mine = (lax.axis_index("dp") >> bit) & 1
            sent = [
                lax.dynamic_slice_in_dim(current, 1 - mine, 1, dim).astype(jnp.bfloat16)
                for current in self.currents
            ]
            self.sent = sent[0] if len(sent) == 1 else jnp.concatenate(sent, axis=self.join)
            self.kept = [
                lax.dynamic_slice_in_dim(current, mine, 1, dim) for current in self.currents
            ]
            self.received = swap(self.sent, "dp", self.count, bit)
        return self

    def take(self, *others):
        if self.received is not None:
            received = after(self.received, *others) if others else self.received
            currents, at = [], 0
            for kept in self.kept:
                size = kept.shape[self.join]
                piece = lax.slice_in_dim(received, at, at + size, axis=self.join % kept.ndim)
                currents.append(kept.astype(jnp.float32) + piece.astype(jnp.float32))
                at += size
            self.currents, self.received = currents, None
        return self

    def merge(self, *others, join=-1):
        every = (self,) + others
        merged = Scatter([], self.count, self.order, join)
        merged.shapes = [shape for one in every for shape in one.shapes]
        merged.currents = [current for one in every for current in one.take().currents]
        return merged

    def finish(self):
        self.take()
        while self.order:
            self.send().take()
        pairs = zip(self.currents, self.shapes)
        return [current.reshape(shape).astype(jnp.float32) for current, shape in pairs]


def sum_all(array, axis, count):
    for bit in range(bits_of(count)):
        array = array + swap(array, axis, count, bit)
    return array


def row_items(unit_pair, row_count, mark_count):
    position = lax.iota(jnp.int32, row_count)
    first_end = unit_pair[0] * mark_count
    second_end = first_end + unit_pair[1] * mark_count
    return jnp.where(position < first_end, 0, jnp.where(position < second_end, 1, 2)).astype(
        jnp.int32
    )


NEGATIVE = -1e30
SCORE_SCALE = 0.125
BLOCK = 128
CHUNK = 256


def dot_with(left, right, left_dim, right_dim):
    return lax.dot_general(
        left, right, (((left_dim,), (right_dim,)), ((), ())), preferred_element_type=jnp.float32
    )


def halves(array):
    high = array.astype(jnp.bfloat16)
    return high, (array - high.astype(jnp.float32)).astype(jnp.bfloat16)


def dot_fine(left, right, left_dim, right_dim):
    left_high, left_low = halves(left)
    right_high, right_low = halves(right)
    return dot_with(
        jnp.concatenate([left_high, left_high, left_low], axis=left_dim),
        jnp.concatenate([right_high, right_low, right_high], axis=right_dim),
        left_dim,
        right_dim,
    )


def dot_low(left, right, left_dim, right_dim):
    return dot_with(left.astype(jnp.bfloat16), right.astype(jnp.bfloat16), left_dim, right_dim)


def item_ends(units_ref):
    first_end = units_ref[0, 0] * LANDMARKS
    return first_end, first_end + units_ref[0, 1] * LANDMARKS


def lane_items(units_ref, row_count):
    first_end, second_end = item_ends(units_ref)
    position = lax.broadcasted_iota(jnp.int32, (1, row_count), 1)
    first = (position < first_end).astype(jnp.float32)
    inside = (position < second_end).astype(jnp.float32)
    return first, inside - first, inside


def landmark_columns(units_ref):
    first_end, second_end = item_ends(units_ref)
    mark = lax.broadcasted_iota(jnp.int32, (2 * LANDMARKS, 1), 0)
    is_first = mark < LANDMARKS
    units = jnp.where(is_first, units_ref[0, 0], units_ref[0, 1])
    start = jnp.where(is_first, 0, first_end)
    low = start + jnp.where(is_first, mark, mark - LANDMARKS) * units
    return is_first, start, jnp.where(is_first, first_end, second_end), low, low + units


def select_matrix(units_ref, row_count):
    _, _, _, low, high = landmark_columns(units_ref)
    position = lax.broadcasted_iota(jnp.int32, (2 * LANDMARKS, row_count), 1)
    return ((position >= low) & (position < high)).astype(jnp.float32).astype(jnp.bfloat16)


def inverse_units(units_ref):
    lane = lax.broadcasted_iota(jnp.int32, (1, 2 * LANDMARKS), 1)
    units = jnp.where(lane < LANDMARKS, units_ref[0, 0], units_ref[0, 1]).astype(jnp.float32)
    return 1.0 / units


def same_item(size):
    row = lax.broadcasted_iota(jnp.int32, (size, size), 0)
    column = lax.broadcasted_iota(jnp.int32, (size, size), 1)
    return (row < LANDMARKS) == (column < LANDMARKS)


def scaled_eye(size, value):
    row = lax.broadcasted_iota(jnp.int32, (size, size), 0)
    column = lax.broadcasted_iota(jnp.int32, (size, size), 1)
    return jnp.where(row == column, value, 0.0)


def column_peaks(matrix):
    sums = jnp.sum(matrix, axis=0, keepdims=True)
    lane = lax.broadcasted_iota(jnp.int32, sums.shape, 1)
    first = jnp.max(jnp.where(lane < LANDMARKS, sums, NEGATIVE), axis=1, keepdims=True)
    second = jnp.max(jnp.where(lane < LANDMARKS, NEGATIVE, sums), axis=1, keepdims=True)
    return sums, jnp.where(lane < LANDMARKS, first, second)


def fill_windows(window_ref, rows, first, second):
    row_count = rows.shape[1]
    lane = lax.broadcasted_iota(jnp.int32, (1, BLOCK), 1)
    before = (lane >= BLOCK - 16).astype(jnp.float32).astype(jnp.bfloat16)
    behind = (lane < 16).astype(jnp.float32).astype(jnp.bfloat16)
    block_count = row_count // BLOCK
    for item, mask in ((0, first), (1, second)):
        kept = rows * mask.astype(jnp.bfloat16)
        for block in range(block_count):
            at = block * BLOCK
            edge = jnp.zeros((rows.shape[0], BLOCK), jnp.bfloat16)
            if block > 0:
                edge = edge + kept[:, at - BLOCK : at] * before
            if block + 1 < block_count:
                edge = edge + kept[:, at + BLOCK : at + 2 * BLOCK] * behind
            base = (2 * block + item) * HEAD_DIM
            window_ref[base : base + HEAD_DIM, :BLOCK] = kept[:, at : at + BLOCK]
            window_ref[base : base + HEAD_DIM, BLOCK:] = edge


def tap_matrix(tap_row):
    return pltpu.roll(
        jnp.broadcast_to(tap_row, (BLOCK, 2 * BLOCK)), 0, axis=1, stride=1, stride_axis=0
    ).astype(jnp.bfloat16)


def attention_start_body(
    units_ref,
    proj_ref,
    marks_ref,
    middle_ref,
    last_ref,
    values_ref,
    approx_ref,
    select_ref,
    in_ref,
):
    parts, _, part_width, row_count = proj_ref.shape
    part_heads = part_width // HEAD_DIM
    heads = parts * part_heads
    marks = 2 * LANDMARKS
    select_ref[...] = select_matrix(units_ref, row_count)
    _, start, end, _, _ = landmark_columns(units_ref)
    position = lax.broadcasted_iota(jnp.int32, (marks, row_count), 1)
    in_ref[...] = jnp.where((position >= start) & (position < end), 0.0, NEGATIVE)
    for part in range(parts):
        for kind in range(2):
            sums = dot_with(proj_ref[part, kind], select_ref[...], 1, 1)
            rows = slice(part * part_width, (part + 1) * part_width)
            marks_ref[kind, rows] = sums * inverse_units(units_ref)
    same = same_item(marks)

    def head_start(head, carry):
        at = pl.multiple_of(head * HEAD_DIM, HEAD_DIM)
        part = head // part_heads
        part_at = pl.multiple_of((head - part * part_heads) * HEAD_DIM, HEAD_DIM)
        mark_query = marks_ref[0, pl.ds(at, HEAD_DIM), :]
        mark_key = marks_ref[1, pl.ds(at, HEAD_DIM), :]
        logits = dot_fine(mark_query, mark_key, 0, 0) * SCORE_SCALE
        logits = jnp.where(same, logits, NEGATIVE)
        raised = jnp.exp(logits - jnp.max(logits, axis=1, keepdims=True))
        middle = raised / jnp.sum(raised, axis=1, keepdims=True)
        middle_ref[head] = middle
        _, peak = column_peaks(middle)
        approx_ref[head] = middle.T / peak
        query_rows = (mark_query * SCORE_SCALE).T.astype(jnp.bfloat16)
        scores = dot_with(query_rows, proj_ref[part, 1, pl.ds(part_at, HEAD_DIM), :], 1, 0) + in_ref[...]
        raised = jnp.exp(scores - jnp.max(scores, axis=1, keepdims=True))
        scale = 1.0 / jnp.sum(raised, axis=1, keepdims=True)
        last = (raised * scale).astype(jnp.bfloat16)
        last_ref[head] = last
        values_ref[head] = dot_with(last, proj_ref[part, 2, pl.ds(part_at, HEAD_DIM), :], 1, 1)
        return carry

    lax.fori_loop(0, heads, head_start, 0, unroll=2)


def attention_finish_body(
    units_ref,
    proj_ref,
    taps_ref,
    marks_ref,
    middle_ref,
    values_ref,
    approx_ref,
    attended_ref,
    first_ref,
    rough_ref,
    fine_ref,
    weighted_ref,
    own_ref,
    state_ref,
    window_ref,
    conv_ref,
):
    parts, _, part_width, row_count = proj_ref.shape
    part_heads = part_width // HEAD_DIM
    heads = parts * part_heads
    marks = 2 * LANDMARKS
    is_first = landmark_columns(units_ref)[0]
    first_end, _ = item_ends(units_ref)
    position = lax.broadcasted_iota(jnp.int32, (marks, row_count), 1)
    own_ref[...] = jnp.where((position < first_end) == is_first, 0.0, NEGATIVE)
    first, second, inside = lane_items(units_ref, row_count)
    state_ref[...] = approx_ref[...]
    seven, fifteen, thirteen = (scaled_eye(marks, value) for value in (7.0, 15.0, 13.0))

    def pinv_steps(saved_ref, count):
        kind = saved_ref.dtype

        def one_step(slot, carry):
            approx = [state_ref[head] for head in range(heads)]
            product = [dot_fine(middle_ref[head], approx[head], 1, 0) for head in range(heads)]
            inner = [
                fifteen - dot_fine(product[head], seven - product[head], 1, 0)
                for head in range(heads)
            ]
            outer = [thirteen - dot_fine(product[head], inner[head], 1, 0) for head in range(heads)]
            for head in range(heads):
                saved_ref[slot, 0, head] = approx[head].astype(kind)
                saved_ref[slot, 1, head] = product[head].astype(kind)
                saved_ref[slot, 2, head] = inner[head].astype(kind)
                saved_ref[slot, 3, head] = outer[head].astype(kind)
                state_ref[head] = dot_fine(0.25 * approx[head], outer[head], 1, 0)
            return carry

        lax.fori_loop(0, count, one_step, 0)

    pinv_steps(rough_ref, ROUGH_STEPS)
    pinv_steps(fine_ref, PINV_STEPS - ROUGH_STEPS)

    def head_end(head, carry):
        at = pl.multiple_of(head * HEAD_DIM, HEAD_DIM)
        part = head // part_heads
        part_at = pl.multiple_of((head - part * part_heads) * HEAD_DIM, HEAD_DIM)
        weighted = dot_fine(state_ref[head], values_ref[head], 1, 0)
        weighted_ref[head] = weighted
        weighted_rows = weighted.T.astype(jnp.bfloat16)
        key_rows = (marks_ref[1, pl.ds(at, HEAD_DIM), :] * SCORE_SCALE).T.astype(jnp.bfloat16)
        values = proj_ref[part, 2, pl.ds(part_at, HEAD_DIM), :]
        fill_windows(window_ref, values, first, second)
        conv_ref[...] = dot_with(window_ref[...], tap_matrix(taps_ref[pl.ds(head, 1), :]), 1, 1)
        for chunk in range(row_count // CHUNK):
            lanes = slice(chunk * CHUNK, (chunk + 1) * CHUNK)
            query = proj_ref[part, 0, pl.ds(part_at, HEAD_DIM), lanes]
            scores = dot_with(key_rows, query, 1, 0) + own_ref[:, lanes]
            raised = jnp.exp(scores - jnp.max(scores, axis=0, keepdims=True))
            scale = 1.0 / jnp.sum(raised, axis=0, keepdims=True)
            kept = (raised * scale).astype(jnp.bfloat16)
            first_ref[head, :, lanes] = kept
            mixed = dot_with(weighted_rows, kept, 1, 0) * inside[:, lanes]
            for piece in range(CHUNK // BLOCK):
                block = chunk * (CHUNK // BLOCK) + piece
                base = 2 * block * HEAD_DIM
                columns = slice(block * BLOCK, (block + 1) * BLOCK)
                conv = (
                    conv_ref[base : base + HEAD_DIM] * first[:, columns]
                    + conv_ref[base + HEAD_DIM : base + 2 * HEAD_DIM] * second[:, columns]
                )
                attended_ref[pl.ds(at, HEAD_DIM), columns] = (
                    mixed[:, piece * BLOCK : (piece + 1) * BLOCK] + conv
                ).astype(jnp.bfloat16)
        return carry

    lax.fori_loop(0, heads, head_end, 0, unroll=2)


def whole(count):
    return [pl.BlockSpec(memory_space=pltpu.VMEM)] * count


def attention_sizes(proj):
    parts, _, part_width, row_count = proj.shape
    width = parts * part_width
    heads = width // HEAD_DIM
    marks = 2 * LANDMARKS
    return width, row_count, heads, marks, (heads, marks, marks), (heads, marks, HEAD_DIM)


def attention_start(item_units, proj):
    width, row_count, heads, marks, square, thin = attention_sizes(proj)
    return pl.pallas_call(
        attention_start_body,
        in_specs=[pl.BlockSpec(memory_space=pltpu.SMEM)]
        + whole(1),
        out_specs=whole(5),
        out_shape=[
            jax.ShapeDtypeStruct((2, width, marks), jnp.float32),
            jax.ShapeDtypeStruct(square, jnp.float32),
            jax.ShapeDtypeStruct((heads, marks, row_count), jnp.bfloat16),
            jax.ShapeDtypeStruct(thin, jnp.float32),
            jax.ShapeDtypeStruct(square, jnp.float32),
        ],
        scratch_shapes=[
            pltpu.VMEM((marks, row_count), jnp.bfloat16),
            pltpu.VMEM((marks, row_count), jnp.float32),
        ],
        compiler_params=pltpu.CompilerParams(vmem_limit_bytes=48 * 1024 * 1024),
        cost_estimate=pl.CostEstimate(
            flops=9_000_000_000, bytes_accessed=8_000_000, transcendentals=0
        ),
    )(item_units, proj)


def attention_finish(item_units, proj, tap_rows, marks_rows, middle, last, values, approx):
    width, row_count, heads, marks, square, thin = attention_sizes(proj)
    stacked = 2 * row_count // BLOCK * HEAD_DIM
    return pl.pallas_call(
        attention_finish_body,
        in_specs=[pl.BlockSpec(memory_space=pltpu.SMEM)] + whole(6),
        out_specs=whole(5),
        out_shape=[
            jax.ShapeDtypeStruct((width, row_count), jnp.bfloat16),
            jax.ShapeDtypeStruct((heads, marks, row_count), jnp.bfloat16),
            jax.ShapeDtypeStruct((ROUGH_STEPS, 4) + square, jnp.bfloat16),
            jax.ShapeDtypeStruct((PINV_STEPS - ROUGH_STEPS, 4) + square, jnp.float32),
            jax.ShapeDtypeStruct(thin, jnp.float32),
        ],
        scratch_shapes=[
            pltpu.VMEM((marks, row_count), jnp.float32),
            pltpu.VMEM(square, jnp.float32),
            pltpu.VMEM((stacked, 2 * BLOCK), jnp.bfloat16),
            pltpu.VMEM((stacked, BLOCK), jnp.float32),
        ],
        compiler_params=pltpu.CompilerParams(vmem_limit_bytes=48 * 1024 * 1024),
        cost_estimate=pl.CostEstimate(
            flops=18_000_000_000, bytes_accessed=16_000_000, transcendentals=0
        ),
    )(item_units, proj, tap_rows, marks_rows, middle, values, approx)


def tap_rows_of(kernel):
    half = kernel.shape[1] // 2
    gap = jnp.zeros((kernel.shape[0], 2 * BLOCK - kernel.shape[1]), jnp.float32)
    return jnp.concatenate([kernel[:, half:], gap, kernel[:, :half]], axis=1)

def attention_backward_body(
    units_ref,
    proj_ref,
    taps_ref,
    grad_ref,
    first_ref,
    last_ref,
    marks_ref,
    middle_ref,
    rough_ref,
    fine_ref,
    values_ref,
    weighted_ref,
    out_ref,
    kernel_ref,
    select_ref,
    d_first_ref,
    d_last_ref,
    d_marks_ref,
    d_weighted_ref,
    d_values_ref,
    d_approx_ref,
    d_middle_ref,
    window_ref,
    d_window_ref,
    conv_ref,
):
    width = proj_ref.shape[1]
    row_count = proj_ref.shape[2]
    heads = width // HEAD_DIM
    marks = 2 * LANDMARKS
    select_ref[...] = select_matrix(units_ref, row_count)
    first, second, _ = lane_items(units_ref, row_count)
    inverse = inverse_units(units_ref)
    same = same_item(marks)
    chunks = [slice(at, at + CHUNK) for at in range(0, row_count, CHUNK)]

    def head_start(head, carry):
        at = pl.multiple_of(head * HEAD_DIM, HEAD_DIM)
        weighted_low = weighted_ref[head].astype(jnp.bfloat16)
        for lanes in chunks:
            kept = first_ref[head, :, lanes].astype(jnp.float32)
            d_kept = dot_with(weighted_low, grad_ref[pl.ds(at, HEAD_DIM), lanes], 1, 0)
            scaled = kept * d_kept
            d_scores = scaled - kept * jnp.sum(scaled, axis=0, keepdims=True)
            d_first_ref[head, :, lanes] = d_scores.astype(jnp.bfloat16)
        d_weighted = dot_with(first_ref[head], grad_ref[pl.ds(at, HEAD_DIM), :], 1, 1)
        d_weighted_ref[head] = d_weighted
        d_marks_ref[1, pl.ds(at, HEAD_DIM), :] = SCORE_SCALE * dot_with(
            proj_ref[0, pl.ds(at, HEAD_DIM), :], d_first_ref[head], 1, 1
        )
        d_approx = dot_fine(d_weighted, values_ref[head], 1, 1)
        d_approx_ref[head] = jnp.where(same, d_approx, 0.0)
        inverse_last = dot_fine(
            0.25 * fine_ref[PINV_STEPS - ROUGH_STEPS - 1, 0, head],
            fine_ref[PINV_STEPS - ROUGH_STEPS - 1, 3, head],
            1,
            0,
        )
        d_values_ref[head] = dot_fine(inverse_last, d_weighted, 0, 0)
        d_middle_ref[head] = jnp.zeros((marks, marks), jnp.float32)
        return carry

    lax.fori_loop(0, heads, head_start, 0, unroll=2)

    seven = scaled_eye(marks, 7.0)
    every = range(heads)

    def pinv_steps(saved_ref, count, dot):
        def one_step(step, carry):
            slot = count - 1 - step
            d_next = [d_approx_ref[head] for head in every]
            d_outer = [0.25 * dot(saved_ref[slot, 0, head], d_next[head], 0, 0) for head in every]
            d_inner = [-dot(saved_ref[slot, 1, head], d_outer[head], 0, 0) for head in every]
            d_lowest = [-dot(saved_ref[slot, 1, head], d_inner[head], 0, 0) for head in every]
            for head in every:
                product = saved_ref[slot, 1, head].astype(jnp.float32)
                d_product = (
                    -dot(d_outer[head], saved_ref[slot, 2, head], 1, 1)
                    - dot(d_inner[head], seven - product, 1, 1)
                    - d_lowest[head]
                )
                d_middle_ref[head] += dot(d_product, saved_ref[slot, 0, head], 1, 1)
                d_approx_ref[head] = 0.25 * dot(d_next[head], saved_ref[slot, 3, head], 1, 1) + dot(
                    middle_ref[head], d_product, 0, 0
                )
            return carry

        lax.fori_loop(0, count, one_step, 0)

    pinv_steps(fine_ref, PINV_STEPS - ROUGH_STEPS, dot_fine)
    pinv_steps(rough_ref, ROUGH_STEPS, dot_low)

    lane = lax.broadcasted_iota(jnp.int32, (1, marks), 1)

    def item_sums(row):
        total = jnp.sum(row, axis=1, keepdims=True)
        start = jnp.sum(jnp.where(lane < LANDMARKS, row, 0.0), axis=1, keepdims=True)
        return jnp.where(lane < LANDMARKS, start, total - start)

    def head_middle(head, carry):
        at = pl.multiple_of(head * HEAD_DIM, HEAD_DIM)
        middle = middle_ref[head]
        sums, peak = column_peaks(middle)
        d_start = d_approx_ref[head]
        d_start_turned = (d_start / peak).T
        d_peak = -item_sums(jnp.sum(d_start_turned * middle, axis=0, keepdims=True)) / peak
        at_peak = (sums == peak).astype(jnp.float32)
        d_column = at_peak * d_peak / item_sums(at_peak)
        d_middle = d_middle_ref[head] + d_start_turned + jnp.where(same, d_column, 0.0)
        scaled = middle * d_middle
        d_logits = SCORE_SCALE * (scaled - middle * jnp.sum(scaled, axis=1, keepdims=True))
        rows = pl.ds(at, HEAD_DIM)
        d_marks_ref[0, rows, :] = dot_fine(marks_ref[1, rows, :], d_logits, 1, 1)
        d_marks_ref[1, rows, :] += dot_fine(marks_ref[0, rows, :], d_logits, 1, 0)
        return carry

    lax.fori_loop(0, heads, head_middle, 0, unroll=2)

    row_index = lax.broadcasted_iota(jnp.int32, (BLOCK, BLOCK), 0)
    column_index = lax.broadcasted_iota(jnp.int32, (BLOCK, BLOCK), 1)
    turn = jnp.where(row_index + column_index == BLOCK - 1, 1.0, 0.0).astype(jnp.bfloat16)

    def head_end(head, carry):
        at = pl.multiple_of(head * HEAD_DIM, HEAD_DIM)
        rows = pl.ds(at, HEAD_DIM)
        d_values = d_values_ref[head]
        d_values_low = d_values.astype(jnp.bfloat16)
        d_values_turned = d_values.T.astype(jnp.bfloat16)
        inner = jnp.sum(d_values * values_ref[head], axis=1, keepdims=True)
        for lanes in chunks:
            d_kept = dot_with(d_values_low, proj_ref[2, rows, lanes], 1, 0)
            d_scores = last_ref[head, :, lanes].astype(jnp.float32) * (d_kept - inner)
            d_last_ref[:, lanes] = d_scores.astype(jnp.bfloat16)
        d_query = d_marks_ref[0, rows, :] + SCORE_SCALE * dot_with(
            proj_ref[1, rows, :], d_last_ref[...], 1, 1
        )
        d_query_low = (d_query * inverse).astype(jnp.bfloat16)
        d_key_low = (d_marks_ref[1, rows, :] * inverse).astype(jnp.bfloat16)
        mark_query = (marks_ref[0, rows, :] * SCORE_SCALE).astype(jnp.bfloat16)
        mark_key = (marks_ref[1, rows, :] * SCORE_SCALE).astype(jnp.bfloat16)
        fill_windows(window_ref, proj_ref[2, rows, :], first, second)
        fill_windows(d_window_ref, grad_ref[rows, :], first, second)
        conv_ref[...] = dot_with(d_window_ref[...], tap_matrix(taps_ref[pl.ds(head, 1), :]), 1, 1)
        joined = dot_with(d_window_ref[:, :BLOCK], window_ref[...], 0, 0)
        joined_high, joined_low = halves(joined)
        joined = dot_with(
            jnp.concatenate([turn, turn], axis=1),
            jnp.concatenate([joined_high, joined_low], axis=0),
            1,
            0,
        )
        joined = pltpu.roll(joined, BLOCK + 1, axis=1, stride=1, stride_axis=0)
        kernel_ref[pl.ds(head, 1), :] = jnp.sum(joined, axis=0, keepdims=True)
        for index, lanes in enumerate(chunks):
            select = select_ref[:, lanes]
            out_ref[rows, lanes] = (
                dot_with(mark_key, d_first_ref[head, :, lanes], 1, 0)
                + dot_with(d_query_low, select, 1, 0)
            ).astype(jnp.bfloat16)
            out_ref[pl.ds(width + at, HEAD_DIM), lanes] = (
                dot_with(mark_query, d_last_ref[:, lanes], 1, 0) + dot_with(d_key_low, select, 1, 0)
            ).astype(jnp.bfloat16)
            d_value = dot_with(d_values_turned, last_ref[head, :, lanes], 1, 0)
            for part in range(CHUNK // BLOCK):
                block = index * (CHUNK // BLOCK) + part
                base = 2 * block * HEAD_DIM
                columns = slice(block * BLOCK, (block + 1) * BLOCK)
                conv = (
                    conv_ref[base : base + HEAD_DIM] * first[:, columns]
                    + conv_ref[base + HEAD_DIM : base + 2 * HEAD_DIM] * second[:, columns]
                )
                out_ref[pl.ds(2 * width + at, HEAD_DIM), columns] = (
                    d_value[:, part * BLOCK : (part + 1) * BLOCK] + conv
                ).astype(jnp.bfloat16)
        return carry

    lax.fori_loop(0, heads, head_end, 0, unroll=2)


def attention_backward(item_units, proj, tap_rows, grad, *saved, part):
    parts, _, width, row_count = proj.shape
    heads = width // HEAD_DIM
    marks = 2 * LANDMARKS
    square = (heads, marks, marks)
    thin = (heads, marks, HEAD_DIM)
    stacked = 2 * row_count // BLOCK * HEAD_DIM

    def block(shape, split):
        place = tuple(part if dim == split else 0 for dim in range(len(shape)))
        sizes = tuple(size // parts if dim == split else size for dim, size in enumerate(shape))
        sizes = (None,) + sizes[1:] if len(shape) == 4 and split == 0 else sizes
        return pl.BlockSpec(sizes, lambda step: place, pipeline_mode=pl.Buffered(1))

    splits = (0, None, 0, 0, 0, 1, 0, 2, 2, 0, 0)
    tap_rows = tap_rows[part * heads : (part + 1) * heads]
    arrays = (proj, tap_rows, grad) + saved
    out, joined = pl.pallas_call(
        attention_backward_body,
        grid=(1,),
        in_specs=[pl.BlockSpec(memory_space=pltpu.SMEM)]
        + [block(array.shape, split) for array, split in zip(arrays, splits)],
        out_specs=[
            pl.BlockSpec((3 * width, row_count), lambda step: (0, 0)),
            pl.BlockSpec((heads, 2 * BLOCK), lambda step: (0, 0)),
        ],
        out_shape=[
            jax.ShapeDtypeStruct((3 * width, row_count), jnp.bfloat16),
            jax.ShapeDtypeStruct((heads, 2 * BLOCK), jnp.float32),
        ],
        scratch_shapes=[
            pltpu.VMEM((marks, row_count), jnp.bfloat16),
            pltpu.VMEM((heads, marks, row_count), jnp.bfloat16),
            pltpu.VMEM((marks, row_count), jnp.bfloat16),
            pltpu.VMEM((2, width, marks), jnp.float32),
            pltpu.VMEM(thin, jnp.float32),
            pltpu.VMEM(thin, jnp.float32),
            pltpu.VMEM(square, jnp.float32),
            pltpu.VMEM(square, jnp.float32),
            pltpu.VMEM((stacked, 2 * BLOCK), jnp.bfloat16),
            pltpu.VMEM((stacked, 2 * BLOCK), jnp.bfloat16),
            pltpu.VMEM((stacked, BLOCK), jnp.float32),
        ],
        compiler_params=pltpu.CompilerParams(vmem_limit_bytes=48 * 1024 * 1024),
        cost_estimate=pl.CostEstimate(
            flops=30_000_000_000 // parts, bytes_accessed=20_000_000 // parts, transcendentals=0
        ),
    )(item_units, *arrays)
    half = TAPS // 2
    return out, jnp.concatenate([joined[:, 2 * BLOCK - half :], joined[:, : TAPS - half]], axis=1)


ROWS = 512
LONG_ROWS = 512
OUTER = 384
PIECE = 512
SUB = 512
GELU_SCALE = 0.7978845608
GELU_CUBE = 0.044715


def row_block(width, rows=ROWS):
    return pl.BlockSpec((rows, width), lambda step: (step, 0))


def fixed_block(shape, column=0):
    return pl.BlockSpec(shape, lambda step: (0, column))


def row_lanes(rows=ROWS):
    return pl.BlockSpec((1, rows), lambda step: (0, step))


def as_column(row):
    return jnp.broadcast_to(row, (128, row.shape[1])).T[:, 0:1]


def as_row(column):
    return jnp.broadcast_to(column, (column.shape[0], 128)).T[0:1]


def dense_params():
    return pltpu.CompilerParams(vmem_limit_bytes=56 * 1024 * 1024)


def cost(flops, size):
    return pl.CostEstimate(flops=flops, bytes_accessed=size, transcendentals=0)


def normalized(rows):
    center = rows - jnp.mean(rows, axis=-1, keepdims=True)
    spread = jnp.mean(center * center, axis=-1, keepdims=True)
    scale = lax.rsqrt(spread + NORM_EPS)
    return center * scale, scale


def norm_backward(grad, gain, unit, scale):
    scaled = grad * gain
    lean = jnp.mean(scaled * unit, axis=-1, keepdims=True)
    return scale * (scaled - jnp.mean(scaled, axis=-1, keepdims=True) - unit * lean)


def column_sum(rows):
    return jnp.sum(rows, axis=0, keepdims=True)


def both(own_ref, other_ref, rows=...):
    return own_ref[rows].astype(jnp.float32) + other_ref[rows].astype(jnp.float32)


def gelu_parts(expanded):
    square = expanded * expanded
    bend = jnp.tanh(expanded * (GELU_SCALE + (GELU_SCALE * GELU_CUBE) * square))
    return square, 0.5 + 0.5 * bend, bend


def weight_blocks(expand, reduce):
    return [fixed_block(reduce.shape), fixed_block(reduce.shape)]


def hidden_forward_body(
    own_ref,
    other_ref,
    tokens_ref,
    weight_ref,
    shared_ref,
    bias_ref,
    expand_ref,
    reduce_ref,
    part_ref,
    low_ref,
    unit_ref,
    scale_ref,
    wide_ref,
    stat_ref,
):
    @pl.when(pl.program_id(0) == 0)
    def _():
        stat_ref[...] = jnp.zeros_like(stat_ref)

    weight_column = as_column(weight_ref[...])
    row_slices = [slice(at, at + SUB) for at in range(0, ROWS, SUB)]
    lows, scales, squares = [], [], []
    for rows in row_slices:
        branch = both(own_ref, other_ref, rows) + shared_ref[0:1]
        squares.append(column_sum(weight_column[rows] * branch * branch))
        unit, scale = normalized(tokens_ref[rows].astype(jnp.float32) + branch)
        hidden = unit * shared_ref[2:3] + shared_ref[3:4]
        unit_ref[rows] = unit.astype(jnp.bfloat16)
        scales.append(scale)
        hidden_low = hidden.astype(jnp.bfloat16)
        low_ref[rows] = hidden_low
        total = jnp.zeros((SUB, part_ref.shape[1]), jnp.float32)
        for at in range(0, reduce_ref.shape[1], PIECE):
            lanes = slice(at, at + PIECE)
            expanded = dot_with(hidden_low, expand_ref[:, lanes], 1, 0) + bias_ref[:, lanes]
            wide_ref[rows, lanes] = expanded.astype(jnp.bfloat16)
            half = gelu_parts(expanded)[1]
            active = (expanded * half).astype(jnp.bfloat16)
            total += dot_with(active, reduce_ref[:, lanes], 1, 1)
        part_ref[rows] = total.astype(jnp.bfloat16)
    stat_ref[...] += sum(squares)
    scale_ref[...] = as_row(jnp.concatenate(scales, axis=0))


def hidden_forward(own, other, tokens, weight_row, shared_rows, expand_bias, *weights):
    row_count, width = tokens.shape
    units = expand_bias.shape[1]
    return pl.pallas_call(
        hidden_forward_body,
        grid=(row_count // ROWS,),
        in_specs=[
            row_block(width),
            row_block(width),
            row_block(width),
            row_lanes(),
            fixed_block((6, width)),
            fixed_block((1, units)),
        ]
        + weight_blocks(*weights),
        out_specs=[
            row_block(width),
            row_block(width),
            row_block(width),
            row_lanes(),
            row_block(units),
            fixed_block((1, width)),
        ],
        out_shape=[
            jax.ShapeDtypeStruct((row_count, width), jnp.bfloat16),
            jax.ShapeDtypeStruct((row_count, width), jnp.bfloat16),
            jax.ShapeDtypeStruct((row_count, width), jnp.bfloat16),
            jax.ShapeDtypeStruct((1, row_count), jnp.float32),
            jax.ShapeDtypeStruct((row_count, units), jnp.bfloat16),
            jax.ShapeDtypeStruct((1, width), jnp.float32),
        ],
        compiler_params=dense_params(),
        cost_estimate=cost(4 * row_count * width * units, 30_000_000),
    )(own, other, tokens, weight_row, shared_rows, expand_bias, *weights)


def hidden_backward_body(
    own_ref,
    other_ref,
    low_ref,
    cotangent_ref,
    weight_ref,
    shared_ref,
    wide_ref,
    expand_ref,
    reduce_ref,
    output_ref,
    d_two_ref,
    reduce_out,
    expand_out,
    part_ref,
    sums_ref,
    bias_ref,
    reduce_sum,
    expand_sum,
):
    @pl.when(pl.program_id(0) == 0)
    def _():
        sums_ref[...] = jnp.zeros_like(sums_ref)
        bias_ref[...] = jnp.zeros_like(bias_ref)
        reduce_sum[...] = jnp.zeros_like(reduce_sum)
        expand_sum[...] = jnp.zeros_like(expand_sum)

    weight_column = as_column(weight_ref[...])
    for start in range(0, ROWS, SUB):
        rows = slice(start, start + SUB)
        branch = both(own_ref, other_ref, rows) + shared_ref[1:2]
        weight = weight_column[rows]
        unit, scale = normalized(low_ref[rows].astype(jnp.float32) + branch)
        output_ref[rows] = unit * shared_ref[4:5] + shared_ref[5:6]
        grad = cotangent_ref[rows].astype(jnp.float32) * weight
        d_res = norm_backward(grad, shared_ref[4:5], unit, scale)
        d_two = d_res.astype(jnp.bfloat16)
        d_two_ref[rows] = d_two
        d_two_turned = d_res.T.astype(jnp.bfloat16)
        low_turned = low_ref[rows].astype(jnp.float32).T.astype(jnp.bfloat16)
        sums_ref[...] += jnp.concatenate(
            [
                column_sum(weight * branch * branch),
                column_sum(d_res),
                column_sum(grad * unit),
                column_sum(grad),
                jnp.broadcast_to(column_sum(weight), (1, grad.shape[1])),
                jnp.zeros((3, grad.shape[1]), jnp.float32),
            ],
            axis=0,
        )
        total = jnp.zeros((SUB, part_ref.shape[1]), jnp.float32)
        for at in range(0, reduce_ref.shape[1], PIECE):
            lanes = slice(at, at + PIECE)
            d_active = dot_with(d_two, reduce_ref[:, lanes], 1, 0)
            expanded = wide_ref[rows, lanes].astype(jnp.float32)
            square, half, bend = gelu_parts(expanded)
            active = (expanded * half).astype(jnp.bfloat16)
            slope = half + (0.5 * expanded) * (1.0 - bend * bend) * (
                GELU_SCALE + (3.0 * GELU_SCALE * GELU_CUBE) * square
            )
            d_expanded = (slope * d_active).astype(jnp.bfloat16)
            reduce_sum[:, lanes] += dot_with(d_two_turned, active, 1, 0)
            expand_sum[:, lanes] += dot_with(low_turned, d_expanded, 1, 0)
            bias_ref[:, lanes] += column_sum(d_expanded.astype(jnp.float32))
            total += dot_with(d_expanded, expand_ref[:, lanes], 1, 1)
        part_ref[rows] = total.astype(jnp.bfloat16)

    @pl.when(pl.program_id(0) == pl.num_programs(0) - 1)
    def _():
        reduce_out[...] = reduce_sum[...].astype(jnp.bfloat16)
        expand_out[...] = expand_sum[...].astype(jnp.bfloat16)


def hidden_backward(own, other, low, cotangent, weight_row, shared_rows, wide, *weights):
    row_count, width = cotangent.shape
    units = wide.shape[1]
    return pl.pallas_call(
        hidden_backward_body,
        grid=(row_count // ROWS,),
        in_specs=[
            row_block(width),
            row_block(width),
            row_block(width),
            row_block(width),
            row_lanes(),
            fixed_block((6, width)),
            row_block(units),
        ]
        + weight_blocks(*weights),
        out_specs=[
            row_block(width),
            row_block(width),
            fixed_block((width, units)),
            fixed_block((width, units)),
            row_block(width),
            fixed_block((8, width)),
            fixed_block((1, units)),
        ],
        out_shape=[
            jax.ShapeDtypeStruct((row_count, width), jnp.float32),
            jax.ShapeDtypeStruct((row_count, width), jnp.bfloat16),
            jax.ShapeDtypeStruct((width, units), jnp.bfloat16),
            jax.ShapeDtypeStruct((width, units), jnp.bfloat16),
            jax.ShapeDtypeStruct((row_count, width), jnp.bfloat16),
            jax.ShapeDtypeStruct((8, width), jnp.float32),
            jax.ShapeDtypeStruct((1, units), jnp.float32),
        ],
        scratch_shapes=[pltpu.VMEM((width, units), jnp.float32)] * 2,
        compiler_params=dense_params(),
        cost_estimate=cost(4 * row_count * width * units, 30_000_000),
    )(own, other, low, cotangent, weight_row, shared_rows, wide, *weights)


def norm_one_body(
    own_ref,
    other_ref,
    d_two_ref,
    unit_ref,
    scale_ref,
    inside_ref,
    shared_ref,
    mixing_ref,
    d_one_ref,
    d_mixed_ref,
    sums_ref,
    turned_ref,
):
    @pl.when(pl.program_id(0) == 0)
    def _():
        sums_ref[...] = jnp.zeros_like(sums_ref)
        turned_ref[...] = mixing_ref[...].astype(jnp.float32).T.astype(jnp.bfloat16)

    grad = both(own_ref, other_ref) + d_two_ref[...].astype(jnp.float32)
    unit = unit_ref[...].astype(jnp.float32)
    d_res = norm_backward(grad, shared_ref[2:3], unit, as_column(scale_ref[...]))
    d_one = d_res.astype(jnp.bfloat16)
    d_one_ref[...] = d_one
    sums_ref[...] += jnp.concatenate(
        [
            column_sum(d_res),
            column_sum(grad * unit),
            column_sum(grad),
            jnp.zeros((5, grad.shape[1]), jnp.float32),
        ],
        axis=0,
    )
    d_mixed = dot_with(turned_ref[...], d_one, 1, 1) * inside_ref[...]
    d_mixed_ref[...] = d_mixed.astype(jnp.bfloat16)


def norm_one_backward(own, other, d_two, unit, scale, inside_row, shared_rows, late_full, local_width):
    row_count, width = d_two.shape
    return pl.pallas_call(
        norm_one_body,
        grid=(row_count // LONG_ROWS,),
        in_specs=[
            row_block(width, LONG_ROWS),
            row_block(width, LONG_ROWS),
            row_block(width, LONG_ROWS),
            row_block(width, LONG_ROWS),
            row_lanes(LONG_ROWS),
            pl.BlockSpec((1, LONG_ROWS), lambda step: (0, step)),
            fixed_block((6, width)),
            fixed_block((width, local_width), late_full.shape[1] // local_width - 1),
        ],
        out_specs=[
            row_block(width, LONG_ROWS),
            pl.BlockSpec((local_width, LONG_ROWS), lambda step: (0, step)),
            fixed_block((8, width)),
        ],
        out_shape=[
            jax.ShapeDtypeStruct((row_count, width), jnp.bfloat16),
            jax.ShapeDtypeStruct((local_width, row_count), jnp.bfloat16),
            jax.ShapeDtypeStruct((8, width), jnp.float32),
        ],
        scratch_shapes=[pltpu.VMEM((local_width, width), jnp.bfloat16)],
        compiler_params=dense_params(),
        cost_estimate=cost(2 * row_count * width * local_width, 14_000_000),
    )(own, other, d_two, unit, scale, inside_row, shared_rows, late_full)


def turned_dot_body(*refs):
    *pairs, out_ref = refs
    total = jnp.zeros(out_ref.shape, jnp.float32)
    for at in range(0, len(pairs), 2):
        left = pairs[at][...]
        left = left.reshape(-1, left.shape[-1])
        total += dot_with(left, pairs[at + 1][...], 0, 1)
    out_ref[...] = total.astype(jnp.bfloat16)


def turned_dot(lefts, rights, columns, width):
    row_count = lefts[0].shape[-1]
    specs, arrays, terms = [], [], 0
    for left, right, column in zip(lefts, rights, columns):
        shape = left.shape[:-1] + (LONG_ROWS,)
        place = (0,) * (left.ndim - 1)
        specs.append(pl.BlockSpec(shape, lambda step, place=place: place + (step,)))
        depth = left.size // row_count
        specs.append(fixed_block((width, depth), column))
        arrays += [left, right]
        terms += depth
    return pl.pallas_call(
        turned_dot_body,
        grid=(row_count // LONG_ROWS,),
        in_specs=specs,
        out_specs=row_block(width, LONG_ROWS),
        out_shape=jax.ShapeDtypeStruct((row_count, width), jnp.bfloat16),
        compiler_params=dense_params(),
        cost_estimate=cost(2 * row_count * width * terms, 8_000_000),
    )(*arrays)

def turned_outer_body(left_ref, right_ref, out_ref):
    product = dot_with(left_ref[...], right_ref[...], 1, 0)
    out_ref[...] = product.T.astype(jnp.bfloat16)


def turned_outer(left, right):
    depth, width = right.shape
    return pl.pallas_call(
        turned_outer_body,
        grid=(width // OUTER,),
        in_specs=[
            fixed_block(left.shape),
            pl.BlockSpec((depth, OUTER), lambda step: (0, step)),
        ],
        out_specs=pl.BlockSpec((OUTER, left.shape[0]), lambda step: (step, 0)),
        out_shape=jax.ShapeDtypeStruct((width, left.shape[0]), jnp.bfloat16),
        compiler_params=dense_params(),
        cost_estimate=cost(2 * depth * width * left.shape[0], 6_000_000),
    )(left, right)


def project_body(first_ref, second_ref, tokens_ref, bias_ref, out_ref, turned_ref):
    part_width = first_ref.shape[1]

    @pl.when(pl.program_id(0) == 0)
    def _():
        for part, weight_ref in enumerate((first_ref, second_ref)):
            turned = weight_ref[...].astype(jnp.float32).T
            turned_ref[part * part_width : (part + 1) * part_width] = turned.astype(jnp.bfloat16)

    rows = dot_with(turned_ref[...], tokens_ref[...], 1, 1) + bias_ref[...]
    out_ref[...] = rows.astype(jnp.bfloat16).reshape(out_ref.shape)


def project(first, second, tokens, bias_column):
    row_count, width = tokens.shape
    part_width = first.shape[1]
    shape = (2, 3, part_width // 3, row_count)
    return pl.pallas_call(
        project_body,
        grid=(row_count // LONG_ROWS,),
        in_specs=[
            fixed_block((width, part_width)),
            fixed_block((width, part_width)),
            row_block(width, LONG_ROWS),
            fixed_block((2 * part_width, 1)),
        ],
        out_specs=pl.BlockSpec(shape[:3] + (LONG_ROWS,), lambda step: (0, 0, 0, step)),
        out_shape=jax.ShapeDtypeStruct(shape, jnp.bfloat16),
        scratch_shapes=[pltpu.VMEM((2 * part_width, width), jnp.bfloat16)],
        compiler_params=dense_params(),
        cost_estimate=cost(4 * row_count * width * part_width, 8_000_000),
    )(first, second, tokens, bias_column)


def adamw(master, moment, square, gradient, factor, learn_rate, decay_rate):
    clipped = gradient * factor
    moment_new = BETA_ONE * moment + (1.0 - BETA_ONE) * clipped
    square_new = BETA_TWO * square + (1.0 - BETA_TWO) * clipped * clipped
    step_size = moment_new / CORRECT_ONE / (jnp.sqrt(square_new / CORRECT_TWO) + ADAM_EPS)
    return (master - learn_rate * (step_size + decay_rate * master), moment_new, square_new)

def finish_body(
    places_ref,
    expand_ref,
    reduce_ref,
    mixing_ref,
    hidden_ref,
    left_ref,
    right_ref,
    inputs_ref,
    stat_ref,
    sums_ref,
    expand_out,
    reduce_out,
    mixing_out,
    left_out,
    right_out,
    row_ref,
    *,
    bias_share,
    shared_share,
):
    mine = places_ref[0]
    squares = jnp.zeros((1, 1), jnp.float32)

    def total(values):
        return jnp.sum(jnp.sum(values, axis=0, keepdims=True), axis=1, keepdims=True)

    at = 0
    for current_ref, out_ref in (
        (expand_ref, expand_out),
        (reduce_ref, reduce_out),
        (mixing_ref, mixing_out),
    ):
        width = out_ref.shape[1]
        share = current_ref[mine] + hidden_ref[:, at : at + width].astype(jnp.float32)
        out_ref[...] = share
        squares += total(share * share)
        at += width
    rows = left_ref.shape[1]
    received = inputs_ref[...].astype(jnp.float32)
    left = left_ref[mine] + received[:rows]
    right = right_ref[mine] + received[rows:]
    left_out[...] = left
    right_out[...] = right
    squares += total(left * left) + total(right[:rows] * right[:rows])
    small = right[rows : rows + 1]
    kernel = right[rows + 1 :]
    lane = lax.broadcasted_iota(jnp.int32, small.shape, 1)
    shared_counts = places_ref[1].astype(jnp.float32)
    factor = jnp.where(
        lane < bias_share, 1.0, jnp.where(lane < bias_share + shared_share, shared_counts, 0.0)
    )
    squares += total(small * small * factor) + total(kernel * kernel)
    lane = lax.broadcasted_iota(jnp.int32, (1, 128), 1)
    row = jnp.where(lane == 0, squares, 0.0)
    row += jnp.where(lane == 1, total(stat_ref[...]), 0.0)
    row += jnp.where(lane == 2, total(sums_ref[0:1]), 0.0)
    row_ref[:, :128] = row + jnp.where(lane == 3, sums_ref[4:5, 0:1], 0.0)
    row_ref[:, 128:] = kernel[:, : row_ref.shape[1] - 128]


def finish(places, hidden, inputs, stat_one, sums_two, bias_share, shared_share):
    def flat(array):
        return array.reshape(array.shape[-2:])

    def pair(array):
        return array.reshape((2,) + array.shape[-2:])

    arrays = [pair(array) for array in hidden.currents] + [flat(hidden.received)]
    arrays += [pair(array) for array in inputs.currents] + [flat(inputs.received)]
    arrays += [stat_one, sums_two]
    shapes = [array.shape[-2:] for array in hidden.currents + inputs.currents] + [(1, 384)]
    return pl.pallas_call(
        functools.partial(finish_body, bias_share=bias_share, shared_share=shared_share),
        in_specs=[pl.BlockSpec(memory_space=pltpu.SMEM)] + whole(len(arrays)),
        out_specs=whole(len(shapes)),
        out_shape=[jax.ShapeDtypeStruct(shape, jnp.float32) for shape in shapes],
        compiler_params=dense_params(),
        cost_estimate=cost(1_000_000, 3_000_000),
    )(places, *arrays)


def update_body(*refs, width, bias_share, shard_rows):
    totals_ref, kernel_ref, expand_ref, reduce_ref, mixing_ref, left_ref, right_ref = refs[:7]
    old_refs, new_refs, row_ref = refs[7:28], refs[28:49], refs[49]
    rows = left_ref.shape[0]
    totals = totals_ref[...]
    lane = lax.broadcasted_iota(jnp.int32, totals.shape, 1)
    means = jnp.sqrt(totals / jnp.where(lane == 0, 1.0, totals[:, 3:4] * width))
    row_ref[...] = means
    factor = CLIP_NORM / (means[:, 0:1] + CLIP_EPS)

    def put(index, place, gradient, rate, decay):
        old = [old_refs[3 * index + kind][place] for kind in range(3)]
        for kind, value in enumerate(adamw(*old, gradient, factor, rate, decay)):
            new_refs[3 * index + kind][place] = value

    part_width = right_ref.shape[1] // 3
    for part, share_ref in enumerate((left_ref, right_ref)):
        for kind in range(3):
            gradient = share_ref[:rows, kind * part_width : (kind + 1) * part_width]
            lanes = slice(part * part_width, (part + 1) * part_width)
            put(0, (kind, slice(None), lanes), gradient, RATE_MATRIX, WEIGHT_DECAY)
    put(1, ..., mixing_ref[...], RATE_MATRIX, WEIGHT_DECAY)
    put(2, ..., expand_ref[...], RATE_MATRIX, WEIGHT_DECAY)
    put(3, ..., reduce_ref[...], RATE_MATRIX, WEIGHT_DECAY)
    small = slice(rows, rows + 1)
    put(4, ..., right_ref[small, :bias_share], RATE_VECTOR, 0.0)
    for row in range(6):
        start = bias_share + row * shard_rows
        place = (slice(row, row + 1), slice(None))
        put(5, place, right_ref[small, start : start + shard_rows], RATE_VECTOR, 0.0)
    heads, taps = old_refs[18].shape
    for row in range(heads):
        start = 128 + row * taps
        place = (slice(row, row + 1), slice(None))
        put(6, place, kernel_ref[:, start : start + taps], RATE_VECTOR, 0.0)


def update(totals, kernel_row, shares, olds, width, bias_share, shard_rows):
    arrays = [totals, kernel_row] + shares + olds
    shapes = [old.shape for old in olds] + [(1, 128)]
    return pl.pallas_call(
        functools.partial(update_body, width=width, bias_share=bias_share, shard_rows=shard_rows),
        in_specs=whole(len(arrays)),
        out_specs=whole(len(shapes)),
        out_shape=[jax.ShapeDtypeStruct(shape, jnp.float32) for shape in shapes],
        compiler_params=dense_params(),
        cost_estimate=cost(5_000_000, 6_000_000),
    )(*arrays)


def body(
    tokens,
    cotangent,
    item_units,
    counted,
    inputs_weight,
    inputs_moment,
    inputs_square,
    mixing_weight,
    mixing_moment,
    mixing_square,
    expand_weight,
    expand_moment,
    expand_square,
    reduce_weight,
    reduce_moment,
    reduce_square,
    biases_weight,
    biases_moment,
    biases_square,
    shared_weight,
    shared_moment,
    shared_square,
    kernel_weight,
    kernel_moment,
    kernel_square,
):
    dp_count = lax.axis_size("dp")
    bits = list(range(bits_of(dp_count)))
    first_order, second_order = bits, bits[:2][::-1] + bits[2:]
    row_count, width_full = tokens.shape
    local_width = inputs_weight.shape[2]
    shard_rows = inputs_weight.shape[1]
    bias_share = biases_weight.shape[1]
    hidden_units = expand_weight.shape[1]
    part_width = local_width // 2
    part_lanes = [slice(0, part_width), slice(part_width, local_width)]

    high_bits = bits[2:][::-1]
    low_orders = (bits[:2][::-1], bits[:2])
    small_low = jnp.concatenate([biases_weight.reshape(-1), shared_weight.reshape(-1)])
    small_low = jnp.pad(small_low, (0, (-small_low.shape[0]) % (3 * part_width)))
    small_low = small_low.astype(jnp.bfloat16).reshape(-1, 3 * part_width)
    inputs_low = [
        jnp.concatenate([inputs_weight[c][:, lanes] for c in range(3)], axis=1).astype(jnp.bfloat16)
        for lanes in part_lanes
    ]
    inputs_low = jnp.concatenate([inputs_low[1], inputs_low[0], small_low], axis=0)
    sizes = (shard_rows, inputs_low.shape[0] - shard_rows)
    inputs_gather = Gather(inputs_low, dp_count, high_bits)
    late_low = jnp.concatenate(
        [expand_weight.astype(jnp.bfloat16)]
        + [weight.astype(jnp.bfloat16).T for weight in (mixing_weight, reduce_weight)],
        axis=1,
    )
    inputs_gather.step()
    late_low = after(late_low, inputs_gather.current)
    for _ in high_bits[1:]:
        inputs_gather.step()
    right_gather, left_gather = inputs_gather.split(sizes, -2, low_orders)
    inputs_right = right_gather.finish()
    left_full = left_gather.finish().reshape(dp_count, sizes[1], 3 * part_width)
    inputs_left = left_full[:, :shard_rows].reshape(-1, 3 * part_width)
    small_full = left_full[:, shard_rows:].reshape(dp_count, -1)
    late_gather = Gather(late_low, dp_count, high_bits)
    for _ in high_bits:
        late_gather.step()
    sizes = (hidden_units + local_width, hidden_units)
    expand_gather, reduce_gather = late_gather.split(sizes, -1, low_orders)
    biases_row = small_full[:, :bias_share].reshape(-1).astype(jnp.float32)
    shared_rows = small_full[:, bias_share : bias_share + 6 * shard_rows]
    shared_rows = shared_rows.reshape(dp_count, 6, shard_rows).transpose(1, 0, 2)
    shared_rows = shared_rows.reshape(6, -1).astype(jnp.float32)
    query_bias = biases_row[:local_width]
    value_bias = biases_row[local_width : 2 * local_width]
    expand_bias = biases_row[2 * local_width :][None, :]
    zero_bias = jnp.zeros((part_width,), jnp.float32)
    bias_column = jnp.concatenate(
        [
            piece
            for lanes in part_lanes
            for piece in (query_bias[lanes], zero_bias, value_bias[lanes])
        ]
    )[:, None]

    row_item = row_items(item_units[0], row_count, LANDMARKS)
    inside = (row_item < 2).astype(jnp.float32)
    weight_rows = counted.astype(jnp.float32) * inside
    weight_row = weight_rows[None, :]

    tied_tokens = after(tokens, expand_gather.current, reduce_gather.current)
    proj = project(inputs_left, inputs_right, tied_tokens, bias_column)
    marks, middle, last, values, approx = attention_start(item_units, proj)
    expand_gather.step(marks)
    reduce_gather.step(marks)
    tied_marks = after(marks, expand_gather.current, reduce_gather.current)
    attended, kept, rough, fine, weighted = attention_finish(
        item_units, proj, tap_rows_of(kernel_weight), tied_marks, middle, last, values, approx
    )
    saved = (kept, last, marks, middle, rough, fine, values, weighted)
    expand_full = expand_gather.finish()
    reduce_full = reduce_gather.finish()
    hidden_weights = (expand_full, reduce_full)
    mixing_column = expand_full.shape[1] // local_width - 1
    tied_attended = after(attended, reduce_full)
    own_one = turned_dot([tied_attended], [expand_full], [mixing_column], width_full)
    other_one = swap(own_one, "head", 2, 0)
    own_two, hidden_low, unit_one, scale_one, wide, stat_one = hidden_forward(
        own_one, other_one, tokens, weight_row, shared_rows, expand_bias, *hidden_weights
    )
    other_two = swap(own_two, "head", 2, 0)
    output_rows, d_two, reduce_grad, expand_grad, own_three, sums_two, expand_sums = hidden_backward(
        own_two, other_two, hidden_low, cotangent, weight_row, shared_rows, wide, *hidden_weights
    )
    other_three = swap(own_three, "head", 2, 0)
    reduce_scatter = Scatter([reduce_grad], dp_count, second_order).send()
    expand_scatter = Scatter([expand_grad], dp_count, first_order).send()
    d_one, d_mixed, sums_one = norm_one_backward(
        own_three,
        other_three,
        d_two,
        unit_one,
        scale_one,
        inside[None, :],
        shared_rows,
        expand_full,
        local_width,
    )
    mixing_grad = jnp.einsum("rd,kr->dk", d_one, attended, preferred_element_type=jnp.float32)
    mixing_scatter = Scatter([mixing_grad.astype(jnp.bfloat16)], dp_count, first_order).send()
    first_scatters = (reduce_scatter, expand_scatter, mixing_scatter)
    d_mixed = after(d_mixed, *[scatter.sent for scatter in first_scatters])
    back_taps = tap_rows_of(kernel_weight[:, ::-1])
    d_left, kernel_left = attention_backward(item_units, proj, back_taps, d_mixed, *saved, part=0)

    for scatter in first_scatters:
        scatter.take(d_left).send()
    left_grad = turned_outer(d_left, tokens)
    left_scatter = Scatter([left_grad], dp_count, second_order).send()
    d_mixed = after(d_mixed, left_scatter.sent, *[scatter.sent for scatter in first_scatters])
    d_right, kernel_right = attention_backward(item_units, proj, back_taps, d_mixed, *saved, part=1)
    right_grad = turned_outer(d_right, tokens)
    left_sums, right_sums = [
        jnp.sum(gradient.astype(jnp.float32), axis=1).reshape(3, part_width)
        for gradient in (d_left, d_right)
    ]
    biases_grad = jnp.concatenate(
        [left_sums[0], right_sums[0], left_sums[2], right_sums[2], expand_sums.reshape(-1)]
    )
    shared_grad = jnp.concatenate(
        [sums_one[0:1], sums_two[1:2], sums_one[1:3], sums_two[2:4]], axis=0
    )
    shared_grad = shared_grad.reshape(6, dp_count, shard_rows).transpose(1, 0, 2)
    kernel_grad = jnp.concatenate([kernel_left, kernel_right], axis=0)
    columns = 3 * part_width

    def widened(array):
        return jnp.pad(array, ((0, 0), (0, columns - array.shape[1])))[:, None]

    tap_count = kernel_grad.shape[1]
    tap_share = -(-tap_count // dp_count)
    tap_owner = jnp.arange(tap_count) // tap_share
    kernel_rows = jnp.where(
        tap_owner[None, None, :] == jnp.arange(dp_count)[:, None, None], kernel_grad[None], 0.0
    )
    small_rows = jnp.concatenate(
        [biases_grad.reshape(dp_count, bias_share), shared_grad.reshape(dp_count, -1)], axis=1
    )
    right_rows = jnp.concatenate(
        [
            right_grad.reshape(dp_count, shard_rows, columns),
            widened(small_rows).astype(jnp.bfloat16),
            widened(kernel_rows.reshape(dp_count, -1)).astype(jnp.bfloat16),
        ],
        axis=1,
    )
    right_rows = right_rows.reshape(-1, columns)
    right_scatter = Scatter([right_rows], dp_count, first_order).send()
    for scatter in first_scatters:
        scatter.take(right_scatter.sent)
    hidden_scatter = expand_scatter.merge(reduce_scatter, mixing_scatter).send()
    left_scatter.take(right_scatter.sent).send()
    d_both = after(d_right, right_scatter.sent, hidden_scatter.sent, left_scatter.sent)
    own_four = turned_dot([d_left, d_both], [inputs_left, inputs_right], [0, 0], width_full)
    other_four = swap(own_four, "head", 2, 0)
    hidden_scatter.take(own_four).send()
    right_scatter.take(own_four).send()
    input_grad = (
        own_four.astype(jnp.float32) + other_four.astype(jnp.float32) + d_one.astype(jnp.float32)
    )
    inputs_scatter = left_scatter.merge(right_scatter, join=-2).send()
    dp_index, head_index = lax.axis_index("dp"), lax.axis_index("head")
    places = jnp.stack([(dp_index >> bits[-1]) & 1, head_index == 0]).astype(jnp.int32)
    inputs_scatter.take(input_grad)
    while hidden_scatter.order:
        hidden_scatter.take().send()
    while inputs_scatter.order:
        inputs_scatter.take().send()
    *shares, final_row = finish(
        places, hidden_scatter, inputs_scatter, stat_one, sums_two, bias_share, 6 * shard_rows
    )
    final_row = sum_all(final_row, "dp", dp_count)
    totals = sum_all(final_row[:, :128], "head", 2)
    olds = [
        inputs_weight,
        inputs_moment,
        inputs_square,
        mixing_weight.T,
        mixing_moment.T,
        mixing_square.T,
        expand_weight,
        expand_moment,
        expand_square,
        reduce_weight.T,
        reduce_moment.T,
        reduce_square.T,
        biases_weight,
        biases_moment,
        biases_square,
        shared_weight,
        shared_moment,
        shared_square,
        kernel_weight,
        kernel_moment,
        kernel_square,
    ]
    *news, row = update(totals, final_row, shares, olds, width_full, bias_share, shard_rows)
    for index in (3, 4, 5, 9, 10, 11):
        news[index] = news[index].T
    return (output_rows, input_grad, *news, row[0, 0], row[0, 1:3])


def solution(mesh):
    placed = (
        P("dp", None),
        P("dp", None),
        P("dp", None),
        P("dp"),
        P(None, "dp", "head"),
        P(None, "dp", "head"),
        P(None, "dp", "head"),
        P("head", "dp"),
        P("head", "dp"),
        P("head", "dp"),
        P("dp", "head"),
        P("dp", "head"),
        P("dp", "head"),
        P("head", "dp"),
        P("head", "dp"),
        P("head", "dp"),
        P("head", "dp"),
        P("head", "dp"),
        P("head", "dp"),
        P(None, "dp"),
        P(None, "dp"),
        P(None, "dp"),
        P("head", None),
        P("head", None),
        P("head", None),
    )
    return jax.shard_map(
        body,
        mesh=mesh,
        in_specs=placed,
        out_specs=(
            P("dp", None),
            P("dp", None),
            P(None, "dp", "head"),
            P(None, "dp", "head"),
            P(None, "dp", "head"),
            P("head", "dp"),
            P("head", "dp"),
            P("head", "dp"),
            P("dp", "head"),
            P("dp", "head"),
            P("dp", "head"),
            P("head", "dp"),
            P("head", "dp"),
            P("head", "dp"),
            P("head", "dp"),
            P("head", "dp"),
            P("head", "dp"),
            P(None, "dp"),
            P(None, "dp"),
            P(None, "dp"),
            P("head", None),
            P("head", None),
            P("head", None),
            P(),
            P(),
        ),
        check_vma=False,
    )
```

```python
import functools

import jax
import jax.numpy as jnp
from jax import lax
from jax.experimental import pallas as pl
from jax.experimental.pallas import tpu as pltpu
from jax.sharding import PartitionSpec as P

HEAD_DIM = 64
LANDMARKS = 64
PINV_STEPS = 6
ROUGH_STEPS = 4
TAPS = 33
NORM_EPS = 1e-05
CLIP_NORM = 1.0
CLIP_EPS = 1e-06
BETA_ONE = 0.9
BETA_TWO = 0.98
ADAM_EPS = 1e-08
RATE_MATRIX = 0.04
RATE_VECTOR = 0.5
WEIGHT_DECAY = 0.01
CORRECT_ONE = 1.0 - BETA_ONE**5
CORRECT_TWO = 1.0 - BETA_TWO**5

def bits_of(count):
    bit_count = 0
    while (1 << bit_count) < count:
        bit_count += 1
    return bit_count


def swap(array, axis, count, bit):
    return lax.ppermute(array, axis, [(i, i ^ (1 << bit)) for i in range(count)])


class Gather:
    def __init__(self, array, count, order):
        self.count, self.order = count, list(order)
        self.shape = (count * array.shape[0],) + array.shape[1:]
        self.current = array.reshape((1,) * bits_of(count) + array.shape)

    def step(self, *others):
        bit = self.order.pop(0)
        dim = bits_of(self.count) - 1 - bit
        other = swap(self.current, "dp", self.count, bit)
        other = after(other, *others) if others else other
        self.current = jnp.where(
            (lax.axis_index("dp") >> bit) & 1 == 0,
            jnp.concatenate([self.current, other], dim),
            jnp.concatenate([other, self.current], dim),
        )
        return self

    def split(self, sizes, dim, orders):
        pieces, at = [], 0
        for size, order in zip(sizes, orders):
            piece = Gather.__new__(Gather)
            piece.count, piece.order = self.count, list(order)
            axis = self.current.ndim + dim
            piece.current = lax.slice_in_dim(self.current, at, at + size, axis=axis)
            rows = self.count * piece.current.shape[-2]
            piece.shape = (rows, piece.current.shape[-1])
            pieces.append(piece)
            at += size
        return pieces

    def finish(self):
        while self.order:
            self.step()
        return self.current.reshape(self.shape)


def after(array, *others):
    return lax.optimization_barrier((array,) + others)[0]


class Scatter:
    def __init__(self, arrays, count, order, join=-1):
        self.count = count
        self.join = join
        self.order = list(order)
        self.shapes = [(array.shape[0] // count,) + array.shape[1:] for array in arrays]
        lead = (2,) * bits_of(count)
        self.currents = [array.reshape(lead + shape) for array, shape in zip(arrays, self.shapes)]
        self.sent = self.kept = self.received = None

    def send(self):
        if self.order:
            bit = self.order.pop(0)
            dim = bits_of(self.count) - 1 - bit
            mine = (lax.axis_index("dp") >> bit) & 1
            sent = [
                lax.dynamic_slice_in_dim(current, 1 - mine, 1, dim).astype(jnp.bfloat16)
                for current in self.currents
            ]
            self.sent = sent[0] if len(sent) == 1 else jnp.concatenate(sent, axis=self.join)
            self.kept = [
                lax.dynamic_slice_in_dim(current, mine, 1, dim) for current in self.currents
            ]
            self.received = swap(self.sent, "dp", self.count, bit)
        return self

    def take(self, *others):
        if self.received is not None:
            received = after(self.received, *others) if others else self.received
            currents, at = [], 0
            for kept in self.kept:
                size = kept.shape[self.join]
                piece = lax.slice_in_dim(received, at, at + size, axis=self.join % kept.ndim)
                currents.append(kept.astype(jnp.float32) + piece.astype(jnp.float32))
                at += size
            self.currents, self.received = currents, None
        return self

    def merge(self, *others, join=-1):
        every = (self,) + others
        merged = Scatter([], self.count, self.order, join)
        merged.shapes = [shape for one in every for shape in one.shapes]
        merged.currents = [current for one in every for current in one.take().currents]
        return merged

    def finish(self):
        self.take()
        while self.order:
            self.send().take()
        pairs = zip(self.currents, self.shapes)
        return [current.reshape(shape).astype(jnp.float32) for current, shape in pairs]


def sum_all(array, axis, count):
    bits = list(range(bits_of(count)))
    while bits:
        group, bits = bits[:2], bits[2:]
        near = array + swap(array, axis, count, group[0])
        if len(group) == 1:
            array = near
            continue
        masks = (1 << group[1], (1 << group[0]) | (1 << group[1]))
        far = [lax.ppermute(array, axis, [(i, i ^ mask) for i in range(count)]) for mask in masks]
        array = near + (far[0] + far[1])
    return array


def row_items(unit_pair, row_count, mark_count):
    position = lax.iota(jnp.int32, row_count)
    first_end = unit_pair[0] * mark_count
    second_end = first_end + unit_pair[1] * mark_count
    return jnp.where(position < first_end, 0, jnp.where(position < second_end, 1, 2)).astype(
        jnp.int32
    )


NEGATIVE = -1e30
SCORE_SCALE = 0.125
BLOCK = 128
CHUNK = 256


def dot_with(left, right, left_dim, right_dim):
    return lax.dot_general(
        left, right, (((left_dim,), (right_dim,)), ((), ())), preferred_element_type=jnp.float32
    )


def halves(array):
    high = array.astype(jnp.bfloat16)
    return high, (array - high.astype(jnp.float32)).astype(jnp.bfloat16)


def dot_fine(left, right, left_dim, right_dim):
    left_high, left_low = halves(left)
    right_high, right_low = halves(right)
    return dot_with(
        jnp.concatenate([left_high, left_high, left_low], axis=left_dim),
        jnp.concatenate([right_high, right_low, right_high], axis=right_dim),
        left_dim,
        right_dim,
    )


def dot_low(left, right, left_dim, right_dim):
    return dot_with(left.astype(jnp.bfloat16), right.astype(jnp.bfloat16), left_dim, right_dim)


def item_ends(units_ref):
    first_end = units_ref[0, 0] * LANDMARKS
    return first_end, first_end + units_ref[0, 1] * LANDMARKS


def lane_items(units_ref, row_count):
    first_end, second_end = item_ends(units_ref)
    position = lax.broadcasted_iota(jnp.int32, (1, row_count), 1)
    first = (position < first_end).astype(jnp.float32)
    inside = (position < second_end).astype(jnp.float32)
    return first, inside - first, inside


def landmark_columns(units_ref):
    first_end, second_end = item_ends(units_ref)
    mark = lax.broadcasted_iota(jnp.int32, (2 * LANDMARKS, 1), 0)
    is_first = mark < LANDMARKS
    units = jnp.where(is_first, units_ref[0, 0], units_ref[0, 1])
    start = jnp.where(is_first, 0, first_end)
    low = start + jnp.where(is_first, mark, mark - LANDMARKS) * units
    return is_first, start, jnp.where(is_first, first_end, second_end), low, low + units


def select_matrix(units_ref, row_count):
    _, _, _, low, high = landmark_columns(units_ref)
    position = lax.broadcasted_iota(jnp.int32, (2 * LANDMARKS, row_count), 1)
    return ((position >= low) & (position < high)).astype(jnp.float32).astype(jnp.bfloat16)


def inverse_units(units_ref):
    lane = lax.broadcasted_iota(jnp.int32, (1, 2 * LANDMARKS), 1)
    units = jnp.where(lane < LANDMARKS, units_ref[0, 0], units_ref[0, 1]).astype(jnp.float32)
    return 1.0 / units


def same_item(size):
    row = lax.broadcasted_iota(jnp.int32, (size, size), 0)
    column = lax.broadcasted_iota(jnp.int32, (size, size), 1)
    return (row < LANDMARKS) == (column < LANDMARKS)


def scaled_eye(size, value):
    row = lax.broadcasted_iota(jnp.int32, (size, size), 0)
    column = lax.broadcasted_iota(jnp.int32, (size, size), 1)
    return jnp.where(row == column, value, 0.0)


def column_peaks(matrix):
    sums = jnp.sum(matrix, axis=0, keepdims=True)
    lane = lax.broadcasted_iota(jnp.int32, sums.shape, 1)
    first = jnp.max(jnp.where(lane < LANDMARKS, sums, NEGATIVE), axis=1, keepdims=True)
    second = jnp.max(jnp.where(lane < LANDMARKS, NEGATIVE, sums), axis=1, keepdims=True)
    return sums, jnp.where(lane < LANDMARKS, first, second)


def fill_windows(window_ref, rows, first, second):
    row_count = rows.shape[1]
    lane = lax.broadcasted_iota(jnp.int32, (1, BLOCK), 1)
    before = (lane >= BLOCK - 16).astype(jnp.float32).astype(jnp.bfloat16)
    behind = (lane < 16).astype(jnp.float32).astype(jnp.bfloat16)
    block_count = row_count // BLOCK
    for item, mask in ((0, first), (1, second)):
        kept = rows * mask.astype(jnp.bfloat16)
        for block in range(block_count):
            at = block * BLOCK
            edge = jnp.zeros((rows.shape[0], BLOCK), jnp.bfloat16)
            if block > 0:
                edge = edge + kept[:, at - BLOCK : at] * before
            if block + 1 < block_count:
                edge = edge + kept[:, at + BLOCK : at + 2 * BLOCK] * behind
            base = (2 * block + item) * HEAD_DIM
            window_ref[base : base + HEAD_DIM, :BLOCK] = kept[:, at : at + BLOCK]
            window_ref[base : base + HEAD_DIM, BLOCK:] = edge


def tap_matrix(tap_row):
    return pltpu.roll(
        jnp.broadcast_to(tap_row, (BLOCK, 2 * BLOCK)), 0, axis=1, stride=1, stride_axis=0
    ).astype(jnp.bfloat16)


def attention_start_body(
    units_ref,
    proj_ref,
    marks_ref,
    middle_ref,
    last_ref,
    values_ref,
    approx_ref,
    select_ref,
    in_ref,
):
    parts, _, part_width, row_count = proj_ref.shape
    part_heads = part_width // HEAD_DIM
    heads = parts * part_heads
    marks = 2 * LANDMARKS
    select_ref[...] = select_matrix(units_ref, row_count)
    _, start, end, _, _ = landmark_columns(units_ref)
    position = lax.broadcasted_iota(jnp.int32, (marks, row_count), 1)
    in_ref[...] = jnp.where((position >= start) & (position < end), 0.0, NEGATIVE)
    for part in range(parts):
        for kind in range(2):
            sums = dot_with(proj_ref[part, kind], select_ref[...], 1, 1)
            rows = slice(part * part_width, (part + 1) * part_width)
            marks_ref[kind, rows] = sums * inverse_units(units_ref)
    same = same_item(marks)

    def head_start(head, carry):
        at = pl.multiple_of(head * HEAD_DIM, HEAD_DIM)
        part = head // part_heads
        part_at = pl.multiple_of((head - part * part_heads) * HEAD_DIM, HEAD_DIM)
        mark_query = marks_ref[0, pl.ds(at, HEAD_DIM), :]
        mark_key = marks_ref[1, pl.ds(at, HEAD_DIM), :]
        logits = dot_fine(mark_query, mark_key, 0, 0) * SCORE_SCALE
        logits = jnp.where(same, logits, NEGATIVE)
        raised = jnp.exp(logits - jnp.max(logits, axis=1, keepdims=True))
        middle = raised / jnp.sum(raised, axis=1, keepdims=True)
        middle_ref[head] = middle
        _, peak = column_peaks(middle)
        approx_ref[head] = middle.T / peak
        query_rows = (mark_query * SCORE_SCALE).T.astype(jnp.bfloat16)
        scores = dot_with(query_rows, proj_ref[part, 1, pl.ds(part_at, HEAD_DIM), :], 1, 0) + in_ref[...]
        raised = jnp.exp(scores - jnp.max(scores, axis=1, keepdims=True))
        scale = 1.0 / jnp.sum(raised, axis=1, keepdims=True)
        last = (raised * scale).astype(jnp.bfloat16)
        last_ref[head] = last
        values_ref[head] = dot_with(last, proj_ref[part, 2, pl.ds(part_at, HEAD_DIM), :], 1, 1)
        return carry

    lax.fori_loop(0, heads, head_start, 0, unroll=2)


def attention_finish_body(
    units_ref,
    proj_ref,
    taps_ref,
    marks_ref,
    middle_ref,
    values_ref,
    approx_ref,
    attended_ref,
    first_ref,
    rough_ref,
    fine_ref,
    weighted_ref,
    own_ref,
    state_ref,
    window_ref,
    conv_ref,
):
    parts, _, part_width, row_count = proj_ref.shape
    part_heads = part_width // HEAD_DIM
    heads = parts * part_heads
    marks = 2 * LANDMARKS
    is_first = landmark_columns(units_ref)[0]
    first_end, _ = item_ends(units_ref)
    position = lax.broadcasted_iota(jnp.int32, (marks, row_count), 1)
    own_ref[...] = jnp.where((position < first_end) == is_first, 0.0, NEGATIVE)
    first, second, inside = lane_items(units_ref, row_count)
    state_ref[...] = approx_ref[...]
    seven, fifteen, thirteen = (scaled_eye(marks, value) for value in (7.0, 15.0, 13.0))

    def pinv_steps(saved_ref, count):
        kind = saved_ref.dtype

        def one_step(slot, carry):
            approx = [state_ref[head] for head in range(heads)]
            product = [dot_fine(middle_ref[head], approx[head], 1, 0) for head in range(heads)]
            inner = [
                fifteen - dot_fine(product[head], seven - product[head], 1, 0)
                for head in range(heads)
            ]
            outer = [thirteen - dot_fine(product[head], inner[head], 1, 0) for head in range(heads)]
            for head in range(heads):
                saved_ref[slot, 0, head] = approx[head].astype(kind)
                saved_ref[slot, 1, head] = product[head].astype(kind)
                saved_ref[slot, 2, head] = inner[head].astype(kind)
                saved_ref[slot, 3, head] = outer[head].astype(kind)
                state_ref[head] = dot_fine(0.25 * approx[head], outer[head], 1, 0)
            return carry

        lax.fori_loop(0, count, one_step, 0)

    pinv_steps(rough_ref, ROUGH_STEPS)
    pinv_steps(fine_ref, PINV_STEPS - ROUGH_STEPS)

    def head_end(head, carry):
        at = pl.multiple_of(head * HEAD_DIM, HEAD_DIM)
        part = head // part_heads
        part_at = pl.multiple_of((head - part * part_heads) * HEAD_DIM, HEAD_DIM)
        weighted = dot_fine(state_ref[head], values_ref[head], 1, 0)
        weighted_ref[head] = weighted
        weighted_rows = weighted.T.astype(jnp.bfloat16)
        key_rows = (marks_ref[1, pl.ds(at, HEAD_DIM), :] * SCORE_SCALE).T.astype(jnp.bfloat16)
        values = proj_ref[part, 2, pl.ds(part_at, HEAD_DIM), :]
        fill_windows(window_ref, values, first, second)
        conv_ref[...] = dot_with(window_ref[...], tap_matrix(taps_ref[pl.ds(head, 1), :]), 1, 1)
        for chunk in range(row_count // CHUNK):
            lanes = slice(chunk * CHUNK, (chunk + 1) * CHUNK)
            query = proj_ref[part, 0, pl.ds(part_at, HEAD_DIM), lanes]
            scores = dot_with(key_rows, query, 1, 0) + own_ref[:, lanes]
            raised = jnp.exp(scores - jnp.max(scores, axis=0, keepdims=True))
            scale = 1.0 / jnp.sum(raised, axis=0, keepdims=True)
            kept = (raised * scale).astype(jnp.bfloat16)
            first_ref[head, :, lanes] = kept
            mixed = dot_with(weighted_rows, kept, 1, 0) * inside[:, lanes]
            for piece in range(CHUNK // BLOCK):
                block = chunk * (CHUNK // BLOCK) + piece
                base = 2 * block * HEAD_DIM
                columns = slice(block * BLOCK, (block + 1) * BLOCK)
                conv = (
                    conv_ref[base : base + HEAD_DIM] * first[:, columns]
                    + conv_ref[base + HEAD_DIM : base + 2 * HEAD_DIM] * second[:, columns]
                )
                attended_ref[pl.ds(at, HEAD_DIM), columns] = (
                    mixed[:, piece * BLOCK : (piece + 1) * BLOCK] + conv
                ).astype(jnp.bfloat16)
        return carry

    lax.fori_loop(0, heads, head_end, 0, unroll=2)


def whole(count):
    return [pl.BlockSpec(memory_space=pltpu.VMEM)] * count


def attention_sizes(proj):
    parts, _, part_width, row_count = proj.shape
    width = parts * part_width
    heads = width // HEAD_DIM
    marks = 2 * LANDMARKS
    return width, row_count, heads, marks, (heads, marks, marks), (heads, marks, HEAD_DIM)


def attention_start(item_units, proj):
    width, row_count, heads, marks, square, thin = attention_sizes(proj)
    return pl.pallas_call(
        attention_start_body,
        in_specs=[pl.BlockSpec(memory_space=pltpu.SMEM)]
        + whole(1),
        out_specs=whole(5),
        out_shape=[
            jax.ShapeDtypeStruct((2, width, marks), jnp.float32),
            jax.ShapeDtypeStruct(square, jnp.float32),
            jax.ShapeDtypeStruct((heads, marks, row_count), jnp.bfloat16),
            jax.ShapeDtypeStruct(thin, jnp.float32),
            jax.ShapeDtypeStruct(square, jnp.float32),
        ],
        scratch_shapes=[
            pltpu.VMEM((marks, row_count), jnp.bfloat16),
            pltpu.VMEM((marks, row_count), jnp.float32),
        ],
        compiler_params=pltpu.CompilerParams(vmem_limit_bytes=48 * 1024 * 1024),
        cost_estimate=pl.CostEstimate(
            flops=9_000_000_000, bytes_accessed=8_000_000, transcendentals=0
        ),
    )(item_units, proj)


def attention_finish(item_units, proj, tap_rows, marks_rows, middle, last, values, approx):
    width, row_count, heads, marks, square, thin = attention_sizes(proj)
    stacked = 2 * row_count // BLOCK * HEAD_DIM
    return pl.pallas_call(
        attention_finish_body,
        in_specs=[pl.BlockSpec(memory_space=pltpu.SMEM)] + whole(6),
        out_specs=whole(5),
        out_shape=[
            jax.ShapeDtypeStruct((width, row_count), jnp.bfloat16),
            jax.ShapeDtypeStruct((heads, marks, row_count), jnp.bfloat16),
            jax.ShapeDtypeStruct((ROUGH_STEPS, 4) + square, jnp.bfloat16),
            jax.ShapeDtypeStruct((PINV_STEPS - ROUGH_STEPS, 4) + square, jnp.float32),
            jax.ShapeDtypeStruct(thin, jnp.float32),
        ],
        scratch_shapes=[
            pltpu.VMEM((marks, row_count), jnp.float32),
            pltpu.VMEM(square, jnp.float32),
            pltpu.VMEM((stacked, 2 * BLOCK), jnp.bfloat16),
            pltpu.VMEM((stacked, BLOCK), jnp.float32),
        ],
        compiler_params=pltpu.CompilerParams(vmem_limit_bytes=48 * 1024 * 1024),
        cost_estimate=pl.CostEstimate(
            flops=18_000_000_000, bytes_accessed=16_000_000, transcendentals=0
        ),
    )(item_units, proj, tap_rows, marks_rows, middle, values, approx)


def tap_rows_of(kernel):
    half = kernel.shape[1] // 2
    gap = jnp.zeros((kernel.shape[0], 2 * BLOCK - kernel.shape[1]), jnp.float32)
    return jnp.concatenate([kernel[:, half:], gap, kernel[:, :half]], axis=1)

def attention_backward_body(
    units_ref,
    proj_ref,
    taps_ref,
    grad_ref,
    first_ref,
    last_ref,
    marks_ref,
    middle_ref,
    rough_ref,
    fine_ref,
    values_ref,
    weighted_ref,
    out_ref,
    kernel_ref,
    select_ref,
    d_first_ref,
    d_last_ref,
    d_marks_ref,
    d_weighted_ref,
    d_values_ref,
    d_approx_ref,
    d_middle_ref,
    window_ref,
    d_window_ref,
    conv_ref,
):
    width = proj_ref.shape[1]
    row_count = proj_ref.shape[2]
    heads = width // HEAD_DIM
    marks = 2 * LANDMARKS
    select_ref[...] = select_matrix(units_ref, row_count)
    first, second, _ = lane_items(units_ref, row_count)
    inverse = inverse_units(units_ref)
    same = same_item(marks)
    chunks = [slice(at, at + CHUNK) for at in range(0, row_count, CHUNK)]

    def head_start(head, carry):
        at = pl.multiple_of(head * HEAD_DIM, HEAD_DIM)
        weighted_low = weighted_ref[head].astype(jnp.bfloat16)
        for lanes in chunks:
            kept = first_ref[head, :, lanes].astype(jnp.float32)
            d_kept = dot_with(weighted_low, grad_ref[pl.ds(at, HEAD_DIM), lanes], 1, 0)
            scaled = kept * d_kept
            d_scores = scaled - kept * jnp.sum(scaled, axis=0, keepdims=True)
            d_first_ref[head, :, lanes] = d_scores.astype(jnp.bfloat16)
        d_weighted = dot_with(first_ref[head], grad_ref[pl.ds(at, HEAD_DIM), :], 1, 1)
        d_weighted_ref[head] = d_weighted
        d_marks_ref[1, pl.ds(at, HEAD_DIM), :] = SCORE_SCALE * dot_with(
            proj_ref[0, pl.ds(at, HEAD_DIM), :], d_first_ref[head], 1, 1
        )
        d_approx = dot_fine(d_weighted, values_ref[head], 1, 1)
        d_approx_ref[head] = jnp.where(same, d_approx, 0.0)
        inverse_last = dot_fine(
            0.25 * fine_ref[PINV_STEPS - ROUGH_STEPS - 1, 0, head],
            fine_ref[PINV_STEPS - ROUGH_STEPS - 1, 3, head],
            1,
            0,
        )
        d_values_ref[head] = dot_fine(inverse_last, d_weighted, 0, 0)
        d_middle_ref[head] = jnp.zeros((marks, marks), jnp.float32)
        return carry

    lax.fori_loop(0, heads, head_start, 0, unroll=2)

    seven = scaled_eye(marks, 7.0)
    every = range(heads)

    def pinv_steps(saved_ref, count, dot):
        def one_step(step, carry):
            slot = count - 1 - step
            d_next = [d_approx_ref[head] for head in every]
            d_outer = [0.25 * dot(saved_ref[slot, 0, head], d_next[head], 0, 0) for head in every]
            d_inner = [-dot(saved_ref[slot, 1, head], d_outer[head], 0, 0) for head in every]
            d_lowest = [-dot(saved_ref[slot, 1, head], d_inner[head], 0, 0) for head in every]
            for head in every:
                product = saved_ref[slot, 1, head].astype(jnp.float32)
                d_product = (
                    -dot(d_outer[head], saved_ref[slot, 2, head], 1, 1)
                    - dot(d_inner[head], seven - product, 1, 1)
                    - d_lowest[head]
                )
                d_middle_ref[head] += dot(d_product, saved_ref[slot, 0, head], 1, 1)
                d_approx_ref[head] = 0.25 * dot(d_next[head], saved_ref[slot, 3, head], 1, 1) + dot(
                    middle_ref[head], d_product, 0, 0
                )
            return carry

        lax.fori_loop(0, count, one_step, 0)

    pinv_steps(fine_ref, PINV_STEPS - ROUGH_STEPS, dot_fine)
    pinv_steps(rough_ref, ROUGH_STEPS, dot_low)

    lane = lax.broadcasted_iota(jnp.int32, (1, marks), 1)

    def item_sums(row):
        total = jnp.sum(row, axis=1, keepdims=True)
        start = jnp.sum(jnp.where(lane < LANDMARKS, row, 0.0), axis=1, keepdims=True)
        return jnp.where(lane < LANDMARKS, start, total - start)

    def head_middle(head, carry):
        at = pl.multiple_of(head * HEAD_DIM, HEAD_DIM)
        middle = middle_ref[head]
        sums, peak = column_peaks(middle)
        d_start = d_approx_ref[head]
        d_start_turned = (d_start / peak).T
        d_peak = -item_sums(jnp.sum(d_start_turned * middle, axis=0, keepdims=True)) / peak
        at_peak = (sums == peak).astype(jnp.float32)
        d_column = at_peak * d_peak / item_sums(at_peak)
        d_middle = d_middle_ref[head] + d_start_turned + jnp.where(same, d_column, 0.0)
        scaled = middle * d_middle
        d_logits = SCORE_SCALE * (scaled - middle * jnp.sum(scaled, axis=1, keepdims=True))
        rows = pl.ds(at, HEAD_DIM)
        d_marks_ref[0, rows, :] = dot_fine(marks_ref[1, rows, :], d_logits, 1, 1)
        d_marks_ref[1, rows, :] += dot_fine(marks_ref[0, rows, :], d_logits, 1, 0)
        return carry

    lax.fori_loop(0, heads, head_middle, 0, unroll=2)

    row_index = lax.broadcasted_iota(jnp.int32, (BLOCK, BLOCK), 0)
    column_index = lax.broadcasted_iota(jnp.int32, (BLOCK, BLOCK), 1)
    turn = jnp.where(row_index + column_index == BLOCK - 1, 1.0, 0.0).astype(jnp.bfloat16)

    def head_end(head, carry):
        at = pl.multiple_of(head * HEAD_DIM, HEAD_DIM)
        rows = pl.ds(at, HEAD_DIM)
        d_values = d_values_ref[head]
        d_values_low = d_values.astype(jnp.bfloat16)
        d_values_turned = d_values.T.astype(jnp.bfloat16)
        inner = jnp.sum(d_values * values_ref[head], axis=1, keepdims=True)
        for lanes in chunks:
            d_kept = dot_with(d_values_low, proj_ref[2, rows, lanes], 1, 0)
            d_scores = last_ref[head, :, lanes].astype(jnp.float32) * (d_kept - inner)
            d_last_ref[:, lanes] = d_scores.astype(jnp.bfloat16)
        d_query = d_marks_ref[0, rows, :] + SCORE_SCALE * dot_with(
            proj_ref[1, rows, :], d_last_ref[...], 1, 1
        )
        d_query_low = (d_query * inverse).astype(jnp.bfloat16)
        d_key_low = (d_marks_ref[1, rows, :] * inverse).astype(jnp.bfloat16)
        mark_query = (marks_ref[0, rows, :] * SCORE_SCALE).astype(jnp.bfloat16)
        mark_key = (marks_ref[1, rows, :] * SCORE_SCALE).astype(jnp.bfloat16)
        fill_windows(window_ref, proj_ref[2, rows, :], first, second)
        fill_windows(d_window_ref, grad_ref[rows, :], first, second)
        conv_ref[...] = dot_with(d_window_ref[...], tap_matrix(taps_ref[pl.ds(head, 1), :]), 1, 1)
        joined = dot_with(d_window_ref[:, :BLOCK], window_ref[...], 0, 0)
        joined_high, joined_low = halves(joined)
        joined = dot_with(
            jnp.concatenate([turn, turn], axis=1),
            jnp.concatenate([joined_high, joined_low], axis=0),
            1,
            0,
        )
        joined = pltpu.roll(joined, BLOCK + 1, axis=1, stride=1, stride_axis=0)
        kernel_ref[pl.ds(head, 1), :] = jnp.sum(joined, axis=0, keepdims=True)
        for index, lanes in enumerate(chunks):
            select = select_ref[:, lanes]
            out_ref[rows, lanes] = (
                dot_with(mark_key, d_first_ref[head, :, lanes], 1, 0)
                + dot_with(d_query_low, select, 1, 0)
            ).astype(jnp.bfloat16)
            out_ref[pl.ds(width + at, HEAD_DIM), lanes] = (
                dot_with(mark_query, d_last_ref[:, lanes], 1, 0) + dot_with(d_key_low, select, 1, 0)
            ).astype(jnp.bfloat16)
            d_value = dot_with(d_values_turned, last_ref[head, :, lanes], 1, 0)
            for part in range(CHUNK // BLOCK):
                block = index * (CHUNK // BLOCK) + part
                base = 2 * block * HEAD_DIM
                columns = slice(block * BLOCK, (block + 1) * BLOCK)
                conv = (
                    conv_ref[base : base + HEAD_DIM] * first[:, columns]
                    + conv_ref[base + HEAD_DIM : base + 2 * HEAD_DIM] * second[:, columns]
                )
                out_ref[pl.ds(2 * width + at, HEAD_DIM), columns] = (
                    d_value[:, part * BLOCK : (part + 1) * BLOCK] + conv
                ).astype(jnp.bfloat16)
        return carry

    lax.fori_loop(0, heads, head_end, 0, unroll=2)


def attention_backward(item_units, proj, tap_rows, grad, *saved, part):
    parts, _, width, row_count = proj.shape
    heads = width // HEAD_DIM
    marks = 2 * LANDMARKS
    square = (heads, marks, marks)
    thin = (heads, marks, HEAD_DIM)
    stacked = 2 * row_count // BLOCK * HEAD_DIM

    def block(shape, split):
        place = tuple(part if dim == split else 0 for dim in range(len(shape)))
        sizes = tuple(size // parts if dim == split else size for dim, size in enumerate(shape))
        sizes = (None,) + sizes[1:] if len(shape) == 4 and split == 0 else sizes
        return pl.BlockSpec(sizes, lambda step: place, pipeline_mode=pl.Buffered(1))

    splits = (0, None, 0, 0, 0, 1, 0, 2, 2, 0, 0)
    tap_rows = tap_rows[part * heads : (part + 1) * heads]
    arrays = (proj, tap_rows, grad) + saved
    out, joined = pl.pallas_call(
        attention_backward_body,
        grid=(1,),
        in_specs=[pl.BlockSpec(memory_space=pltpu.SMEM)]
        + [block(array.shape, split) for array, split in zip(arrays, splits)],
        out_specs=[
            pl.BlockSpec((3 * width, row_count), lambda step: (0, 0)),
            pl.BlockSpec((heads, 2 * BLOCK), lambda step: (0, 0)),
        ],
        out_shape=[
            jax.ShapeDtypeStruct((3 * width, row_count), jnp.bfloat16),
            jax.ShapeDtypeStruct((heads, 2 * BLOCK), jnp.float32),
        ],
        scratch_shapes=[
            pltpu.VMEM((marks, row_count), jnp.bfloat16),
            pltpu.VMEM((heads, marks, row_count), jnp.bfloat16),
            pltpu.VMEM((marks, row_count), jnp.bfloat16),
            pltpu.VMEM((2, width, marks), jnp.float32),
            pltpu.VMEM(thin, jnp.float32),
            pltpu.VMEM(thin, jnp.float32),
            pltpu.VMEM(square, jnp.float32),
            pltpu.VMEM(square, jnp.float32),
            pltpu.VMEM((stacked, 2 * BLOCK), jnp.bfloat16),
            pltpu.VMEM((stacked, 2 * BLOCK), jnp.bfloat16),
            pltpu.VMEM((stacked, BLOCK), jnp.float32),
        ],
        compiler_params=pltpu.CompilerParams(vmem_limit_bytes=48 * 1024 * 1024),
        cost_estimate=pl.CostEstimate(
            flops=30_000_000_000 // parts, bytes_accessed=20_000_000 // parts, transcendentals=0
        ),
    )(item_units, *arrays)
    half = TAPS // 2
    return out, jnp.concatenate([joined[:, 2 * BLOCK - half :], joined[:, : TAPS - half]], axis=1)


ROWS = 512
LONG_ROWS = 512
OUTER = 384
PIECE = 512
SUB = 512
GELU_SCALE = 0.7978845608
GELU_CUBE = 0.044715


def row_block(width, rows=ROWS):
    return pl.BlockSpec((rows, width), lambda step: (step, 0))


def fixed_block(shape, column=0):
    return pl.BlockSpec(shape, lambda step: (0, column))


def row_lanes(rows=ROWS):
    return pl.BlockSpec((1, rows), lambda step: (0, step))


def as_column(row):
    return jnp.broadcast_to(row, (128, row.shape[1])).T[:, 0:1]


def as_row(column):
    return jnp.broadcast_to(column, (column.shape[0], 128)).T[0:1]


def dense_params():
    return pltpu.CompilerParams(vmem_limit_bytes=56 * 1024 * 1024)


def cost(flops, size):
    return pl.CostEstimate(flops=flops, bytes_accessed=size, transcendentals=0)


def normalized(rows):
    center = rows - jnp.mean(rows, axis=-1, keepdims=True)
    spread = jnp.mean(center * center, axis=-1, keepdims=True)
    scale = lax.rsqrt(spread + NORM_EPS)
    return center * scale, scale


def norm_backward(grad, gain, unit, scale):
    scaled = grad * gain
    lean = jnp.mean(scaled * unit, axis=-1, keepdims=True)
    return scale * (scaled - jnp.mean(scaled, axis=-1, keepdims=True) - unit * lean)


def column_sum(rows):
    return jnp.sum(rows, axis=0, keepdims=True)


def both(own_ref, other_ref, rows=...):
    return own_ref[rows].astype(jnp.float32) + other_ref[rows].astype(jnp.float32)


def gelu_parts(expanded):
    square = expanded * expanded
    bend = jnp.tanh(expanded * (GELU_SCALE + (GELU_SCALE * GELU_CUBE) * square))
    return square, 0.5 + 0.5 * bend, bend


def weight_blocks(expand, reduce):
    return [fixed_block(reduce.shape), fixed_block(reduce.shape)]


def hidden_forward_body(
    own_ref,
    other_ref,
    tokens_ref,
    weight_ref,
    shared_ref,
    bias_ref,
    expand_ref,
    reduce_ref,
    part_ref,
    low_ref,
    unit_ref,
    scale_ref,
    wide_ref,
    stat_ref,
):
    @pl.when(pl.program_id(0) == 0)
    def _():
        stat_ref[...] = jnp.zeros_like(stat_ref)

    weight_column = as_column(weight_ref[...])
    row_slices = [slice(at, at + SUB) for at in range(0, ROWS, SUB)]
    lows, scales, squares = [], [], []
    for rows in row_slices:
        branch = both(own_ref, other_ref, rows) + shared_ref[0:1]
        squares.append(column_sum(weight_column[rows] * branch * branch))
        unit, scale = normalized(tokens_ref[rows].astype(jnp.float32) + branch)
        hidden = unit * shared_ref[2:3] + shared_ref[3:4]
        unit_ref[rows] = unit.astype(jnp.bfloat16)
        scales.append(scale)
        hidden_low = hidden.astype(jnp.bfloat16)
        low_ref[rows] = hidden_low
        total = jnp.zeros((SUB, part_ref.shape[1]), jnp.float32)
        for at in range(0, reduce_ref.shape[1], PIECE):
            lanes = slice(at, at + PIECE)
            expanded = dot_with(hidden_low, expand_ref[:, lanes], 1, 0) + bias_ref[:, lanes]
            wide_ref[rows, lanes] = expanded.astype(jnp.bfloat16)
            half = gelu_parts(expanded)[1]
            active = (expanded * half).astype(jnp.bfloat16)
            total += dot_with(active, reduce_ref[:, lanes], 1, 1)
        part_ref[rows] = total.astype(jnp.bfloat16)
    stat_ref[...] += sum(squares)
    scale_ref[...] = as_row(jnp.concatenate(scales, axis=0))


def hidden_forward(own, other, tokens, weight_row, shared_rows, expand_bias, *weights):
    row_count, width = tokens.shape
    units = expand_bias.shape[1]
    return pl.pallas_call(
        hidden_forward_body,
        grid=(row_count // ROWS,),
        in_specs=[
            row_block(width),
            row_block(width),
            row_block(width),
            row_lanes(),
            fixed_block((6, width)),
            fixed_block((1, units)),
        ]
        + weight_blocks(*weights),
        out_specs=[
            row_block(width),
            row_block(width),
            row_block(width),
            row_lanes(),
            row_block(units),
            fixed_block((1, width)),
        ],
        out_shape=[
            jax.ShapeDtypeStruct((row_count, width), jnp.bfloat16),
            jax.ShapeDtypeStruct((row_count, width), jnp.bfloat16),
            jax.ShapeDtypeStruct((row_count, width), jnp.bfloat16),
            jax.ShapeDtypeStruct((1, row_count), jnp.float32),
            jax.ShapeDtypeStruct((row_count, units), jnp.bfloat16),
            jax.ShapeDtypeStruct((1, width), jnp.float32),
        ],
        compiler_params=dense_params(),
        cost_estimate=cost(4 * row_count * width * units, 30_000_000),
    )(own, other, tokens, weight_row, shared_rows, expand_bias, *weights)


def hidden_backward_body(
    own_ref,
    other_ref,
    low_ref,
    cotangent_ref,
    weight_ref,
    shared_ref,
    wide_ref,
    expand_ref,
    reduce_ref,
    output_ref,
    d_two_ref,
    reduce_out,
    expand_out,
    part_ref,
    sums_ref,
    bias_ref,
    reduce_sum,
    expand_sum,
):
    @pl.when(pl.program_id(0) == 0)
    def _():
        sums_ref[...] = jnp.zeros_like(sums_ref)
        bias_ref[...] = jnp.zeros_like(bias_ref)
        reduce_sum[...] = jnp.zeros_like(reduce_sum)
        expand_sum[...] = jnp.zeros_like(expand_sum)

    weight_column = as_column(weight_ref[...])
    for start in range(0, ROWS, SUB):
        rows = slice(start, start + SUB)
        branch = both(own_ref, other_ref, rows) + shared_ref[1:2]
        weight = weight_column[rows]
        unit, scale = normalized(low_ref[rows].astype(jnp.float32) + branch)
        output_ref[rows] = unit * shared_ref[4:5] + shared_ref[5:6]
        grad = cotangent_ref[rows].astype(jnp.float32) * weight
        d_res = norm_backward(grad, shared_ref[4:5], unit, scale)
        d_two = d_res.astype(jnp.bfloat16)
        d_two_ref[rows] = d_two
        d_two_turned = d_res.T.astype(jnp.bfloat16)
        low_turned = low_ref[rows].astype(jnp.float32).T.astype(jnp.bfloat16)
        sums_ref[...] += jnp.concatenate(
            [
                column_sum(weight * branch * branch),
                column_sum(d_res),
                column_sum(grad * unit),
                column_sum(grad),
                jnp.broadcast_to(column_sum(weight), (1, grad.shape[1])),
                jnp.zeros((3, grad.shape[1]), jnp.float32),
            ],
            axis=0,
        )
        total = jnp.zeros((SUB, part_ref.shape[1]), jnp.float32)
        for at in range(0, reduce_ref.shape[1], PIECE):
            lanes = slice(at, at + PIECE)
            d_active = dot_with(d_two, reduce_ref[:, lanes], 1, 0)
            expanded = wide_ref[rows, lanes].astype(jnp.float32)
            square, half, bend = gelu_parts(expanded)
            active = (expanded * half).astype(jnp.bfloat16)
            slope = half + (0.5 * expanded) * (1.0 - bend * bend) * (
                GELU_SCALE + (3.0 * GELU_SCALE * GELU_CUBE) * square
            )
            d_expanded = (slope * d_active).astype(jnp.bfloat16)
            reduce_sum[:, lanes] += dot_with(d_two_turned, active, 1, 0)
            expand_sum[:, lanes] += dot_with(low_turned, d_expanded, 1, 0)
            bias_ref[:, lanes] += column_sum(d_expanded.astype(jnp.float32))
            total += dot_with(d_expanded, expand_ref[:, lanes], 1, 1)
        part_ref[rows] = total.astype(jnp.bfloat16)

    @pl.when(pl.program_id(0) == pl.num_programs(0) - 1)
    def _():
        reduce_out[...] = reduce_sum[...].astype(jnp.bfloat16)
        expand_out[...] = expand_sum[...].astype(jnp.bfloat16)


def hidden_backward(own, other, low, cotangent, weight_row, shared_rows, wide, *weights):
    row_count, width = cotangent.shape
    units = wide.shape[1]
    return pl.pallas_call(
        hidden_backward_body,
        grid=(row_count // ROWS,),
        in_specs=[
            row_block(width),
            row_block(width),
            row_block(width),
            row_block(width),
            row_lanes(),
            fixed_block((6, width)),
            row_block(units),
        ]
        + weight_blocks(*weights),
        out_specs=[
            row_block(width),
            row_block(width),
            fixed_block((width, units)),
            fixed_block((width, units)),
            row_block(width),
            fixed_block((8, width)),
            fixed_block((1, units)),
        ],
        out_shape=[
            jax.ShapeDtypeStruct((row_count, width), jnp.float32),
            jax.ShapeDtypeStruct((row_count, width), jnp.bfloat16),
            jax.ShapeDtypeStruct((width, units), jnp.bfloat16),
            jax.ShapeDtypeStruct((width, units), jnp.bfloat16),
            jax.ShapeDtypeStruct((row_count, width), jnp.bfloat16),
            jax.ShapeDtypeStruct((8, width), jnp.float32),
            jax.ShapeDtypeStruct((1, units), jnp.float32),
        ],
        scratch_shapes=[pltpu.VMEM((width, units), jnp.float32)] * 2,
        compiler_params=dense_params(),
        cost_estimate=cost(4 * row_count * width * units, 30_000_000),
    )(own, other, low, cotangent, weight_row, shared_rows, wide, *weights)


def norm_one_body(
    own_ref,
    other_ref,
    d_two_ref,
    unit_ref,
    scale_ref,
    inside_ref,
    shared_ref,
    mixing_ref,
    d_one_ref,
    d_mixed_ref,
    sums_ref,
    turned_ref,
):
    @pl.when(pl.program_id(0) == 0)
    def _():
        sums_ref[...] = jnp.zeros_like(sums_ref)
        turned_ref[...] = mixing_ref[...].astype(jnp.float32).T.astype(jnp.bfloat16)

    grad = both(own_ref, other_ref) + d_two_ref[...].astype(jnp.float32)
    unit = unit_ref[...].astype(jnp.float32)
    d_res = norm_backward(grad, shared_ref[2:3], unit, as_column(scale_ref[...]))
    d_one = d_res.astype(jnp.bfloat16)
    d_one_ref[...] = d_one
    sums_ref[...] += jnp.concatenate(
        [
            column_sum(d_res),
            column_sum(grad * unit),
            column_sum(grad),
            jnp.zeros((5, grad.shape[1]), jnp.float32),
        ],
        axis=0,
    )
    d_mixed = dot_with(turned_ref[...], d_one, 1, 1) * inside_ref[...]
    d_mixed_ref[...] = d_mixed.astype(jnp.bfloat16)


def norm_one_backward(own, other, d_two, unit, scale, inside_row, shared_rows, late_full, local_width):
    row_count, width = d_two.shape
    return pl.pallas_call(
        norm_one_body,
        grid=(row_count // LONG_ROWS,),
        in_specs=[
            row_block(width, LONG_ROWS),
            row_block(width, LONG_ROWS),
            row_block(width, LONG_ROWS),
            row_block(width, LONG_ROWS),
            row_lanes(LONG_ROWS),
            pl.BlockSpec((1, LONG_ROWS), lambda step: (0, step)),
            fixed_block((6, width)),
            fixed_block((width, local_width), late_full.shape[1] // local_width - 1),
        ],
        out_specs=[
            row_block(width, LONG_ROWS),
            pl.BlockSpec((local_width, LONG_ROWS), lambda step: (0, step)),
            fixed_block((8, width)),
        ],
        out_shape=[
            jax.ShapeDtypeStruct((row_count, width), jnp.bfloat16),
            jax.ShapeDtypeStruct((local_width, row_count), jnp.bfloat16),
            jax.ShapeDtypeStruct((8, width), jnp.float32),
        ],
        scratch_shapes=[pltpu.VMEM((local_width, width), jnp.bfloat16)],
        compiler_params=dense_params(),
        cost_estimate=cost(2 * row_count * width * local_width, 14_000_000),
    )(own, other, d_two, unit, scale, inside_row, shared_rows, late_full)


def turned_dot_body(*refs):
    *pairs, out_ref = refs
    total = jnp.zeros(out_ref.shape, jnp.float32)
    for at in range(0, len(pairs), 2):
        left = pairs[at][...]
        left = left.reshape(-1, left.shape[-1])
        total += dot_with(left, pairs[at + 1][...], 0, 1)
    out_ref[...] = total.astype(jnp.bfloat16)


def turned_dot(lefts, rights, columns, width):
    row_count = lefts[0].shape[-1]
    specs, arrays, terms = [], [], 0
    for left, right, column in zip(lefts, rights, columns):
        shape = left.shape[:-1] + (LONG_ROWS,)
        place = (0,) * (left.ndim - 1)
        specs.append(pl.BlockSpec(shape, lambda step, place=place: place + (step,)))
        depth = left.size // row_count
        specs.append(fixed_block((width, depth), column))
        arrays += [left, right]
        terms += depth
    return pl.pallas_call(
        turned_dot_body,
        grid=(row_count // LONG_ROWS,),
        in_specs=specs,
        out_specs=row_block(width, LONG_ROWS),
        out_shape=jax.ShapeDtypeStruct((row_count, width), jnp.bfloat16),
        compiler_params=dense_params(),
        cost_estimate=cost(2 * row_count * width * terms, 8_000_000),
    )(*arrays)

def turned_outer_body(left_ref, right_ref, out_ref):
    product = dot_with(left_ref[...], right_ref[...], 1, 0)
    out_ref[...] = product.T.astype(jnp.bfloat16)


def turned_outer(left, right):
    depth, width = right.shape
    return pl.pallas_call(
        turned_outer_body,
        grid=(width // OUTER,),
        in_specs=[
            fixed_block(left.shape),
            pl.BlockSpec((depth, OUTER), lambda step: (0, step)),
        ],
        out_specs=pl.BlockSpec((OUTER, left.shape[0]), lambda step: (step, 0)),
        out_shape=jax.ShapeDtypeStruct((width, left.shape[0]), jnp.bfloat16),
        compiler_params=dense_params(),
        cost_estimate=cost(2 * depth * width * left.shape[0], 6_000_000),
    )(left, right)


def project_body(first_ref, second_ref, tokens_ref, bias_ref, out_ref, turned_ref):
    part_width = first_ref.shape[1]

    @pl.when(pl.program_id(0) == 0)
    def _():
        for part, weight_ref in enumerate((first_ref, second_ref)):
            turned = weight_ref[...].astype(jnp.float32).T
            turned_ref[part * part_width : (part + 1) * part_width] = turned.astype(jnp.bfloat16)

    rows = dot_with(turned_ref[...], tokens_ref[...], 1, 1) + bias_ref[...]
    out_ref[...] = rows.astype(jnp.bfloat16).reshape(out_ref.shape)


def project(first, second, tokens, bias_column):
    row_count, width = tokens.shape
    part_width = first.shape[1]
    shape = (2, 3, part_width // 3, row_count)
    return pl.pallas_call(
        project_body,
        grid=(row_count // LONG_ROWS,),
        in_specs=[
            fixed_block((width, part_width)),
            fixed_block((width, part_width)),
            row_block(width, LONG_ROWS),
            fixed_block((2 * part_width, 1)),
        ],
        out_specs=pl.BlockSpec(shape[:3] + (LONG_ROWS,), lambda step: (0, 0, 0, step)),
        out_shape=jax.ShapeDtypeStruct(shape, jnp.bfloat16),
        scratch_shapes=[pltpu.VMEM((2 * part_width, width), jnp.bfloat16)],
        compiler_params=dense_params(),
        cost_estimate=cost(4 * row_count * width * part_width, 8_000_000),
    )(first, second, tokens, bias_column)


def adamw(master, moment, square, gradient, factor, learn_rate, decay_rate):
    clipped = gradient * factor
    moment_new = BETA_ONE * moment + (1.0 - BETA_ONE) * clipped
    square_new = BETA_TWO * square + (1.0 - BETA_TWO) * clipped * clipped
    step_size = moment_new / CORRECT_ONE / (jnp.sqrt(square_new / CORRECT_TWO) + ADAM_EPS)
    return (master - learn_rate * (step_size + decay_rate * master), moment_new, square_new)

def finish_body(
    places_ref,
    expand_ref,
    reduce_ref,
    mixing_ref,
    hidden_ref,
    left_ref,
    right_ref,
    inputs_ref,
    stat_ref,
    sums_ref,
    expand_out,
    reduce_out,
    mixing_out,
    left_out,
    right_out,
    row_ref,
    *,
    bias_share,
    shared_share,
):
    mine = places_ref[0]
    squares = jnp.zeros((1, 1), jnp.float32)

    def total(values):
        return jnp.sum(jnp.sum(values, axis=0, keepdims=True), axis=1, keepdims=True)

    at = 0
    for current_ref, out_ref in (
        (expand_ref, expand_out),
        (reduce_ref, reduce_out),
        (mixing_ref, mixing_out),
    ):
        width = out_ref.shape[1]
        share = current_ref[mine] + hidden_ref[:, at : at + width].astype(jnp.float32)
        out_ref[...] = share
        squares += total(share * share)
        at += width
    rows = left_ref.shape[1]
    received = inputs_ref[...].astype(jnp.float32)
    left = left_ref[mine] + received[:rows]
    right = right_ref[mine] + received[rows:]
    left_out[...] = left
    right_out[...] = right
    squares += total(left * left) + total(right[:rows] * right[:rows])
    small = right[rows : rows + 1]
    kernel = right[rows + 1 :]
    lane = lax.broadcasted_iota(jnp.int32, small.shape, 1)
    shared_counts = places_ref[1].astype(jnp.float32)
    factor = jnp.where(
        lane < bias_share, 1.0, jnp.where(lane < bias_share + shared_share, shared_counts, 0.0)
    )
    squares += total(small * small * factor) + total(kernel * kernel)
    lane = lax.broadcasted_iota(jnp.int32, (1, 128), 1)
    row = jnp.where(lane == 0, squares, 0.0)
    row += jnp.where(lane == 1, total(stat_ref[...]), 0.0)
    row += jnp.where(lane == 2, total(sums_ref[0:1]), 0.0)
    row_ref[:, :128] = row + jnp.where(lane == 3, sums_ref[4:5, 0:1], 0.0)
    row_ref[:, 128:] = kernel[:, : row_ref.shape[1] - 128]


def finish(places, hidden, inputs, stat_one, sums_two, bias_share, shared_share):
    def flat(array):
        return array.reshape(array.shape[-2:])

    def pair(array):
        return array.reshape((2,) + array.shape[-2:])

    arrays = [pair(array) for array in hidden.currents] + [flat(hidden.received)]
    arrays += [pair(array) for array in inputs.currents] + [flat(inputs.received)]
    arrays += [stat_one, sums_two]
    shapes = [array.shape[-2:] for array in hidden.currents + inputs.currents] + [(1, 384)]
    return pl.pallas_call(
        functools.partial(finish_body, bias_share=bias_share, shared_share=shared_share),
        in_specs=[pl.BlockSpec(memory_space=pltpu.SMEM)] + whole(len(arrays)),
        out_specs=whole(len(shapes)),
        out_shape=[jax.ShapeDtypeStruct(shape, jnp.float32) for shape in shapes],
        compiler_params=dense_params(),
        cost_estimate=cost(1_000_000, 3_000_000),
    )(places, *arrays)


def update_body(*refs, width, bias_share, shard_rows):
    totals_ref, kernel_ref, expand_ref, reduce_ref, mixing_ref, left_ref, right_ref = refs[:7]
    old_refs, new_refs, norm_ref, mean_ref = refs[7:28], refs[28:49], refs[49], refs[50]
    rows = left_ref.shape[0]
    totals = totals_ref[...]
    lane = lax.broadcasted_iota(jnp.int32, totals.shape, 1)
    means = jnp.sqrt(totals / jnp.where(lane == 0, 1.0, totals[:, 3:4] * width))
    norm_ref[...] = means[:, 0:1]
    mean_ref[...] = means[:, 1:3]
    factor = CLIP_NORM / (means[:, 0:1] + CLIP_EPS)

    def put(index, place, gradient, rate, decay):
        old = [old_refs[3 * index + kind][place] for kind in range(3)]
        for kind, value in enumerate(adamw(*old, gradient, factor, rate, decay)):
            new_refs[3 * index + kind][place] = value

    part_width = right_ref.shape[1] // 3
    for part, share_ref in enumerate((left_ref, right_ref)):
        for kind in range(3):
            gradient = share_ref[:rows, kind * part_width : (kind + 1) * part_width]
            lanes = slice(part * part_width, (part + 1) * part_width)
            put(0, (kind, slice(None), lanes), gradient, RATE_MATRIX, WEIGHT_DECAY)
    put(1, ..., mixing_ref[...], RATE_MATRIX, WEIGHT_DECAY)
    put(2, ..., expand_ref[...], RATE_MATRIX, WEIGHT_DECAY)
    put(3, ..., reduce_ref[...], RATE_MATRIX, WEIGHT_DECAY)
    small = slice(rows, rows + 1)
    put(4, ..., right_ref[small, :bias_share], RATE_VECTOR, 0.0)
    for row in range(6):
        start = bias_share + row * shard_rows
        place = (slice(row, row + 1), slice(None))
        put(5, place, right_ref[small, start : start + shard_rows], RATE_VECTOR, 0.0)
    heads, taps = old_refs[18].shape
    for row in range(heads):
        start = 128 + row * taps
        place = (slice(row, row + 1), slice(None))
        put(6, place, kernel_ref[:, start : start + taps], RATE_VECTOR, 0.0)


def update(totals, kernel_row, shares, olds, width, bias_share, shard_rows):
    arrays = [totals, kernel_row] + shares + olds
    shapes = [old.shape for old in olds] + [(1, 1), (1, 2)]
    return pl.pallas_call(
        functools.partial(update_body, width=width, bias_share=bias_share, shard_rows=shard_rows),
        in_specs=whole(len(arrays)),
        out_specs=whole(len(shapes)),
        out_shape=[jax.ShapeDtypeStruct(shape, jnp.float32) for shape in shapes],
        compiler_params=dense_params(),
        cost_estimate=cost(5_000_000, 6_000_000),
    )(*arrays)


def body(
    tokens,
    cotangent,
    item_units,
    counted,
    inputs_weight,
    inputs_moment,
    inputs_square,
    mixing_weight,
    mixing_moment,
    mixing_square,
    expand_weight,
    expand_moment,
    expand_square,
    reduce_weight,
    reduce_moment,
    reduce_square,
    biases_weight,
    biases_moment,
    biases_square,
    shared_weight,
    shared_moment,
    shared_square,
    kernel_weight,
    kernel_moment,
    kernel_square,
):
    dp_count = lax.axis_size("dp")
    bits = list(range(bits_of(dp_count)))
    first_order, second_order = bits, bits[:2][::-1] + bits[2:]
    row_count, width_full = tokens.shape
    local_width = inputs_weight.shape[2]
    shard_rows = inputs_weight.shape[1]
    bias_share = biases_weight.shape[1]
    hidden_units = expand_weight.shape[1]
    part_width = local_width // 2
    part_lanes = [slice(0, part_width), slice(part_width, local_width)]

    high_bits = bits[2:][::-1]
    low_orders = (bits[:2][::-1], bits[:2])
    small_low = jnp.concatenate([biases_weight.reshape(-1), shared_weight.reshape(-1)])
    small_low = jnp.pad(small_low, (0, (-small_low.shape[0]) % (3 * part_width)))
    small_low = small_low.astype(jnp.bfloat16).reshape(-1, 3 * part_width)
    inputs_low = [
        jnp.concatenate([inputs_weight[c][:, lanes] for c in range(3)], axis=1).astype(jnp.bfloat16)
        for lanes in part_lanes
    ]
    inputs_low = jnp.concatenate([inputs_low[1], inputs_low[0], small_low], axis=0)
    sizes = (shard_rows, inputs_low.shape[0] - shard_rows)
    inputs_gather = Gather(inputs_low, dp_count, high_bits)
    late_low = jnp.concatenate(
        [expand_weight.astype(jnp.bfloat16)]
        + [weight.astype(jnp.bfloat16).T for weight in (mixing_weight, reduce_weight)],
        axis=1,
    )
    inputs_gather.step()
    late_low = after(late_low, inputs_gather.current)
    for _ in high_bits[1:]:
        inputs_gather.step()
    right_gather, left_gather = inputs_gather.split(sizes, -2, low_orders)
    inputs_right = right_gather.finish()
    left_full = left_gather.finish().reshape(dp_count, sizes[1], 3 * part_width)
    inputs_left = left_full[:, :shard_rows].reshape(-1, 3 * part_width)
    small_full = left_full[:, shard_rows:].reshape(dp_count, -1)
    late_gather = Gather(late_low, dp_count, high_bits)
    for _ in high_bits:
        late_gather.step()
    sizes = (hidden_units + local_width, hidden_units)
    expand_gather, reduce_gather = late_gather.split(sizes, -1, low_orders)
    biases_row = small_full[:, :bias_share].reshape(-1).astype(jnp.float32)
    shared_rows = small_full[:, bias_share : bias_share + 6 * shard_rows]
    shared_rows = shared_rows.reshape(dp_count, 6, shard_rows).transpose(1, 0, 2)
    shared_rows = shared_rows.reshape(6, -1).astype(jnp.float32)
    query_bias = biases_row[:local_width]
    value_bias = biases_row[local_width : 2 * local_width]
    expand_bias = biases_row[2 * local_width :][None, :]
    zero_bias = jnp.zeros((part_width,), jnp.float32)
    bias_column = jnp.concatenate(
        [
            piece
            for lanes in part_lanes
            for piece in (query_bias[lanes], zero_bias, value_bias[lanes])
        ]
    )[:, None]

    row_item = row_items(item_units[0], row_count, LANDMARKS)
    inside = (row_item < 2).astype(jnp.float32)
    weight_rows = counted.astype(jnp.float32) * inside
    weight_row = weight_rows[None, :]

    tied_tokens = after(tokens, expand_gather.current, reduce_gather.current)
    proj = project(inputs_left, inputs_right, tied_tokens, bias_column)
    marks, middle, last, values, approx = attention_start(item_units, proj)
    expand_gather.step(marks)
    reduce_gather.step(marks)
    tied_marks = after(marks, expand_gather.current, reduce_gather.current)
    attended, kept, rough, fine, weighted = attention_finish(
        item_units, proj, tap_rows_of(kernel_weight), tied_marks, middle, last, values, approx
    )
    saved = (kept, last, marks, middle, rough, fine, values, weighted)
    expand_full = expand_gather.finish()
    reduce_full = reduce_gather.finish()
    hidden_weights = (expand_full, reduce_full)
    mixing_column = expand_full.shape[1] // local_width - 1
    tied_attended = after(attended, reduce_full)
    own_one = turned_dot([tied_attended], [expand_full], [mixing_column], width_full)
    other_one = swap(own_one, "head", 2, 0)
    own_two, hidden_low, unit_one, scale_one, wide, stat_one = hidden_forward(
        own_one, other_one, tokens, weight_row, shared_rows, expand_bias, *hidden_weights
    )
    other_two = swap(own_two, "head", 2, 0)
    output_rows, d_two, reduce_grad, expand_grad, own_three, sums_two, expand_sums = hidden_backward(
        own_two, other_two, hidden_low, cotangent, weight_row, shared_rows, wide, *hidden_weights
    )
    other_three = swap(own_three, "head", 2, 0)
    reduce_scatter = Scatter([reduce_grad], dp_count, second_order).send()
    expand_scatter = Scatter([expand_grad], dp_count, first_order).send()
    d_one, d_mixed, sums_one = norm_one_backward(
        own_three,
        other_three,
        d_two,
        unit_one,
        scale_one,
        inside[None, :],
        shared_rows,
        expand_full,
        local_width,
    )
    mixing_grad = jnp.einsum("rd,kr->dk", d_one, attended, preferred_element_type=jnp.float32)
    mixing_scatter = Scatter([mixing_grad.astype(jnp.bfloat16)], dp_count, first_order).send()
    first_scatters = (reduce_scatter, expand_scatter, mixing_scatter)
    d_mixed = after(d_mixed, *[scatter.sent for scatter in first_scatters])
    back_taps = tap_rows_of(kernel_weight[:, ::-1])
    d_left, kernel_left = attention_backward(item_units, proj, back_taps, d_mixed, *saved, part=0)

    for scatter in first_scatters:
        scatter.take(d_left).send()
    left_grad = turned_outer(d_left, tokens)
    left_scatter = Scatter([left_grad], dp_count, second_order).send()
    d_mixed = after(d_mixed, left_scatter.sent, *[scatter.sent for scatter in first_scatters])
    d_right, kernel_right = attention_backward(item_units, proj, back_taps, d_mixed, *saved, part=1)
    right_grad = turned_outer(d_right, tokens)
    left_sums, right_sums = [
        jnp.sum(gradient.astype(jnp.float32), axis=1).reshape(3, part_width)
        for gradient in (d_left, d_right)
    ]
    biases_grad = jnp.concatenate(
        [left_sums[0], right_sums[0], left_sums[2], right_sums[2], expand_sums.reshape(-1)]
    )
    shared_grad = jnp.concatenate(
        [sums_one[0:1], sums_two[1:2], sums_one[1:3], sums_two[2:4]], axis=0
    )
    shared_grad = shared_grad.reshape(6, dp_count, shard_rows).transpose(1, 0, 2)
    kernel_grad = jnp.concatenate([kernel_left, kernel_right], axis=0)
    columns = 3 * part_width

    def widened(array):
        return jnp.pad(array, ((0, 0), (0, columns - array.shape[1])))[:, None]

    tap_count = kernel_grad.shape[1]
    tap_share = -(-tap_count // dp_count)
    tap_owner = jnp.arange(tap_count) // tap_share
    kernel_rows = jnp.where(
        tap_owner[None, None, :] == jnp.arange(dp_count)[:, None, None], kernel_grad[None], 0.0
    )
    small_rows = jnp.concatenate(
        [biases_grad.reshape(dp_count, bias_share), shared_grad.reshape(dp_count, -1)], axis=1
    )
    right_rows = jnp.concatenate(
        [
            right_grad.reshape(dp_count, shard_rows, columns),
            widened(small_rows).astype(jnp.bfloat16),
            widened(kernel_rows.reshape(dp_count, -1)).astype(jnp.bfloat16),
        ],
        axis=1,
    )
    right_rows = right_rows.reshape(-1, columns)
    right_scatter = Scatter([right_rows], dp_count, first_order).send()
    for scatter in first_scatters:
        scatter.take(right_scatter.sent)
    hidden_scatter = expand_scatter.merge(reduce_scatter, mixing_scatter).send()
    left_scatter.take(right_scatter.sent).send()
    d_both = after(d_right, right_scatter.sent, hidden_scatter.sent, left_scatter.sent)
    own_four = turned_dot([d_left, d_both], [inputs_left, inputs_right], [0, 0], width_full)
    other_four = swap(own_four, "head", 2, 0)
    hidden_scatter.take(own_four).send()
    right_scatter.take(own_four).send()
    input_grad = (
        own_four.astype(jnp.float32) + other_four.astype(jnp.float32) + d_one.astype(jnp.float32)
    )
    inputs_scatter = left_scatter.merge(right_scatter, join=-2).send()
    dp_index, head_index = lax.axis_index("dp"), lax.axis_index("head")
    places = jnp.stack([(dp_index >> bits[-1]) & 1, head_index == 0]).astype(jnp.int32)
    inputs_scatter.take(input_grad)
    while hidden_scatter.order:
        hidden_scatter.take().send()
    while inputs_scatter.order:
        inputs_scatter.take().send()
    *shares, final_row = finish(
        places, hidden_scatter, inputs_scatter, stat_one, sums_two, bias_share, 6 * shard_rows
    )
    final_row = sum_all(final_row, "dp", dp_count)
    totals = sum_all(final_row[:, :128], "head", 2)
    olds = [
        inputs_weight,
        inputs_moment,
        inputs_square,
        mixing_weight.T,
        mixing_moment.T,
        mixing_square.T,
        expand_weight,
        expand_moment,
        expand_square,
        reduce_weight.T,
        reduce_moment.T,
        reduce_square.T,
        biases_weight,
        biases_moment,
        biases_square,
        shared_weight,
        shared_moment,
        shared_square,
        kernel_weight,
        kernel_moment,
        kernel_square,
    ]
    *news, norm, means = update(totals, final_row, shares, olds, width_full, bias_share, shard_rows)
    for index in (3, 4, 5, 9, 10, 11):
        news[index] = news[index].T
    return (output_rows, input_grad, *news, norm.reshape(()), means.reshape(2))


def solution(mesh):
    placed = (
        P("dp", None),
        P("dp", None),
        P("dp", None),
        P("dp"),
        P(None, "dp", "head"),
        P(None, "dp", "head"),
        P(None, "dp", "head"),
        P("head", "dp"),
        P("head", "dp"),
        P("head", "dp"),
        P("dp", "head"),
        P("dp", "head"),
        P("dp", "head"),
        P("head", "dp"),
        P("head", "dp"),
        P("head", "dp"),
        P("head", "dp"),
        P("head", "dp"),
        P("head", "dp"),
        P(None, "dp"),
        P(None, "dp"),
        P(None, "dp"),
        P("head", None),
        P("head", None),
        P("head", None),
    )
    return jax.shard_map(
        body,
        mesh=mesh,
        in_specs=placed,
        out_specs=(
            P("dp", None),
            P("dp", None),
            P(None, "dp", "head"),
            P(None, "dp", "head"),
            P(None, "dp", "head"),
            P("head", "dp"),
            P("head", "dp"),
            P("head", "dp"),
            P("dp", "head"),
            P("dp", "head"),
            P("dp", "head"),
            P("head", "dp"),
            P("head", "dp"),
            P("head", "dp"),
            P("head", "dp"),
            P("head", "dp"),
            P("head", "dp"),
            P(None, "dp"),
            P(None, "dp"),
            P(None, "dp"),
            P("head", None),
            P("head", None),
            P("head", None),
            P(),
            P(),
        ),
        check_vma=False,
    )
```
